256 devices in a mesh: dp: 32 (over z_hi, y, core), mp: 8 (over z_lo, x).
Axes of the slice: x: 4, y: 4, z: 8 (z_hi: 4, z_lo: 2; z = z_hi * 2 + z_lo), core: 2. Of those that a mesh axis runs over, the one named last changes fastest.
Arguments:
- features: bfloat16 [2, 8192, 1024], P(None, 'dp'), may hold values from -8 to 8
- projections: bfloat16 [2, 1024, 768], P(None, 'mp'), may hold values from -1 to 1
- solution: float32 [2, 1024, 768], P(None, 'mp'), may hold values from -6 to 6
- residual: float32 [2, 1024, 768], P(None, 'mp'), may hold values from -6 to 6
- direction: float32 [2, 1024, 768], P(None, 'mp'), may hold values from -6 to 6
Outputs:
- new_solution: float32 [2, 1024, 768], P(None, 'mp')
- new_residual: float32 [2, 1024, 768], P(None, 'mp')
- new_direction: float32 [2, 1024, 768], P(None, 'mp')
The draws below stay inside these ranges and needn't reach their ends.
All inputs are finite; a program needn't handle non-finite values.
Results may differ from the reference program's by a relative error of at most 0.0016.
The reference program's roundings to bfloat16 on the way (of `packed` and `tdz`) count: a program that leaves them out, or rounds other values in their place, can miss the bound.
Values may be sent and summed in bfloat16 or wider, within the bound.
A program may use at most 64 MiB of HBM per device.

```python
import jax
import jax.numpy as jnp
from jax import lax

D = 1024
P_SIZE = 768
TOK_DEV = 256
TOKENS = 8192
N_DP = 32


def draw_features(key, part):
    key = jax.random.fold_in(key, 11)
    first_key, second_key, third_key = jax.random.split(key, 3)
    shape = (TOKENS, D)
    common = 1.6 * jax.random.truncated_normal(third_key, -2.5, 2.5, (1, D), jnp.float32)
    sar_noise = jax.random.truncated_normal(first_key, -3.0, 3.0, shape, jnp.float32)
    other_noise = jax.random.truncated_normal(second_key, -3.0, 3.0, shape, jnp.float32)
    sar = common + sar_noise
    optical = common + 0.25 * sar_noise + 0.97 * other_noise
    return jnp.stack([sar, optical]).astype(jnp.bfloat16)


def draw_projections(key, part):
    key = jax.random.fold_in(key, 23)
    first_key, second_key = jax.random.split(key)
    shape = (D, P_SIZE)
    base = jax.random.truncated_normal(first_key, -3.0, 3.0, shape, jnp.float32)
    noise = jax.random.truncated_normal(second_key, -3.0, 3.0, shape, jnp.float32)
    other = 0.6 * base + 0.8 * noise
    factor = 76.8 / P_SIZE * D ** (-0.5)
    return (jnp.stack([base, other]) * factor).astype(jnp.bfloat16)


def level_of(key, shape, pieces, smallest, top_value):
    loudness, own = 1.0, jax.random.fold_in(key, 6)
    for dim, blocks in pieces:
        heights = jnp.exp(jax.random.uniform(jax.random.fold_in(own, dim), (blocks,), jnp.float32, smallest / len(pieces), top_value / len(pieces)))
        loudness = loudness * jnp.repeat(heights, shape[dim] // blocks).reshape([-1 if axis == dim else 1 for axis in range(len(shape))])
    return loudness


def bell_draw(rng, shape, deviation, bound, pieces=(), kind=jnp.bfloat16):
    values = deviation * jax.random.normal(rng, shape, jnp.float32)
    if pieces:
        values = values * level_of(rng, shape, pieces, -0.22, 0.18)
    return jnp.clip(values, -bound, bound).astype(kind)


def setup_inputs(seed: int = 0) -> dict:
    seeds = jax.random.split(jax.random.key(seed), 6)
    return {
        "features": draw_features(jax.random.fold_in(seeds[5], 71), 0),
        "projections": draw_projections(jax.random.fold_in(seeds[5], 71), 0),
        "solution": bell_draw(seeds[2], (2, D, P_SIZE), 1.0, 6.0, ((1, 8),), jnp.float32),
        "residual": bell_draw(seeds[3], (2, D, P_SIZE), 1.0, 6.0, ((1, 8),), jnp.float32),
        "direction": bell_draw(seeds[4], (2, D, P_SIZE), 1.0, 6.0, ((1, 8),), jnp.float32),
    }


LOGIT_SCALE = 100.0
DAMPING = 1.0
EPSILON = 1e-06

def normalize(raw, tangent):
    inverse = lax.rsqrt(lax.optimization_barrier(jnp.sum(raw * raw, -1, keepdims=True)) + EPSILON)
    unit_vec = raw * inverse
    turned = (tangent - unit_vec * lax.optimization_barrier(jnp.sum(unit_vec * tangent, -1, keepdims=True))) * inverse
    return (unit_vec, turned, inverse)

def grad_tangent(unit_vec, turned, inverse, tangent, grads, tgrads):
    along = lax.optimization_barrier(jnp.sum(unit_vec * grads, -1, keepdims=True))
    plain = (grads - unit_vec * along) * inverse
    mixed = lax.optimization_barrier(jnp.sum(turned * grads, -1, keepdims=True)) + lax.optimization_barrier(jnp.sum(unit_vec * tgrads, -1, keepdims=True))
    result = (tgrads - turned * along - unit_vec * mixed) * inverse
    return result - plain * inverse * lax.optimization_barrier(jnp.sum(unit_vec * tangent, -1, keepdims=True))

def reference(features, projections, solution, residual, direction):
    total = features.shape[1]
    packed = direction.astype(jnp.bfloat16)
    raw = jnp.stack([jnp.dot(features[tower], projections[tower], preferred_element_type=jnp.float32) for tower in range(2)])
    tangent = jnp.stack([jnp.dot(features[tower], packed[tower], preferred_element_type=jnp.float32) for tower in range(2)])
    unit_vec, turned, inverse = normalize(raw, tangent)
    unit_low = unit_vec.astype(jnp.bfloat16)
    turned_low = turned.astype(jnp.bfloat16)
    left, right = (unit_low[0], unit_low[1])
    left_t, right_t = (turned_low[0], turned_low[1])
    starts = jnp.arange(N_DP, dtype=jnp.int32) * TOK_DEV
    index_cols = jnp.arange(total, dtype=jnp.int32)
    index_rows = jnp.arange(TOK_DEV, dtype=jnp.int32)

    def first_pass(carry, start):
        col_max, col_sum = carry
        rows_left = lax.dynamic_slice_in_dim(left, start, TOK_DEV, 0)
        scores = LOGIT_SCALE * jnp.dot(rows_left, right.T, preferred_element_type=jnp.float32)
        merged = jnp.maximum(col_max, lax.optimization_barrier(jnp.max(scores, 0)))
        col_sum = col_sum * jnp.exp(col_max - merged) + lax.optimization_barrier(jnp.sum(jnp.exp(scores - merged[None, :]), 0))
        row_max = lax.optimization_barrier(jnp.max(scores, 1))
        row_lse = row_max + jnp.log(lax.optimization_barrier(jnp.sum(jnp.exp(scores - row_max[:, None]), 1)))
        return ((merged, col_sum), row_lse)
    start_carry = (jnp.full((total,), -1e+30, jnp.float32), jnp.zeros((total,), jnp.float32))
    (col_max, col_sum), row_lse = lax.scan(first_pass, start_carry, starts)
    col_lse = col_max + jnp.log(col_sum)

    def weights_at(start, lse_rows):
        rows_left = lax.dynamic_slice_in_dim(left, start, TOK_DEV, 0)
        rows_tan = lax.dynamic_slice_in_dim(left_t, start, TOK_DEV, 0)
        scores = LOGIT_SCALE * jnp.dot(rows_left, right.T, preferred_element_type=jnp.float32)
        tscores = LOGIT_SCALE * (jnp.dot(rows_tan, right.T, preferred_element_type=jnp.float32) + jnp.dot(rows_left, right_t.T, preferred_element_type=jnp.float32))
        row_w = jnp.exp(scores - lse_rows[:, None])
        col_w = jnp.exp(scores - col_lse[None, :])
        return (rows_left, rows_tan, tscores, row_w, col_w)

    def second_pass(carry, inputs):
        start, lse_rows = inputs
        rows_left, rows_tan, tscores, row_w, col_w = weights_at(start, lse_rows)
        return (carry + lax.optimization_barrier(jnp.sum(col_w * tscores, 0)), lax.optimization_barrier(jnp.sum(row_w * tscores, 1)))
    col_dot, row_dot = lax.scan(second_pass, jnp.zeros((total,), jnp.float32), (starts, row_lse))

    def third_pass(carry, inputs):
        start, lse_rows, dots = inputs
        rows_left, rows_tan, tscores, row_w, col_w = weights_at(start, lse_rows)
        positive = (index_cols[None, :] == (start + index_rows)[:, None]).astype(jnp.float32)
        dscore = ((row_w + col_w - 2.0 * positive) / (2.0 * total)).astype(jnp.bfloat16)
        tdscore = ((row_w * (tscores - dots[:, None]) + col_w * (tscores - col_dot[None, :])) / (2.0 * total)).astype(jnp.bfloat16)
        row_grad = LOGIT_SCALE * jnp.dot(dscore, right, preferred_element_type=jnp.float32)
        row_tgrad = LOGIT_SCALE * (jnp.dot(tdscore, right, preferred_element_type=jnp.float32) + jnp.dot(dscore, right_t, preferred_element_type=jnp.float32))
        col_grad, col_tgrad = carry
        col_grad = col_grad + LOGIT_SCALE * jnp.dot(dscore.T, rows_left, preferred_element_type=jnp.float32)
        col_tgrad = col_tgrad + LOGIT_SCALE * (jnp.dot(tdscore.T, rows_left, preferred_element_type=jnp.float32) + jnp.dot(dscore.T, rows_tan, preferred_element_type=jnp.float32))
        return ((col_grad, col_tgrad), (row_grad, row_tgrad))
    width = right.shape[1]
    zero_grads = (jnp.zeros((total, width), jnp.float32), jnp.zeros((total, width), jnp.float32))
    (col_grad, col_tgrad), (row_grad, row_tgrad) = lax.scan(third_pass, zero_grads, (starts, row_lse, row_dot))
    grads = jnp.stack([row_grad.reshape(total, width), col_grad])
    tgrads = jnp.stack([row_tgrad.reshape(total, width), col_tgrad])
    tdz = grad_tangent(unit_vec, turned, inverse, tangent, grads, tgrads).astype(jnp.bfloat16)
    hess = jnp.stack([jnp.dot(features[tower].T, tdz[tower], preferred_element_type=jnp.float32) for tower in range(2)])
    hess = hess + DAMPING * direction
    norm_old = jnp.sum(residual * residual)
    curve = jnp.sum(direction * hess)
    alpha = norm_old / curve
    new_solution = solution + alpha * direction
    new_residual = residual - alpha * hess
    norm_new = jnp.sum(new_residual * new_residual)
    new_direction = new_residual + norm_new / norm_old * direction
    return (new_solution, new_residual, new_direction)
```

```python
import functools

import jax
import jax.numpy as jnp
from jax import lax
from jax.experimental import pallas as pl
from jax.experimental.pallas import tpu as pltpu
from jax.sharding import PartitionSpec as P

LOGIT_SCALE = 100.0
DAMPING = 1.0
EPSILON = 1e-06

NC, NY, NH, NX, NL = 2, 4, 4, 4, 2
NM = NX * NL
ROWS, DEPTH, WIDTH = 256, 1024, 768
PART = DEPTH // NM
SHARE = ROWS // NM
COLS = SHARE * NC * NY * NH
HALF = COLS // NC
PAIRS = ROWS * NC * NY * NH
TILE = 256
SEMS = 224
F32, BF16 = jnp.float32, jnp.bfloat16
MESH = pl.DeviceIdType.MESH


def dot(left, right, dims=((1,), (0,))):
    return lax.dot_general(left, right, (dims, ((), ())), preferred_element_type=F32)


def unit_of(raw):
    inverse = lax.rsqrt(jnp.sum(raw * raw, -1, keepdims=True) + EPSILON)
    return raw * inverse, inverse


def turn_of(tangent, unit, inverse):
    along = jnp.sum(unit * tangent, -1, keepdims=True)
    return (tangent - unit * along) * inverse, along


def pack_lanes(columns):
    size = columns[0].shape[0]
    lane = lax.broadcasted_iota(jnp.int32, (size, 128), 1)
    wide = jnp.zeros((size, 128), F32)
    for place, column in enumerate(columns):
        wide = jnp.where(lane == place, column, wide)
    return wide.T[0:8]


def unpack_lanes(rows):
    return jnp.concatenate([rows, jnp.zeros((120, rows.shape[1]), F32)], 0).T


def stack_rows(rows):
    size = rows[0].shape[1]
    return jnp.concatenate(list(rows) + [jnp.zeros((8 - len(rows), size), F32)], 0)


def softmax_join(slots):
    top = functools.reduce(jnp.maximum, [slot[0] for slot in slots])
    total = 0.0
    weighted = 0.0
    for slot in slots:
        factor = jnp.exp(slot[0] - top)
        total = total + factor * slot[1]
        weighted = weighted + factor * slot[2]
    return top, total, weighted


def kernel(
    feats, proj, direc, resid, solu,
    out_sol, out_res, out_dir,
    weights, rawbuf, tanbuf, rows_u, rows_t, cols_u, cols_t,
    scores, left_ts, right_ts, dsc, tdsc, cvec,
    row_slots, core_stat, y_stat, z_stat,
    grad_slots, core_grad, y_grad, z_grad,
    row_part, row_recv, col_part, col_recv, y_recv, z_recv,
    grad_cols, grad_rows, tdz, part_hess, core_hess, y_hess, z_hess, hess,
    scal_m, scal_c, scal_y, scal_z, norm_m, norm_c, norm_y, norm_z,
    send_sem, recv_sem,
):
    dp, mp = lax.axis_index("dp"), lax.axis_index("mp")
    c, y, zh = dp % NC, (dp // NC) % NY, dp // (NC * NY)
    x, zl = mp % NX, mp // NX
    counter = [0]

    def device(core=None, row=None, high=None, model=None):
        core, row, high = c if core is None else core, y if row is None else row, zh if high is None else high
        return {"dp": (high * NY + row) * NC + core, "mp": mp if model is None else model}

    def m_at(step):
        return ((zl + step // NX) % NL) * NX + (x + step % NX) % NX

    def m_from(step):
        return ((zl + step // NX) % NL) * NX + (x + NX - step % NX) % NX

    def y_at(step):
        return (y + step) % NY

    def h_at(step):
        return (zh + step) % NH

    def send(source, target, where):
        place = counter[0]
        counter[0] += 1
        copy = pltpu.make_async_remote_copy(
            src_ref=source, dst_ref=target, send_sem=send_sem.at[place], recv_sem=recv_sem.at[place],
            device_id=where, device_id_type=MESH,
        )
        copy.start()
        pending.append(copy)
        return copy

    pending = []

    def arrive(copies):
        for copy in copies:
            copy.wait_recv()

    def over_m(source, target):
        return [send(source(m_at(q)), target(q), device(model=m_at(q))) for q in range(1, NM)]

    def over_y(source, target):
        return [send(source(y_at(q)), target(q), device(row=y_at(q))) for q in range(1, NY)]

    def over_h(source, target):
        return [send(source(h_at(q)), target(q), device(high=h_at(q))) for q in range(1, NH)]

    def over_c(source, target):
        return [send(source, target, device(core=1 - c))]

    barrier = pltpu.get_barrier_semaphore()
    for q in range(1, NM):
        pl.semaphore_signal(barrier, inc=1, device_id=device(model=m_at(q)), device_id_type=MESH)
    for q in range(1, NY):
        pl.semaphore_signal(barrier, inc=1, device_id=device(row=y_at(q)), device_id_type=MESH)
    for q in range(1, NH):
        pl.semaphore_signal(barrier, inc=1, device_id=device(high=h_at(q)), device_id_type=MESH)
    pl.semaphore_signal(barrier, inc=1, device_id=device(core=1 - c), device_id_type=MESH)
    pl.semaphore_wait(barrier, NM + NY + NH - 2)

    for tower in range(2):
        weights[0, tower, pl.ds(mp, 1)] = proj[tower][None]
        weights[1, tower, pl.ds(mp, 1)] = direc[tower].astype(BF16)[None]

    def fetch(kind):
        return over_m(lambda m: weights.at[kind, c, mp], lambda q: weights.at[kind, c, mp])

    def hand_over(kind, copies):
        passed = []
        for q, copy in enumerate(copies, 1):
            copy.wait_recv()
            block = weights.at[kind, c, m_from(q)]
            passed += over_c(block, block)
        return passed

    def embed(kind, into):
        for tile in range(WIDTH // TILE):
            span = slice(tile * TILE, (tile + 1) * TILE)
            total = jnp.zeros((ROWS, TILE), F32)
            other = jnp.zeros((SHARE, TILE), F32)
            for block in range(0, NM, 2):
                deep = slice(block * PART, (block + 2) * PART)
                piece = weights[kind, 0, block : block + 2, :, span].reshape(2 * PART, TILE)
                total += dot(feats[0, :, deep], piece)
                piece = weights[kind, 1, block : block + 2, :, span].reshape(2 * PART, TILE)
                other += dot(feats[1, pl.ds(pl.multiple_of(mp * SHARE, SHARE), SHARE), deep], piece)
            into[0:ROWS, span] = total
            into[ROWS : ROWS + SHARE, span] = other

    first = fetch(0)
    passed = hand_over(0, first)
    second = fetch(1)
    arrive(passed)
    embed(0, rawbuf)
    unit_all, inverse_all = unit_of(rawbuf[...])
    low = unit_all.astype(BF16)
    rows_u[...] = low[0:ROWS]
    cols_u[c, y, zh] = low[ROWS : ROWS + SHARE]

    def columns_high(cols):
        block = cols.at[c, y, zh]
        return over_h(lambda h: block, lambda q: block)

    def columns_row(cols):
        block = cols.at[c, y]
        return over_y(lambda r: block, lambda q: block)

    def columns_core(cols, copies):
        passed = over_c(cols.at[c, y], cols.at[c, y])
        for q, copy in enumerate(copies, 1):
            copy.wait_recv()
            block = cols.at[c, (y + NY - q) % NY]
            passed += over_c(block, block)
        return passed

    copies = columns_high(cols_u)
    arrive(copies)
    copies = columns_row(cols_u)
    passed_t = hand_over(1, second)
    passed_u = columns_core(cols_u, copies)
    arrive(passed_t)
    embed(1, tanbuf)
    unit_all, inverse_all = unit_of(rawbuf[...])
    turned_all, along_all = turn_of(tanbuf[...], unit_all, inverse_all)
    low = turned_all.astype(BF16)
    rows_t[...] = low[0:ROWS]
    cols_t[c, y, zh] = low[ROWS : ROWS + SHARE]
    slope = inverse_all * along_all
    copies = columns_high(cols_t)
    first_col = pl.multiple_of(((c * NY + y) * NH + zh) * SHARE, SHARE)
    cvec[...] = jnp.zeros_like(cvec)
    cvec[pl.ds(first_col, SHARE)] = jnp.broadcast_to(slope[ROWS : ROWS + SHARE], (SHARE, 128))
    slope_row = cvec[...].T[0:1]
    row_slope = slope[0:ROWS]
    own = pl.ds(pl.multiple_of(mp * SHARE, SHARE), SHARE)
    arrive(passed_u)
    arrive(copies)
    copies = columns_row(cols_t)

    def column_tile(cols, tile):
        return cols[tile // 2, (tile % 2) * 2 : (tile % 2) * 2 + 2].reshape(TILE, WIDTH)

    NT = ((1,), (1,))
    tiles = COLS // TILE
    for tile in range(tiles):
        span = slice(tile * TILE, (tile + 1) * TILE)
        piece = column_tile(cols_u, tile)
        scores[:, span] = LOGIT_SCALE * dot(rows_u[...], piece, NT)
        left_ts[:, span] = LOGIT_SCALE * dot(rows_t[...], piece, NT)
    passed = columns_core(cols_t, copies)
    row_max = jnp.max(scores[...], 1, keepdims=True)
    col_max = jnp.max(scores[...], 0, keepdims=True)
    arrive(passed)
    for tile in range(tiles):
        span = slice(tile * TILE, (tile + 1) * TILE)
        right_ts[:, span] = LOGIT_SCALE * dot(rows_u[...], column_tile(cols_t, tile), NT)

    row_sum = jnp.zeros((ROWS, 1), F32)
    row_weighted = jnp.zeros((ROWS, 1), F32)
    col_sum, col_weighted = [], []
    for tile in range(tiles):
        span = slice(tile * TILE, (tile + 1) * TILE)
        score = scores[:, span]
        tscore = left_ts[:, span] + right_ts[:, span]
        weight = jnp.exp(score - row_max)
        row_sum += jnp.sum(weight, 1, keepdims=True)
        row_weighted += jnp.sum(weight * tscore, 1, keepdims=True)
        weight = jnp.exp(score - col_max[:, span])
        col_sum.append(jnp.sum(weight, 0, keepdims=True))
        col_weighted.append(jnp.sum(weight * tscore, 0, keepdims=True))
    resid_norm = jnp.sum(resid[...] * resid[...])
    direc_norm = jnp.sum(direc[...] * direc[...])
    constant = lambda value: jnp.full((ROWS, 1), value, F32)
    row_slots[pl.ds(mp, 1)] = pack_lanes(
        [row_max, row_sum, row_weighted, constant(resid_norm), constant(direc_norm)]
    )[None]
    core_stat[pl.ds(c, 1)] = stack_rows(
        [col_max, jnp.concatenate(col_sum, 1), jnp.concatenate(col_weighted, 1), slope_row]
    )[None]

    def join_columns(slots, count):
        parts = [slots[k] for k in range(count)]
        top, total, weighted = softmax_join([(part[0:1], part[1:2], part[2:3]) for part in parts])
        slopes = functools.reduce(jnp.add, [part[3:4] for part in parts])
        return top, total, weighted, slopes

    def sum_slots(slots, count):
        return functools.reduce(jnp.add, [slots[k] for k in range(count)])

    def spread_c(slots):
        return over_c(slots.at[c], slots.at[c])

    def spread_y(slots):
        return over_y(lambda r: slots.at[y], lambda q: slots.at[y])

    def spread_h(slots):
        return over_h(lambda h: slots.at[zh], lambda q: slots.at[zh])

    def spread_m(slots):
        return over_m(lambda m: slots.at[mp], lambda q: slots.at[mp])

    copies = spread_c(core_stat)
    row_copies = spread_m(row_slots)
    arrive(copies)
    y_stat[pl.ds(y, 1)] = stack_rows(join_columns(core_stat, NC))[None]
    copies = spread_y(y_stat)
    arrive(copies)
    z_stat[pl.ds(zh, 1)] = stack_rows(join_columns(y_stat, NY))[None]
    copies = spread_h(z_stat)
    arrive(row_copies)
    parts = [row_slots[k] for k in range(NM)]
    top, total, weighted = softmax_join([(part[0:1], part[1:2], part[2:3]) for part in parts])
    norms = functools.reduce(jnp.add, [part[3:5] for part in parts])
    norm_old = norms[0:1, 0:1]
    norm_direc = norms[1:2, 0:1]
    row_info = unpack_lanes(stack_rows([top + jnp.log(total), weighted / total]))
    row_lse, row_dot = row_info[:, 0:1], row_info[:, 1:2]
    arrive(copies)
    top, total, weighted, slopes = join_columns(z_stat, NH)
    col_lse, col_dot = top + jnp.log(total), weighted / total
    col_slope = unpack_lanes(stack_rows([slopes]))

    row_ids = lax.broadcasted_iota(jnp.int32, (ROWS, TILE), 0)
    col_ids = lax.broadcasted_iota(jnp.int32, (ROWS, TILE), 1)
    offset = mp * SHARE - first_col
    row_along = jnp.zeros((ROWS, 1), F32)
    row_turned = jnp.zeros((ROWS, 1), F32)
    col_along, col_turned = [], []
    for tile in range(tiles):
        span = slice(tile * TILE, (tile + 1) * TILE)
        score = scores[:, span]
        left, right = left_ts[:, span], right_ts[:, span]
        tscore = left + right
        row_w = jnp.exp(score - row_lse)
        col_w = jnp.exp(score - col_lse[:, span])
        place = col_ids + tile * TILE
        mine = (place >= first_col) & (place < first_col + SHARE) & (row_ids == place + offset)
        low = ((row_w + col_w - 2.0 * mine.astype(F32)) / (2.0 * PAIRS)).astype(BF16)
        dsc[:, span] = low
        tdsc[:, span] = (
            (row_w * (tscore - row_dot) + col_w * (tscore - col_dot[:, span])) / (2.0 * PAIRS)
        ).astype(BF16)
        wide = low.astype(F32)
        row_along += jnp.sum(wide * score, 1, keepdims=True)
        row_turned += jnp.sum(wide * left, 1, keepdims=True)
        col_along.append(jnp.sum(wide * score, 0, keepdims=True))
        col_turned.append(jnp.sum(wide * right, 0, keepdims=True))
    grad_slots[pl.ds(mp, 1)] = pack_lanes([row_along, row_turned])[None]
    core_grad[pl.ds(c, 1)] = stack_rows([jnp.concatenate(col_along, 1), jnp.concatenate(col_turned, 1)])[None]
    grad_copies = spread_m(grad_slots)
    core_copies = spread_c(core_grad)

    TN = ((0,), (0,))
    cvec[...] = col_slope

    def column_terms(tile):
        start = pl.multiple_of(tile * TILE, TILE)
        d_low, t_low = dsc[:, pl.ds(start, TILE)], tdsc[:, pl.ds(start, TILE)]
        total = dot(t_low, rows_u[...], TN) + dot(d_low, rows_t[...], TN)
        total -= cvec[pl.ds(start, TILE), 0:1] * dot(d_low, rows_u[...], TN)
        return LOGIT_SCALE * total

    half_tiles = HALF // TILE
    passed = []
    for tile in range(half_tiles):
        terms = column_terms((1 - c) * half_tiles + tile)
        block = col_part.at[0, tile]
        block[...] = terms.reshape(block.shape)
        passed += over_c(block, col_recv.at[tile])
    for tile in range(half_tiles):
        terms = column_terms(c * half_tiles + tile)
        col_part[1, tile] = terms.reshape(col_part.shape[2:])
    for tile in range(half_tiles):
        passed[tile].wait_recv()
        col_part[1, tile] += col_recv[tile]
    copies = over_y(lambda r: col_part.at[1, r // 2, r % 2], lambda q: y_recv.at[q - 1])
    arrive(core_copies)
    y_grad[pl.ds(y, 1)] = sum_slots(core_grad, NC)[None]
    y_copies = spread_y(y_grad)

    for tile in range(WIDTH // TILE):
        span = slice(tile * TILE, (tile + 1) * TILE)
        u_piece = cols_u[:, :, :, :, span].reshape(COLS, TILE)
        t_piece = cols_t[:, :, :, :, span].reshape(COLS, TILE)
        total = dot(tdsc[...], u_piece) + dot(dsc[...], t_piece) - row_slope * dot(dsc[...], u_piece)
        row_part[:, :, span] = (LOGIT_SCALE * total).reshape(NM, SHARE, TILE)
    row_copies = over_m(lambda m: row_part.at[m], lambda q: row_recv.at[q - 1])

    arrive(y_copies)
    z_grad[pl.ds(zh, 1)] = sum_slots(y_grad, NY)[None]
    z_copies = spread_h(z_grad)
    arrive(grad_copies)
    grad_rows[...] = unpack_lanes(sum_slots(grad_slots, NM))
    arrive(copies)
    col_total = col_part[1, y // 2, y % 2] + y_recv[0] + y_recv[1] + y_recv[2]
    col_part[1, y // 2, y % 2] = col_total
    copies = over_h(lambda h: col_part.at[1, y // 2, y % 2, h], lambda q: z_recv.at[q - 1])
    arrive(z_copies)
    grad_cols[...] = unpack_lanes(sum_slots(z_grad, NH))

    def finish(raw, tangent, value, info):
        unit, inverse = unit_of(raw)
        turned, _ = turn_of(tangent, unit, inverse)
        mixed = info[:, 1:2] + jnp.sum(unit * value, -1, keepdims=True)
        return ((value - turned * info[:, 0:1] - unit * mixed) * inverse).astype(BF16)

    arrive(row_copies)
    value = row_part[mp]
    for q in range(NM - 1):
        value = value + row_recv[q]
    tdz[0, mp] = finish(rawbuf[own], tanbuf[own], value, grad_rows[own])
    arrive(copies)
    value = col_part[1, y // 2, y % 2, zh] + z_recv[0] + z_recv[1] + z_recv[2]
    tdz[1, mp] = finish(
        rawbuf[ROWS : ROWS + SHARE], tanbuf[ROWS : ROWS + SHARE], value, grad_cols[pl.ds(first_col, SHARE)]
    )
    copies = over_m(lambda m: tdz.at[:, mp], lambda q: tdz.at[:, mp])
    arrive(copies)

    curve = 0.0
    for tower in range(2):
        part = dot(feats[tower, :, pl.ds(pl.multiple_of(mp * PART, PART), PART)], tdz[tower].reshape(ROWS, WIDTH), TN)
        part_hess[tower] = part.reshape(part_hess.shape[1:])
        curve += jnp.sum(direc[tower] * part)
    passed = over_c(part_hess.at[1 - c], core_hess)
    scal_m[pl.ds(mp, 1)] = jnp.full((1, 8, 128), curve, F32)
    scal_copies = spread_m(scal_m)
    arrive(passed)
    part_hess[pl.ds(c, 1)] += core_hess[...][None]
    copies = over_y(lambda r: part_hess.at[c, r], lambda q: y_hess.at[q - 1])
    arrive(scal_copies)
    scal_c[pl.ds(c, 1)] = sum_slots(scal_m, NM)[None]
    scal_copies = spread_c(scal_c)
    arrive(scal_copies)
    scal_y[pl.ds(y, 1)] = sum_slots(scal_c, NC)[None]
    scal_copies = spread_y(scal_y)
    arrive(copies)
    part_hess[c, y] += y_hess[0] + y_hess[1] + y_hess[2]
    copies = over_h(lambda h: part_hess.at[c, y, h], lambda q: z_hess.at[q - 1])
    arrive(scal_copies)
    scal_z[pl.ds(zh, 1)] = sum_slots(scal_y, NY)[None]
    scal_copies = spread_h(scal_z)
    arrive(copies)
    hess[c, y, zh] = part_hess[c, y, zh] + z_hess[0] + z_hess[1] + z_hess[2]
    copies = over_h(lambda h: hess.at[c, y, zh], lambda q: hess.at[c, y, zh])
    arrive(scal_copies)
    curve = sum_slots(scal_z, NH)[0:1, 0:1] + DAMPING * norm_direc
    alpha = norm_old / curve
    piece = pl.ds(pl.multiple_of((y * NH + zh) * 8, 8), 8)
    after = resid[c, piece] - alpha * (hess[c, y, zh] + DAMPING * direc[c, piece])
    norm_m[pl.ds(mp, 1)] = jnp.full((1, 8, 128), jnp.sum(after * after), F32)
    scal_copies = spread_m(norm_m)
    arrive(copies)
    block = hess.at[c, y]
    copies = over_y(lambda r: block, lambda q: block)
    out_sol[...] = solu[...] + alpha * direc[...]
    arrive(scal_copies)
    norm_c[pl.ds(c, 1)] = sum_slots(norm_m, NM)[None]
    scal_copies = spread_c(norm_c)
    arrive(scal_copies)
    norm_y[pl.ds(y, 1)] = sum_slots(norm_c, NC)[None]
    scal_copies = spread_y(norm_y)
    arrive(copies)
    copies = over_c(hess.at[c], hess.at[c])
    arrive(scal_copies)
    norm_z[pl.ds(zh, 1)] = sum_slots(norm_y, NY)[None]
    scal_copies = spread_h(norm_z)
    arrive(copies)
    after = resid[...] - alpha * (hess[...].reshape(2, PART, WIDTH) + DAMPING * direc[...])
    out_res[...] = after
    arrive(scal_copies)
    norm_new = sum_slots(norm_z, NH)[0:1, 0:1]
    out_dir[...] = after + norm_new / norm_old * direc[...]
    for copy in pending:
        copy.wait_send()
    assert counter[0] <= SEMS


def body(features, projections, solution, residual, direction):
    vmem = pl.BlockSpec(memory_space=pltpu.VMEM)
    shape = jax.ShapeDtypeStruct((2, PART, WIDTH), F32)
    f32 = lambda *size: pltpu.VMEM(size, F32)
    bf16 = lambda *size: pltpu.VMEM(size, BF16)
    scratch = [
        bf16(2, 2, NM, PART, WIDTH),
        f32(ROWS + SHARE, WIDTH), f32(ROWS + SHARE, WIDTH),
        bf16(ROWS, WIDTH), bf16(ROWS, WIDTH),
        bf16(NC, NY, NH, SHARE, WIDTH), bf16(NC, NY, NH, SHARE, WIDTH),
        f32(ROWS, COLS), f32(ROWS, COLS), f32(ROWS, COLS),
        bf16(ROWS, COLS), bf16(ROWS, COLS), f32(COLS, 128),
        f32(NM, 8, ROWS), f32(NC, 8, COLS), f32(NY, 8, COLS), f32(NH, 8, COLS),
        f32(NM, 8, ROWS), f32(NC, 8, COLS), f32(NY, 8, COLS), f32(NH, 8, COLS),
        f32(NM, SHARE, WIDTH), f32(NM - 1, SHARE, WIDTH),
        f32(2, 2, 2, NH, SHARE, WIDTH), f32(2, 2, NH, SHARE, WIDTH),
        f32(NY - 1, NH, SHARE, WIDTH), f32(NH - 1, SHARE, WIDTH),
        f32(COLS, 128), f32(ROWS, 128),
        bf16(2, NM, SHARE, WIDTH),
        f32(2, NY, NH, 8, WIDTH), f32(NY, NH, 8, WIDTH),
        f32(NY - 1, NH, 8, WIDTH), f32(NH - 1, 8, WIDTH), f32(2, NY, NH, 8, WIDTH),
        f32(NM, 8, 128), f32(NC, 8, 128), f32(NY, 8, 128), f32(NH, 8, 128),
        f32(NM, 8, 128), f32(NC, 8, 128), f32(NY, 8, 128), f32(NH, 8, 128),
        pltpu.SemaphoreType.DMA((SEMS,)), pltpu.SemaphoreType.DMA((SEMS,)),
    ]
    return pl.pallas_call(
        kernel,
        name="cg_step",
        out_shape=(shape, shape, shape),
        in_specs=[vmem] * 5,
        out_specs=(vmem, vmem, vmem),
        scratch_shapes=scratch,
        compiler_params=pltpu.CompilerParams(
            collective_id=0, has_side_effects=True, vmem_limit_bytes=60 * 2**20
        ),
    )(features, projections, direction, residual, solution)


def solution(mesh):
    placed = (
        P(None, "dp", None),
        P(None, "mp", None),
        P(None, "mp", None),
        P(None, "mp", None),
        P(None, "mp", None),
    )
    return jax.shard_map(
        body,
        mesh=mesh,
        in_specs=placed,
        out_specs=(P(None, "mp", None), P(None, "mp", None), P(None, "mp", None)),
        check_vma=False,
    )
```

```python
import functools

import jax
import jax.numpy as jnp
from jax import lax
from jax.experimental import pallas as pl
from jax.experimental.pallas import tpu as pltpu
from jax.sharding import PartitionSpec as P

LOGIT_SCALE = 100.0
DAMPING = 1.0
EPSILON = 1e-06

NC, NY, NH, NX, NL = 2, 4, 4, 4, 2
NM = NX * NL
ROWS, DEPTH, WIDTH = 256, 1024, 768
PART = DEPTH // NM
SHARE = ROWS // NM
COLS = SHARE * NC * NY * NH
HALF = COLS // NC
PAIRS = ROWS * NC * NY * NH
TILE = 256
SEMS = 224
QUARTER = 16
DIRECT = PART - NY * QUARTER
F32, BF16 = jnp.float32, jnp.bfloat16
MESH = pl.DeviceIdType.MESH


def dot(left, right, dims=((1,), (0,))):
    return lax.dot_general(left, right, (dims, ((), ())), preferred_element_type=F32)


def unit_of(raw):
    inverse = lax.rsqrt(jnp.sum(raw * raw, -1, keepdims=True) + EPSILON)
    return raw * inverse, inverse


def turn_of(tangent, unit, inverse):
    along = jnp.sum(unit * tangent, -1, keepdims=True)
    return (tangent - unit * along) * inverse, along


def pack_lanes(columns):
    size = columns[0].shape[0]
    lane = lax.broadcasted_iota(jnp.int32, (size, 128), 1)
    wide = jnp.zeros((size, 128), F32)
    for place, column in enumerate(columns):
        wide = jnp.where(lane == place, column, wide)
    return wide.T[0:8]


def unpack_lanes(rows):
    return jnp.concatenate([rows, jnp.zeros((120, rows.shape[1]), F32)], 0).T


def stack_rows(rows):
    size = rows[0].shape[1]
    return jnp.concatenate(list(rows) + [jnp.zeros((8 - len(rows), size), F32)], 0)


def softmax_join(slots):
    top = functools.reduce(jnp.maximum, [slot[0] for slot in slots])
    total = 0.0
    weighted = 0.0
    for slot in slots:
        factor = jnp.exp(slot[0] - top)
        total = total + factor * slot[1]
        weighted = weighted + factor * slot[2]
    return top, total, weighted


def kernel(
    feats_in, proj_in, direc_in, resid_in,
    hess_out, info_out,
    feats, direc, resid, weights, quarters, rawbuf, tanbuf, rows_u, rows_t, cols_u, cols_t,
    scores, left_ts, right_ts, dsc, tdsc, cvec,
    row_slots, core_stat, y_stat, z_stat,
    grad_slots, core_grad, y_grad, z_grad,
    row_part, row_recv, col_part, col_recv, y_recv, z_recv,
    grad_cols, grad_rows, tdz, part_hess, core_hess, y_hess, z_hess, hess,
    scal_m, scal_c, scal_y, scal_z, norm_m, norm_c, norm_y, norm_z,
    send_sem, recv_sem, load_sem,
):
    dp, mp = lax.axis_index("dp"), lax.axis_index("mp")
    c, y, zh = dp % NC, (dp // NC) % NY, dp // (NC * NY)
    x, zl = mp % NX, mp // NX
    counter = [0]

    def device(core=None, row=None, high=None, model=None):
        core, row, high = c if core is None else core, y if row is None else row, zh if high is None else high
        return {"dp": (high * NY + row) * NC + core, "mp": mp if model is None else model}

    def m_at(step):
        return ((zl + step // NX) % NL) * NX + (x + step % NX) % NX

    def m_from(step):
        return ((zl + step // NX) % NL) * NX + (x + NX - step % NX) % NX

    def y_at(step):
        return (y + step) % NY

    def h_at(step):
        return (zh + step) % NH

    def send(source, target, where):
        place = counter[0]
        counter[0] += 1
        copy = pltpu.make_async_remote_copy(
            src_ref=source, dst_ref=target, send_sem=send_sem.at[place], recv_sem=recv_sem.at[place],
            device_id=where, device_id_type=MESH,
        )
        copy.start()
        pending.append(copy)
        return copy

    pending = []

    def arrive(copies):
        for copy in copies:
            copy.wait_recv()

    def over_m(source, target):
        return [send(source(m_at(q)), target(q), device(model=m_at(q))) for q in range(1, NM)]

    def over_y(source, target):
        return [send(source(y_at(q)), target(q), device(row=y_at(q))) for q in range(1, NY)]

    def over_h(source, target):
        return [send(source(h_at(q)), target(q), device(high=h_at(q))) for q in range(1, NH)]

    def over_c(source, target):
        return [send(source, target, device(core=1 - c))]

    def load(source, target, place):
        copy = pltpu.make_async_copy(source, target, load_sem.at[place])
        copy.start()
        return copy

    load_direc = [load(direc_in.at[tower], direc.at[tower], tower) for tower in (1, 0)]
    load_proj = [load(proj_in.at[tower], weights.at[0, tower, mp], 2 + tower) for tower in (1, 0)]
    load_feats = [load(feats_in.at[tower], feats.at[tower], 4 + tower) for tower in (1, 0)]
    load_resid = load(resid_in, resid, 6)

    barrier = pltpu.get_barrier_semaphore()
    for q in range(1, NM):
        pl.semaphore_signal(barrier, inc=1, device_id=device(model=m_at(q)), device_id_type=MESH)
    for q in range(1, NY):
        pl.semaphore_signal(barrier, inc=1, device_id=device(row=y_at(q)), device_id_type=MESH)
    for q in range(1, NH):
        pl.semaphore_signal(barrier, inc=1, device_id=device(high=h_at(q)), device_id_type=MESH)
    pl.semaphore_signal(barrier, inc=1, device_id=device(core=1 - c), device_id_type=MESH)
    load_direc[0].wait()
    weights[1, 1, pl.ds(mp, 1)] = direc[1].astype(BF16)[None]
    load_proj[0].wait()
    pl.semaphore_wait(barrier, NM + NY + NH - 2)

    part = weights.at[c, 1, mp, pl.ds(pl.multiple_of(DIRECT + y * QUARTER, QUARTER), QUARTER)]
    quarter_copies = over_m(lambda m: part, lambda q: quarters.at[c, y, q - 1])
    whole = weights.at[c, 1, mp, pl.ds(0, DIRECT)]
    direct_copies = over_m(lambda m: whole, lambda q: whole)
    load_direc[1].wait()
    weights[1, 0, pl.ds(mp, 1)] = direc[0].astype(BF16)[None]
    load_proj[1].wait()
    arrive(quarter_copies)
    mine = quarters.at[c, y]
    row_copies = over_y(lambda r: mine, lambda q: mine)
    passed = over_c(mine, mine)
    for q, copy in enumerate(direct_copies, 1):
        copy.wait_recv()
        block = weights.at[c, 1, m_from(q), pl.ds(0, DIRECT)]
        passed += over_c(block, block)

    whole_sar = weights.at[c, 0, mp]
    sar_copies = over_m(lambda m: whole_sar, lambda q: whole_sar)
    for q, copy in enumerate(row_copies, 1):
        copy.wait_recv()
        block = quarters.at[c, (y + NY - q) % NY]
        passed += over_c(block, block)
    load_feats[0].wait()
    arrive(passed)
    for kind in range(2):
        for q in range(1, NM):
            for r in range(NY):
                weights[kind, 1, m_from(q), DIRECT + r * QUARTER : DIRECT + (r + 1) * QUARTER] = quarters[kind, r, q - 1]

    def embed(kind, tower, rows, into, first):
        for tile in range(WIDTH // TILE):
            span = slice(tile * TILE, (tile + 1) * TILE)
            total = 0.0
            for block in range(0, NM, 2):
                deep = slice(block * PART, (block + 2) * PART)
                piece = weights[kind, tower, block : block + 2, :, span].reshape(2 * PART, TILE)
                total += dot(feats[tower, rows, deep], piece)
            into[first : first + total.shape[0], span] = total

    own = pl.ds(pl.multiple_of(mp * SHARE, SHARE), SHARE)
    embed(0, 1, own, rawbuf, ROWS)
    embed(1, 1, own, tanbuf, ROWS)
    unit, inverse = unit_of(rawbuf[ROWS : ROWS + SHARE])
    turned, along = turn_of(tanbuf[ROWS : ROWS + SHARE], unit, inverse)
    cols_u[c, y, zh] = unit.astype(BF16)
    cols_t[c, y, zh] = turned.astype(BF16)
    slope = inverse * along

    def columns_high(cols):
        block = cols.at[c, y, zh]
        return over_h(lambda h: block, lambda q: block)

    def columns_row(cols):
        block = cols.at[c, y]
        return over_y(lambda r: block, lambda q: block)

    def columns_core(cols, copies):
        passed = over_c(cols.at[c, y], cols.at[c, y])
        for q, copy in enumerate(copies, 1):
            copy.wait_recv()
            block = cols.at[c, (y + NY - q) % NY]
            passed += over_c(block, block)
        return passed

    high_u = columns_high(cols_u)
    high_t = columns_high(cols_t)
    first_col = pl.multiple_of(((c * NY + y) * NH + zh) * SHARE, SHARE)
    cvec[...] = jnp.zeros_like(cvec)
    cvec[pl.ds(first_col, SHARE)] = jnp.broadcast_to(slope, (SHARE, 128))
    slope_row = cvec[...].T[0:1]
    arrive(high_u)
    copies_u = columns_row(cols_u)
    arrive(high_t)
    copies_t = columns_row(cols_t)
    passed_u = columns_core(cols_u, copies_u)
    passed = []
    for q, copy in enumerate(sar_copies, 1):
        copy.wait_recv()
        block = weights.at[c, 0, m_from(q)]
        passed += over_c(block, block)
    load_feats[1].wait()
    arrive(passed)
    passed_t = columns_core(cols_t, copies_t)
    every = slice(0, ROWS)
    embed(0, 0, every, rawbuf, 0)
    embed(1, 0, every, tanbuf, 0)
    unit, inverse = unit_of(rawbuf[every])
    turned, along = turn_of(tanbuf[every], unit, inverse)
    rows_u[...] = unit.astype(BF16)
    rows_t[...] = turned.astype(BF16)
    row_slope = inverse * along
    arrive(passed_u)

    def column_tile(cols, tile):
        return cols[tile // 2, (tile % 2) * 2 : (tile % 2) * 2 + 2].reshape(TILE, WIDTH)

    NT = ((1,), (1,))
    tiles = COLS // TILE
    for tile in range(tiles):
        span = slice(tile * TILE, (tile + 1) * TILE)
        piece = column_tile(cols_u, tile)
        scores[:, span] = LOGIT_SCALE * dot(rows_u[...], piece, NT)
        left_ts[:, span] = LOGIT_SCALE * dot(rows_t[...], piece, NT)
    row_max = jnp.max(scores[...], 1, keepdims=True)
    col_max = jnp.max(scores[...], 0, keepdims=True)
    arrive(passed_t)
    for tile in range(tiles):
        span = slice(tile * TILE, (tile + 1) * TILE)
        right_ts[:, span] = LOGIT_SCALE * dot(rows_u[...], column_tile(cols_t, tile), NT)

    row_sum = jnp.zeros((ROWS, 1), F32)
    row_weighted = jnp.zeros((ROWS, 1), F32)
    col_sum, col_weighted = [], []
    for tile in range(tiles):
        span = slice(tile * TILE, (tile + 1) * TILE)
        score = scores[:, span]
        tscore = left_ts[:, span] + right_ts[:, span]
        weight = jnp.exp(score - row_max)
        row_sum += jnp.sum(weight, 1, keepdims=True)
        row_weighted += jnp.sum(weight * tscore, 1, keepdims=True)
        weight = jnp.exp(score - col_max[:, span])
        col_sum.append(jnp.sum(weight, 0, keepdims=True))
        col_weighted.append(jnp.sum(weight * tscore, 0, keepdims=True))
    load_resid.wait()
    resid_norm = jnp.sum(resid[...] * resid[...])
    direc_norm = jnp.sum(direc[...] * direc[...])
    constant = lambda value: jnp.full((ROWS, 1), value, F32)
    row_slots[pl.ds(mp, 1)] = pack_lanes(
        [row_max, row_sum, row_weighted, constant(resid_norm), constant(direc_norm)]
    )[None]
    core_stat[pl.ds(c, 1)] = stack_rows(
        [col_max, jnp.concatenate(col_sum, 1), jnp.concatenate(col_weighted, 1), slope_row]
    )[None]

    def join_columns(slots, count):
        parts = [slots[k] for k in range(count)]
        top, total, weighted = softmax_join([(part[0:1], part[1:2], part[2:3]) for part in parts])
        slopes = functools.reduce(jnp.add, [part[3:4] for part in parts])
        return top, total, weighted, slopes

    def sum_slots(slots, count):
        return functools.reduce(jnp.add, [slots[k] for k in range(count)])

    def spread_c(slots):
        return over_c(slots.at[c], slots.at[c])

    def spread_y(slots):
        return over_y(lambda r: slots.at[y], lambda q: slots.at[y])

    def spread_h(slots):
        return over_h(lambda h: slots.at[zh], lambda q: slots.at[zh])

    def spread_m(slots):
        return over_m(lambda m: slots.at[mp], lambda q: slots.at[mp])

    copies = spread_c(core_stat)
    row_copies = spread_m(row_slots)
    arrive(copies)
    y_stat[pl.ds(y, 1)] = stack_rows(join_columns(core_stat, NC))[None]
    copies = spread_y(y_stat)
    arrive(copies)
    z_stat[pl.ds(zh, 1)] = stack_rows(join_columns(y_stat, NY))[None]
    copies = spread_h(z_stat)
    arrive(row_copies)
    parts = [row_slots[k] for k in range(NM)]
    top, total, weighted = softmax_join([(part[0:1], part[1:2], part[2:3]) for part in parts])
    norms = functools.reduce(jnp.add, [part[3:5] for part in parts])
    norm_old = norms[0:1, 0:1]
    norm_direc = norms[1:2, 0:1]
    row_info = unpack_lanes(stack_rows([top + jnp.log(total), weighted / total]))
    row_lse, row_dot = row_info[:, 0:1], row_info[:, 1:2]
    arrive(copies)
    top, total, weighted, slopes = join_columns(z_stat, NH)
    col_lse, col_dot = top + jnp.log(total), weighted / total
    col_slope = unpack_lanes(stack_rows([slopes]))

    row_ids = lax.broadcasted_iota(jnp.int32, (ROWS, TILE), 0)
    col_ids = lax.broadcasted_iota(jnp.int32, (ROWS, TILE), 1)
    offset = mp * SHARE - first_col
    row_along = jnp.zeros((ROWS, 1), F32)
    row_turned = jnp.zeros((ROWS, 1), F32)
    col_along, col_turned = [], []
    for tile in range(tiles):
        span = slice(tile * TILE, (tile + 1) * TILE)
        score = scores[:, span]
        left, right = left_ts[:, span], right_ts[:, span]
        tscore = left + right
        row_w = jnp.exp(score - row_lse)
        col_w = jnp.exp(score - col_lse[:, span])
        place = col_ids + tile * TILE
        mine = (place >= first_col) & (place < first_col + SHARE) & (row_ids == place + offset)
        low = ((row_w + col_w - 2.0 * mine.astype(F32)) / (2.0 * PAIRS)).astype(BF16)
        dsc[:, span] = low
        tdsc[:, span] = (
            (row_w * (tscore - row_dot) + col_w * (tscore - col_dot[:, span])) / (2.0 * PAIRS)
        ).astype(BF16)
        wide = low.astype(F32)
        row_along += jnp.sum(wide * score, 1, keepdims=True)
        row_turned += jnp.sum(wide * left, 1, keepdims=True)
        col_along.append(jnp.sum(wide * score, 0, keepdims=True))
        col_turned.append(jnp.sum(wide * right, 0, keepdims=True))
    grad_slots[pl.ds(mp, 1)] = pack_lanes([row_along, row_turned])[None]
    core_grad[pl.ds(c, 1)] = stack_rows([jnp.concatenate(col_along, 1), jnp.concatenate(col_turned, 1)])[None]
    grad_copies = spread_m(grad_slots)
    core_copies = spread_c(core_grad)

    TN = ((0,), (0,))
    cvec[...] = col_slope

    def column_terms(tile):
        start = pl.multiple_of(tile * TILE, TILE)
        d_low, t_low = dsc[:, pl.ds(start, TILE)], tdsc[:, pl.ds(start, TILE)]
        total = dot(t_low, rows_u[...], TN) + dot(d_low, rows_t[...], TN)
        total -= cvec[pl.ds(start, TILE), 0:1] * dot(d_low, rows_u[...], TN)
        return LOGIT_SCALE * total

    half_tiles = HALF // TILE
    passed = []
    for tile in range(half_tiles):
        terms = column_terms((1 - c) * half_tiles + tile)
        block = col_part.at[0, tile]
        block[...] = terms.reshape(block.shape)
        passed += over_c(block, col_recv.at[tile])
    for tile in range(half_tiles):
        terms = column_terms(c * half_tiles + tile)
        col_part[1, tile] = terms.reshape(col_part.shape[2:])
    for tile in range(half_tiles):
        passed[tile].wait_recv()
        col_part[1, tile] += col_recv[tile]
    copies = over_y(lambda r: col_part.at[1, r // 2, r % 2], lambda q: y_recv.at[q - 1])
    arrive(core_copies)
    y_grad[pl.ds(y, 1)] = sum_slots(core_grad, NC)[None]
    y_copies = spread_y(y_grad)

    for tile in range(WIDTH // TILE):
        span = slice(tile * TILE, (tile + 1) * TILE)
        u_piece = cols_u[:, :, :, :, span].reshape(COLS, TILE)
        t_piece = cols_t[:, :, :, :, span].reshape(COLS, TILE)
        total = dot(tdsc[...], u_piece) + dot(dsc[...], t_piece) - row_slope * dot(dsc[...], u_piece)
        row_part[:, :, span] = (LOGIT_SCALE * total).reshape(NM, SHARE, TILE)
    row_copies = over_m(lambda m: row_part.at[m], lambda q: row_recv.at[q - 1])

    arrive(y_copies)
    z_grad[pl.ds(zh, 1)] = sum_slots(y_grad, NY)[None]
    z_copies = spread_h(z_grad)
    arrive(grad_copies)
    grad_rows[...] = unpack_lanes(sum_slots(grad_slots, NM))
    arrive(copies)
    col_total = col_part[1, y // 2, y % 2] + y_recv[0] + y_recv[1] + y_recv[2]
    col_part[1, y // 2, y % 2] = col_total
    copies = over_h(lambda h: col_part.at[1, y // 2, y % 2, h], lambda q: z_recv.at[q - 1])
    arrive(z_copies)
    grad_cols[...] = unpack_lanes(sum_slots(z_grad, NH))

    def finish(raw, tangent, value, info):
        unit, inverse = unit_of(raw)
        turned, _ = turn_of(tangent, unit, inverse)
        mixed = info[:, 1:2] + jnp.sum(unit * value, -1, keepdims=True)
        return ((value - turned * info[:, 0:1] - unit * mixed) * inverse).astype(BF16)

    arrive(row_copies)
    value = row_part[mp]
    for q in range(NM - 1):
        value = value + row_recv[q]
    tdz[0, mp] = finish(rawbuf[own], tanbuf[own], value, grad_rows[own])
    arrive(copies)
    value = col_part[1, y // 2, y % 2, zh] + z_recv[0] + z_recv[1] + z_recv[2]
    tdz[1, mp] = finish(
        rawbuf[ROWS : ROWS + SHARE], tanbuf[ROWS : ROWS + SHARE], value, grad_cols[pl.ds(first_col, SHARE)]
    )
    copies = over_m(lambda m: tdz.at[:, mp], lambda q: tdz.at[:, mp])
    arrive(copies)

    curve = 0.0
    for tower in range(2):
        part = dot(feats[tower, :, pl.ds(pl.multiple_of(mp * PART, PART), PART)], tdz[tower].reshape(ROWS, WIDTH), TN)
        part_hess[tower] = part.reshape(part_hess.shape[1:])
        curve += jnp.sum(direc[tower] * part)
    passed = over_c(part_hess.at[1 - c], core_hess)
    scal_m[pl.ds(mp, 1)] = jnp.full((1, 8, 128), curve, F32)
    scal_copies = spread_m(scal_m)
    arrive(passed)
    part_hess[pl.ds(c, 1)] += core_hess[...][None]
    copies = over_y(lambda r: part_hess.at[c, r], lambda q: y_hess.at[q - 1])
    arrive(scal_copies)
    scal_c[pl.ds(c, 1)] = sum_slots(scal_m, NM)[None]
    scal_copies = spread_c(scal_c)
    arrive(scal_copies)
    scal_y[pl.ds(y, 1)] = sum_slots(scal_c, NC)[None]
    scal_copies = spread_y(scal_y)
    arrive(copies)
    part_hess[c, y] += y_hess[0] + y_hess[1] + y_hess[2]
    copies = over_h(lambda h: part_hess.at[c, y, h], lambda q: z_hess.at[q - 1])
    arrive(scal_copies)
    scal_z[pl.ds(zh, 1)] = sum_slots(scal_y, NY)[None]
    scal_copies = spread_h(scal_z)
    arrive(copies)
    hess[c, y, zh] = part_hess[c, y, zh] + z_hess[0] + z_hess[1] + z_hess[2]
    copies = over_h(lambda h: hess.at[c, y, zh], lambda q: hess.at[c, y, zh])
    arrive(scal_copies)
    curve = sum_slots(scal_z, NH)[0:1, 0:1] + DAMPING * norm_direc
    alpha = norm_old / curve
    piece = pl.ds(pl.multiple_of((y * NH + zh) * 8, 8), 8)
    after = resid[c, piece] - alpha * (hess[c, y, zh] + DAMPING * direc[c, piece])
    norm_m[pl.ds(mp, 1)] = jnp.full((1, 8, 128), jnp.sum(after * after), F32)
    scal_copies = spread_m(norm_m)
    arrive(copies)
    block = hess.at[c, y]
    copies = over_y(lambda r: block, lambda q: block)
    arrive(scal_copies)
    norm_c[pl.ds(c, 1)] = sum_slots(norm_m, NM)[None]
    scal_copies = spread_c(norm_c)
    arrive(scal_copies)
    norm_y[pl.ds(y, 1)] = sum_slots(norm_c, NC)[None]
    scal_copies = spread_y(norm_y)
    arrive(copies)
    copies = over_c(hess.at[c], hess.at[c])
    arrive(scal_copies)
    norm_z[pl.ds(zh, 1)] = sum_slots(norm_y, NY)[None]
    scal_copies = spread_h(norm_z)
    arrive(copies)
    arrive(scal_copies)
    store = load(hess, hess_out, 7)
    norm_new = sum_slots(norm_z, NH)[0:1, 0:1]
    first_row = lax.broadcasted_iota(jnp.int32, (8, 128), 0) == 0
    info_out[...] = jnp.where(first_row, alpha, norm_new / norm_old)
    store.wait()
    for copy in pending:
        copy.wait_send()
    assert counter[0] <= SEMS


def body(features, projections, solution, residual, direction):
    vmem = pl.BlockSpec(memory_space=pltpu.VMEM)
    hbm = pl.BlockSpec(memory_space=pl.ANY)
    f32 = lambda *size: pltpu.VMEM(size, F32)
    bf16 = lambda *size: pltpu.VMEM(size, BF16)
    scratch = [
        bf16(2, ROWS, DEPTH), f32(2, PART, WIDTH), f32(2, PART, WIDTH),
        bf16(2, 2, NM, PART, WIDTH), bf16(2, NY, NM - 1, QUARTER, WIDTH),
        f32(ROWS + SHARE, WIDTH), f32(ROWS + SHARE, WIDTH),
        bf16(ROWS, WIDTH), bf16(ROWS, WIDTH),
        bf16(NC, NY, NH, SHARE, WIDTH), bf16(NC, NY, NH, SHARE, WIDTH),
        f32(ROWS, COLS), f32(ROWS, COLS), f32(ROWS, COLS),
        bf16(ROWS, COLS), bf16(ROWS, COLS), f32(COLS, 128),
        f32(NM, 8, ROWS), f32(NC, 8, COLS), f32(NY, 8, COLS), f32(NH, 8, COLS),
        f32(NM, 8, ROWS), f32(NC, 8, COLS), f32(NY, 8, COLS), f32(NH, 8, COLS),
        f32(NM, SHARE, WIDTH), f32(NM - 1, SHARE, WIDTH),
        f32(2, 2, 2, NH, SHARE, WIDTH), f32(2, 2, NH, SHARE, WIDTH),
        f32(NY - 1, NH, SHARE, WIDTH), f32(NH - 1, SHARE, WIDTH),
        f32(COLS, 128), f32(ROWS, 128),
        bf16(2, NM, SHARE, WIDTH),
        f32(2, NY, NH, 8, WIDTH), f32(NY, NH, 8, WIDTH),
        f32(NY - 1, NH, 8, WIDTH), f32(NH - 1, 8, WIDTH), f32(2, NY, NH, 8, WIDTH),
        f32(NM, 8, 128), f32(NC, 8, 128), f32(NY, 8, 128), f32(NH, 8, 128),
        f32(NM, 8, 128), f32(NC, 8, 128), f32(NY, 8, 128), f32(NH, 8, 128),
        pltpu.SemaphoreType.DMA((SEMS,)), pltpu.SemaphoreType.DMA((SEMS,)), pltpu.SemaphoreType.DMA((8,)),
    ]
    hess, info = pl.pallas_call(
        kernel,
        name="cg_step",
        out_shape=(
            jax.ShapeDtypeStruct((2, NY, NH, 8, WIDTH), F32),
            jax.ShapeDtypeStruct((8, 128), F32),
        ),
        in_specs=[hbm] * 4,
        out_specs=(hbm, vmem),
        scratch_shapes=scratch,
        compiler_params=pltpu.CompilerParams(
            collective_id=0, has_side_effects=True, vmem_limit_bytes=60 * 2**20
        ),
    )(features, projections, direction, residual)
    alpha, beta = info[0, 0], info[1, 0]
    hess = hess.reshape(direction.shape) + DAMPING * direction
    new_residual = residual - alpha * hess
    return solution + alpha * direction, new_residual, new_residual + beta * direction


def solution(mesh):
    placed = (
        P(None, "dp", None),
        P(None, "mp", None),
        P(None, "mp", None),
        P(None, "mp", None),
        P(None, "mp", None),
    )
    return jax.shard_map(
        body,
        mesh=mesh,
        in_specs=placed,
        out_specs=(P(None, "mp", None), P(None, "mp", None), P(None, "mp", None)),
        check_vma=False,
    )
```

```python
import functools

import jax
import jax.numpy as jnp
from jax import lax
from jax.experimental import pallas as pl
from jax.experimental.pallas import tpu as pltpu
from jax.sharding import PartitionSpec as P

LOGIT_SCALE = 100.0
DAMPING = 1.0
EPSILON = 1e-06

NC, NY, NH, NX, NL = 2, 4, 4, 4, 2
NM = NX * NL
ROWS, DEPTH, WIDTH = 256, 1024, 768
PART = DEPTH // NM
SHARE = ROWS // NM
COLS = SHARE * NC * NY * NH
HALF = COLS // NC
PAIRS = ROWS * NC * NY * NH
TILE = 256
SEMS = 224
QUARTER = 16
DIRECT = PART - NY * QUARTER
WIDE = WIDTH // 2
BLOCK = PART // NY
F32, BF16 = jnp.float32, jnp.bfloat16
MESH = pl.DeviceIdType.MESH


def dot(left, right, dims=((1,), (0,))):
    return lax.dot_general(left, right, (dims, ((), ())), preferred_element_type=F32)


def unit_of(raw):
    inverse = lax.rsqrt(jnp.sum(raw * raw, -1, keepdims=True) + EPSILON)
    return raw * inverse, inverse


def turn_of(tangent, unit, inverse):
    along = jnp.sum(unit * tangent, -1, keepdims=True)
    return (tangent - unit * along) * inverse, along


def pack_lanes(columns):
    size = columns[0].shape[0]
    lane = lax.broadcasted_iota(jnp.int32, (size, 128), 1)
    wide = jnp.zeros((size, 128), F32)
    for place, column in enumerate(columns):
        wide = jnp.where(lane == place, column, wide)
    return wide.T[0:8]


def unpack_lanes(rows):
    return jnp.concatenate([rows, jnp.zeros((128 - rows.shape[0], rows.shape[1]), F32)], 0).T


def fold(rows):
    size = rows[0].shape[1] * len(rows) // 8
    stacked = jnp.concatenate(rows, 0)
    return jnp.concatenate([stacked[:, k : k + size] for k in range(0, stacked.shape[1], size)], 0)


def unfold(block, count):
    return jnp.concatenate([block[k : k + count] for k in range(0, 8, count)], 1)


def softmax_join(slots):
    top = functools.reduce(jnp.maximum, [slot[0] for slot in slots])
    total = 0.0
    weighted = 0.0
    for slot in slots:
        factor = jnp.exp(slot[0] - top)
        total = total + factor * slot[1]
        weighted = weighted + factor * slot[2]
    return top, total, weighted


def kernel(
    feats_in, proj_in, direc_in, resid_in,
    hess_out, info_out,
    feats, direc, resid, weights, quarters, rawbuf, tanbuf, rows_u, rows_t, cols_u, cols_t,
    scores, left_ts, right_ts, dsc, tdsc, cvec,
    row_slots, core_stat, y_stat, z_stat,
    grad_slots, core_grad, y_grad, z_grad,
    row_part, x_recv, l_recv, col_part, col_recv, y_recv, z_recv,
    grad_cols, grad_rows, tdz, part_hess, core_hess, y_hess, z_hess, hess,
    scal_m, scal_p, scal_z, norm_p, norm_m,
    send_sem, recv_sem, load_sem,
):
    dp, mp = lax.axis_index("dp"), lax.axis_index("mp")
    c, y, zh = dp % NC, (dp // NC) % NY, dp // (NC * NY)
    x, zl = mp % NX, mp // NX
    partner = (1 - zl) * NX + x
    counter = [0]

    def device(core=None, row=None, high=None, model=None):
        core, row, high = c if core is None else core, y if row is None else row, zh if high is None else high
        return {"dp": (high * NY + row) * NC + core, "mp": mp if model is None else model}

    def m_at(step):
        return ((zl + step // NX) % NL) * NX + (x + step % NX) % NX

    def m_from(step):
        return ((zl + step // NX) % NL) * NX + (x + NX - step % NX) % NX

    def x_at(step):
        return (x + step) % NX

    def y_at(step):
        return (y + step) % NY

    def h_at(step):
        return (zh + step) % NH

    def send(source, target, where):
        place = counter[0]
        counter[0] += 1
        copy = pltpu.make_async_remote_copy(
            src_ref=source, dst_ref=target, send_sem=send_sem.at[place], recv_sem=recv_sem.at[place],
            device_id=where, device_id_type=MESH,
        )
        copy.start()
        pending.append(copy)
        return copy

    pending = []

    def arrive(copies):
        for copy in copies:
            copy.wait_recv()

    def over_m(source, target):
        return [send(source(m_at(q)), target(q), device(model=m_at(q))) for q in range(1, NM)]

    def over_y(source, target):
        return [send(source(y_at(q)), target(q), device(row=y_at(q))) for q in range(1, NY)]

    def over_h(source, target):
        return [send(source(h_at(q)), target(q), device(high=h_at(q))) for q in range(1, NH)]

    def over_x(source, target):
        return [send(source(x_at(q)), target(q), device(model=zl * NX + x_at(q))) for q in range(1, NX)]

    def over_l(source, target):
        return [send(source, target, device(model=partner))]

    def over_plane(slots):
        place = slots.at[c * NY + y]
        return [
            send(place, place, device(core=(c + q // NY) % NC, row=(y + q % NY) % NY)) for q in range(1, NC * NY)
        ]

    def over_c(source, target):
        return [send(source, target, device(core=1 - c))]

    def load(source, target, place):
        copy = pltpu.make_async_copy(source, target, load_sem.at[place])
        copy.start()
        return copy

    load_direc = [load(direc_in.at[tower], direc.at[tower], tower) for tower in (1, 0)]
    load_proj = [load(proj_in.at[tower], weights.at[0, tower, mp], 2 + tower) for tower in (1, 0)]
    load_feats = [load(feats_in.at[tower], feats.at[tower], 4 + tower) for tower in (1, 0)]
    load_resid = load(resid_in, resid, 6)

    barrier = pltpu.get_barrier_semaphore()
    for q in range(1, NM):
        pl.semaphore_signal(barrier, inc=1, device_id=device(model=m_at(q)), device_id_type=MESH)
    for q in range(1, NC * NY):
        where = device(core=(c + q // NY) % NC, row=(y + q % NY) % NY)
        pl.semaphore_signal(barrier, inc=1, device_id=where, device_id_type=MESH)
    for q in range(1, NH):
        pl.semaphore_signal(barrier, inc=1, device_id=device(high=h_at(q)), device_id_type=MESH)
    load_direc[0].wait()
    weights[1, 1, pl.ds(mp, 1)] = direc[1].astype(BF16)[None]
    load_proj[0].wait()
    pl.semaphore_wait(barrier, NM + NC * NY + NH - 3)

    part = weights.at[c, 1, mp, pl.ds(pl.multiple_of(DIRECT + y * QUARTER, QUARTER), QUARTER)]
    quarter_copies = over_m(lambda m: part, lambda q: quarters.at[c, y, q - 1])
    def optical(m):
        return weights.at[c, 1, m, pl.ds(0, DIRECT)]

    def sar(m):
        return weights.at[c, 0, m]

    def spread_x(block):
        return over_x(lambda m: block, lambda q: block)

    def pass_on(blocks, low, copies):
        passed = []
        for q, copy in enumerate(copies, 1):
            copy.wait_recv()
            block = blocks(low * NX + (x + NX - q) % NX)
            passed += over_c(block, block)
        return passed

    l_copies = over_l(optical(mp), optical(mp))
    x_copies = spread_x(optical(mp))
    load_direc[1].wait()
    weights[1, 0, pl.ds(mp, 1)] = direc[0].astype(BF16)[None]
    load_proj[1].wait()
    sar_l_copies = over_l(sar(mp), sar(mp))
    arrive(quarter_copies)
    mine = quarters.at[c, y]
    row_copies = over_y(lambda r: mine, lambda q: mine)
    arrive(l_copies)
    x_relays = spread_x(optical(partner))
    passed = over_c(mine, mine) + over_c(optical(partner), optical(partner))
    passed += pass_on(optical, zl, x_copies)
    sar_x_copies = spread_x(sar(mp))
    passed += pass_on(optical, 1 - zl, x_relays)
    arrive(sar_l_copies)
    sar_x_relays = spread_x(sar(partner))
    for q, copy in enumerate(row_copies, 1):
        copy.wait_recv()
        block = quarters.at[c, (y + NY - q) % NY]
        passed += over_c(block, block)
    load_feats[0].wait()
    arrive(passed)
    for kind in range(2):
        for q in range(1, NM):
            for r in range(NY):
                weights[kind, 1, m_from(q), DIRECT + r * QUARTER : DIRECT + (r + 1) * QUARTER] = quarters[kind, r, q - 1]

    def embed(kind, tower, rows, into, first):
        for tile in range(WIDTH // TILE):
            span = slice(tile * TILE, (tile + 1) * TILE)
            total = 0.0
            for block in range(0, NM, 2):
                deep = slice(block * PART, (block + 2) * PART)
                piece = weights[kind, tower, block : block + 2, :, span].reshape(2 * PART, TILE)
                total += dot(feats[tower, rows, deep], piece)
            into[first : first + total.shape[0], span] = total

    own = pl.ds(pl.multiple_of(mp * SHARE, SHARE), SHARE)
    embed(0, 1, own, rawbuf, ROWS)
    embed(1, 1, own, tanbuf, ROWS)
    unit, inverse = unit_of(rawbuf[ROWS : ROWS + SHARE])
    turned, along = turn_of(tanbuf[ROWS : ROWS + SHARE], unit, inverse)
    cols_u[c, y, zh] = unit.astype(BF16)
    cols_t[c, y, zh] = turned.astype(BF16)
    slope = inverse * along

    def columns_high(cols):
        block = cols.at[c, y, zh]
        return over_h(lambda h: block, lambda q: block)

    def columns_row(cols):
        block = cols.at[c, y]
        return over_y(lambda r: block, lambda q: block)

    def columns_core(cols, copies):
        passed = over_c(cols.at[c, y], cols.at[c, y])
        for q, copy in enumerate(copies, 1):
            copy.wait_recv()
            block = cols.at[c, (y + NY - q) % NY]
            passed += over_c(block, block)
        return passed

    high_u = columns_high(cols_u)
    high_t = columns_high(cols_t)
    first_col = pl.multiple_of(((c * NY + y) * NH + zh) * SHARE, SHARE)
    cvec[...] = jnp.zeros_like(cvec)
    cvec[pl.ds(first_col, SHARE)] = jnp.broadcast_to(slope, (SHARE, 128))
    slope_row = cvec[...].T[0:1]
    arrive(high_u)
    copies_u = columns_row(cols_u)
    arrive(high_t)
    copies_t = columns_row(cols_t)
    passed_u = columns_core(cols_u, copies_u)
    passed = over_c(sar(partner), sar(partner))
    passed += pass_on(sar, zl, sar_x_copies)
    passed += pass_on(sar, 1 - zl, sar_x_relays)
    load_feats[1].wait()
    arrive(passed)
    passed_t = columns_core(cols_t, copies_t)
    every = slice(0, ROWS)
    embed(0, 0, every, rawbuf, 0)
    embed(1, 0, every, tanbuf, 0)
    unit, inverse = unit_of(rawbuf[every])
    turned, along = turn_of(tanbuf[every], unit, inverse)
    rows_u[...] = unit.astype(BF16)
    rows_t[...] = turned.astype(BF16)
    row_slope = inverse * along
    arrive(passed_u)

    def column_tile(cols, tile):
        return cols[tile // 2, (tile % 2) * 2 : (tile % 2) * 2 + 2].reshape(TILE, WIDTH)

    NT = ((1,), (1,))
    tiles = COLS // TILE
    for tile in range(tiles):
        span = slice(tile * TILE, (tile + 1) * TILE)
        piece = column_tile(cols_u, tile)
        scores[:, span] = LOGIT_SCALE * dot(rows_u[...], piece, NT)
        left_ts[:, span] = LOGIT_SCALE * dot(rows_t[...], piece, NT)
    row_max = jnp.max(scores[...], 1, keepdims=True)
    col_max = jnp.max(scores[...], 0, keepdims=True)
    arrive(passed_t)
    for tile in range(tiles):
        span = slice(tile * TILE, (tile + 1) * TILE)
        right_ts[:, span] = LOGIT_SCALE * dot(rows_u[...], column_tile(cols_t, tile), NT)

    row_sum = jnp.zeros((ROWS, 1), F32)
    row_weighted = jnp.zeros((ROWS, 1), F32)
    col_sum, col_weighted = [], []
    for tile in range(tiles):
        span = slice(tile * TILE, (tile + 1) * TILE)
        score = scores[:, span]
        tscore = left_ts[:, span] + right_ts[:, span]
        weight = jnp.exp(score - row_max)
        row_sum += jnp.sum(weight, 1, keepdims=True)
        row_weighted += jnp.sum(weight * tscore, 1, keepdims=True)
        weight = jnp.exp(score - col_max[:, span])
        col_sum.append(jnp.sum(weight, 0, keepdims=True))
        col_weighted.append(jnp.sum(weight * tscore, 0, keepdims=True))
    load_resid.wait()
    resid_norm = jnp.sum(resid[...] * resid[...])
    direc_norm = jnp.sum(direc[...] * direc[...])
    constant = lambda value: jnp.full((ROWS, 1), value, F32)
    row_slots[pl.ds(mp, 1)] = pack_lanes(
        [row_max, row_sum, row_weighted, constant(resid_norm), constant(direc_norm)]
    )[None]
    core_stat[pl.ds(c, 1)] = fold(
        [col_max, jnp.concatenate(col_sum, 1), jnp.concatenate(col_weighted, 1), slope_row]
    )[None]

    def join_columns(slots, count):
        parts = [unfold(slots[k], 4) for k in range(count)]
        top, total, weighted = softmax_join([(part[0:1], part[1:2], part[2:3]) for part in parts])
        slopes = functools.reduce(jnp.add, [part[3:4] for part in parts])
        return top, total, weighted, slopes

    def sum_slots(slots, count):
        return functools.reduce(jnp.add, [slots[k] for k in range(count)])

    def spread_c(slots):
        return over_c(slots.at[c], slots.at[c])

    def spread_y(slots):
        return over_y(lambda r: slots.at[y], lambda q: slots.at[y])

    def spread_h(slots):
        return over_h(lambda h: slots.at[zh], lambda q: slots.at[zh])

    def spread_m(slots):
        return over_m(lambda m: slots.at[mp], lambda q: slots.at[mp])

    copies = spread_c(core_stat)
    row_copies = spread_m(row_slots)
    arrive(copies)
    y_stat[pl.ds(y, 1)] = fold(join_columns(core_stat, NC))[None]
    copies = spread_y(y_stat)
    arrive(copies)
    z_stat[pl.ds(zh, 1)] = fold(join_columns(y_stat, NY))[None]
    copies = spread_h(z_stat)
    arrive(row_copies)
    parts = [row_slots[k] for k in range(NM)]
    top, total, weighted = softmax_join([(part[0:1], part[1:2], part[2:3]) for part in parts])
    norms = functools.reduce(jnp.add, [part[3:5] for part in parts])
    norm_old = norms[0:1, 0:1]
    norm_direc = norms[1:2, 0:1]
    row_info = unpack_lanes(jnp.concatenate([top + jnp.log(total), weighted / total], 0))
    row_lse, row_dot = row_info[:, 0:1], row_info[:, 1:2]
    arrive(copies)
    top, total, weighted, slopes = join_columns(z_stat, NH)
    col_lse, col_dot = top + jnp.log(total), weighted / total
    col_slope = unpack_lanes(slopes)

    row_ids = lax.broadcasted_iota(jnp.int32, (ROWS, TILE), 0)
    col_ids = lax.broadcasted_iota(jnp.int32, (ROWS, TILE), 1)
    offset = mp * SHARE - first_col
    row_along = jnp.zeros((ROWS, 1), F32)
    row_turned = jnp.zeros((ROWS, 1), F32)
    col_along, col_turned = [], []
    for tile in range(tiles):
        span = slice(tile * TILE, (tile + 1) * TILE)
        score = scores[:, span]
        left, right = left_ts[:, span], right_ts[:, span]
        tscore = left + right
        row_w = jnp.exp(score - row_lse)
        col_w = jnp.exp(score - col_lse[:, span])
        place = col_ids + tile * TILE
        mine = (place >= first_col) & (place < first_col + SHARE) & (row_ids == place + offset)
        low = ((row_w + col_w - 2.0 * mine.astype(F32)) / (2.0 * PAIRS)).astype(BF16)
        dsc[:, span] = low
        tdsc[:, span] = (
            (row_w * (tscore - row_dot) + col_w * (tscore - col_dot[:, span])) / (2.0 * PAIRS)
        ).astype(BF16)
        wide = low.astype(F32)
        row_along += jnp.sum(wide * score, 1, keepdims=True)
        row_turned += jnp.sum(wide * left, 1, keepdims=True)
        col_along.append(jnp.sum(wide * score, 0, keepdims=True))
        col_turned.append(jnp.sum(wide * right, 0, keepdims=True))
    grad_slots[pl.ds(mp, 1)] = pack_lanes([row_along, row_turned])[None]
    core_grad[pl.ds(c, 1)] = fold([jnp.concatenate(col_along, 1), jnp.concatenate(col_turned, 1)])[None]
    grad_copies = spread_m(grad_slots)
    core_copies = spread_c(core_grad)

    TN = ((0,), (0,))
    cvec[...] = col_slope

    def column_terms(tile, half):
        start = pl.multiple_of(tile * TILE, TILE)
        d_low, t_low = dsc[:, pl.ds(start, TILE)], tdsc[:, pl.ds(start, TILE)]
        span = slice(half * WIDE, (half + 1) * WIDE)
        total = dot(t_low, rows_u[:, span], TN) + dot(d_low, rows_t[:, span], TN)
        total -= cvec[pl.ds(start, TILE), 0:1] * dot(d_low, rows_u[:, span], TN)
        return LOGIT_SCALE * total

    half_tiles = HALF // TILE
    passed = []
    for half in range(2):
        for tile in range(half_tiles):
            terms = column_terms((1 - c) * half_tiles + tile, half)
            block = col_part.at[half, 0, tile]
            block[...] = terms.reshape(block.shape)
            passed += over_c(block, col_recv.at[half, tile])
    y_copies = []
    for half in range(2):
        for tile in range(half_tiles):
            terms = column_terms(c * half_tiles + tile, half).reshape(col_part.shape[3:])
            passed[half * half_tiles + tile].wait_recv()
            col_part[half, 1, tile] = terms + col_recv[half, tile]
        y_copies.append(
            over_y(lambda r: col_part.at[half, 1, r // 2, r % 2], lambda q: y_recv.at[half, q - 1])
        )
    arrive(core_copies)
    y_grad[pl.ds(y, 1)] = sum_slots(core_grad, NC)[None]
    y_grad_copies = spread_y(y_grad)

    for tile in range(WIDTH // TILE):
        span = slice(tile * TILE, (tile + 1) * TILE)
        u_piece = cols_u[:, :, :, :, span].reshape(COLS, TILE)
        t_piece = cols_t[:, :, :, :, span].reshape(COLS, TILE)
        total = dot(tdsc[...], u_piece) + dot(dsc[...], t_piece) - row_slope * dot(dsc[...], u_piece)
        row_part[:, :, :, span] = (LOGIT_SCALE * total).reshape(NL, NX, SHARE, TILE)
    x_copies = over_x(lambda k: row_part.at[:, k], lambda q: x_recv.at[q - 1])

    arrive(y_grad_copies)
    z_grad[pl.ds(zh, 1)] = sum_slots(y_grad, NY)[None]
    z_grad_copies = spread_h(z_grad)

    def column_high(half):
        arrive(y_copies[half])
        here = col_part[half, 1, y // 2, y % 2]
        col_part[half, 1, y // 2, y % 2] = here + y_recv[half, 0] + y_recv[half, 1] + y_recv[half, 2]
        return over_h(lambda h: col_part.at[half, 1, y // 2, y % 2, h], lambda q: z_recv.at[half, q - 1])

    high_first = column_high(0)
    arrive(x_copies)
    for low in range(NL):
        row_part[low, x] += x_recv[0, low] + x_recv[1, low] + x_recv[2, low]
    l_copies = over_l(row_part.at[1 - zl, x], l_recv)
    arrive(grad_copies)
    grad_rows[...] = unpack_lanes(sum_slots(grad_slots, NM))

    def finish(raw, tangent, value, info):
        unit, inverse = unit_of(raw)
        turned, _ = turn_of(tangent, unit, inverse)
        mixed = info[:, 1:2] + jnp.sum(unit * value, -1, keepdims=True)
        return ((value - turned * info[:, 0:1] - unit * mixed) * inverse).astype(BF16)

    def spread_tdz(tower):
        block = tdz.at[tower, mp]
        return over_m(lambda m: block, lambda q: block)

    high_second = column_high(1)
    arrive(z_grad_copies)
    grad_cols[...] = unpack_lanes(unfold(sum_slots(z_grad, NH), 2))
    arrive(l_copies)
    tdz[0, mp] = finish(rawbuf[own], tanbuf[own], row_part[zl, x] + l_recv[...], grad_rows[own])
    sar_copies = spread_tdz(0)
    arrive(high_first)
    arrive(high_second)
    halves = [
        col_part[half, 1, y // 2, y % 2, zh] + z_recv[half, 0] + z_recv[half, 1] + z_recv[half, 2]
        for half in range(2)
    ]
    tdz[1, mp] = finish(
        rawbuf[ROWS : ROWS + SHARE],
        tanbuf[ROWS : ROWS + SHARE],
        jnp.concatenate(halves, 1),
        grad_cols[pl.ds(first_col, SHARE)],
    )
    optical_copies = spread_tdz(1)

    curve = 0.0
    for tower, copies in enumerate((sar_copies, optical_copies)):
        arrive(copies)
        part = dot(feats[tower, :, pl.ds(pl.multiple_of(mp * PART, PART), PART)], tdz[tower].reshape(ROWS, WIDTH), TN)
        part_hess[tower] = part.reshape(part_hess.shape[1:])
        curve += jnp.sum(direc[tower] * part)
    passed = over_c(part_hess.at[1 - c], core_hess)
    scal_m[pl.ds(mp, 1)] = jnp.full((1, 8, 128), curve, F32)
    scal_copies = spread_m(scal_m)
    arrive(passed)
    part_hess[pl.ds(c, 1)] += core_hess[...][None]
    copies = over_y(lambda r: part_hess.at[c, r], lambda q: y_hess.at[q - 1])
    arrive(scal_copies)
    scal_p[pl.ds(c * NY + y, 1)] = sum_slots(scal_m, NM)[None]
    scal_copies = over_plane(scal_p)
    arrive(copies)
    z_hess[zh] = part_hess[c, y] + y_hess[0] + y_hess[1] + y_hess[2]
    copies = spread_h(z_hess)
    arrive(scal_copies)
    scal_z[pl.ds(zh, 1)] = sum_slots(scal_p, NC * NY)[None]
    scal_copies = spread_h(scal_z)
    arrive(copies)
    block_hess = sum_slots(z_hess, NH)
    hess[c, y] = block_hess
    block = hess.at[c, y]
    copies = over_y(lambda r: block, lambda q: block)
    arrive(scal_copies)
    curve = sum_slots(scal_z, NH)[0:1, 0:1] + DAMPING * norm_direc
    alpha = norm_old / curve
    piece = pl.ds(pl.multiple_of(y * BLOCK, BLOCK), BLOCK)
    after = resid[c, piece] - alpha * (block_hess + DAMPING * direc[c, piece])
    norm_p[pl.ds(c * NY + y, 1)] = jnp.full((1, 8, 128), jnp.sum(after * after), F32)
    scal_copies = over_plane(norm_p)
    passed = over_c(block, block)
    for q, copy in enumerate(copies, 1):
        copy.wait_recv()
        block = hess.at[c, (y + NY - q) % NY]
        passed += over_c(block, block)
    arrive(scal_copies)
    norm_m[pl.ds(mp, 1)] = sum_slots(norm_p, NC * NY)[None]
    scal_copies = spread_m(norm_m)
    arrive(passed)
    store = load(hess, hess_out, 7)
    arrive(scal_copies)
    norm_new = sum_slots(norm_m, NM)[0:1, 0:1]
    first_row = lax.broadcasted_iota(jnp.int32, (8, 128), 0) == 0
    info_out[...] = jnp.where(first_row, alpha, norm_new / norm_old)
    store.wait()
    for copy in pending:
        copy.wait_send()
    assert counter[0] <= SEMS


def last_kernel(info, hess, direc, resid, solu, out_sol, out_res, out_dir):
    alpha, beta = info[0:1, 0:1], info[1:2, 0:1]
    for tower in range(2):
        direction = direc[tower]
        out_sol[tower] = solu[tower] + alpha * direction
        after = resid[tower] - alpha * (hess[tower] + DAMPING * direction)
        out_res[tower] = after
        out_dir[tower] = after + beta * direction


def body(features, projections, solution, residual, direction):
    vmem = pl.BlockSpec(memory_space=pltpu.VMEM)
    hbm = pl.BlockSpec(memory_space=pl.ANY)
    f32 = lambda *size: pltpu.VMEM(size, F32)
    bf16 = lambda *size: pltpu.VMEM(size, BF16)
    scratch = [
        bf16(2, ROWS, DEPTH), f32(2, PART, WIDTH), f32(2, PART, WIDTH),
        bf16(2, 2, NM, PART, WIDTH), bf16(2, NY, NM - 1, QUARTER, WIDTH),
        f32(ROWS + SHARE, WIDTH), f32(ROWS + SHARE, WIDTH),
        bf16(ROWS, WIDTH), bf16(ROWS, WIDTH),
        bf16(NC, NY, NH, SHARE, WIDTH), bf16(NC, NY, NH, SHARE, WIDTH),
        f32(ROWS, COLS), f32(ROWS, COLS), f32(ROWS, COLS),
        bf16(ROWS, COLS), bf16(ROWS, COLS), f32(COLS, 128),
        f32(NM, 8, ROWS), f32(NC, 8, COLS // 2), f32(NY, 8, COLS // 2), f32(NH, 8, COLS // 2),
        f32(NM, 8, ROWS), f32(NC, 8, COLS // 4), f32(NY, 8, COLS // 4), f32(NH, 8, COLS // 4),
        f32(NL, NX, SHARE, WIDTH), f32(NX - 1, NL, SHARE, WIDTH), f32(SHARE, WIDTH),
        f32(2, 2, 2, 2, NH, SHARE, WIDE), f32(2, 2, 2, NH, SHARE, WIDE),
        f32(2, NY - 1, NH, SHARE, WIDE), f32(2, NH - 1, SHARE, WIDE),
        f32(COLS, 128), f32(ROWS, 128),
        bf16(2, NM, SHARE, WIDTH),
        f32(2, NY, BLOCK, WIDTH), f32(NY, BLOCK, WIDTH),
        f32(NY - 1, BLOCK, WIDTH), f32(NH, BLOCK, WIDTH), f32(2, NY, BLOCK, WIDTH),
        f32(NM, 8, 128), f32(NC * NY, 8, 128), f32(NH, 8, 128),
        f32(NC * NY, 8, 128), f32(NM, 8, 128),
        pltpu.SemaphoreType.DMA((SEMS,)), pltpu.SemaphoreType.DMA((SEMS,)), pltpu.SemaphoreType.DMA((8,)),
    ]
    hess, info = pl.pallas_call(
        kernel,
        name="cg_step",
        out_shape=(
            jax.ShapeDtypeStruct((2, NY, BLOCK, WIDTH), F32),
            jax.ShapeDtypeStruct((8, 128), F32),
        ),
        in_specs=[hbm] * 4,
        out_specs=(hbm, vmem),
        scratch_shapes=scratch,
        compiler_params=pltpu.CompilerParams(
            collective_id=0, has_side_effects=True, vmem_limit_bytes=60 * 2**20
        ),
    )(features, projections, direction, residual)
    whole = pl.BlockSpec((2, BLOCK, WIDTH), lambda step: (0, step, 0))
    shape = jax.ShapeDtypeStruct(direction.shape, F32)
    return pl.pallas_call(
        last_kernel,
        name="updates",
        grid=(NY,),
        out_shape=(shape, shape, shape),
        in_specs=[pl.BlockSpec((8, 128), lambda step: (0, 0))] + [whole] * 4,
        out_specs=(whole, whole, whole),
    )(info, hess.reshape(direction.shape), direction, residual, solution)


def solution(mesh):
    placed = (
        P(None, "dp", None),
        P(None, "mp", None),
        P(None, "mp", None),
        P(None, "mp", None),
        P(None, "mp", None),
    )
    return jax.shard_map(
        body,
        mesh=mesh,
        in_specs=placed,
        out_specs=(P(None, "mp", None), P(None, "mp", None), P(None, "mp", None)),
        check_vma=False,
    )
```

```python
import functools

import jax
import jax.numpy as jnp
from jax import lax
from jax.experimental import pallas as pl
from jax.experimental.pallas import tpu as pltpu
from jax.sharding import PartitionSpec as P

LOGIT_SCALE = 100.0
DAMPING = 1.0
EPSILON = 1e-06

NC, NY, NH, NX, NL = 2, 4, 4, 4, 2
NM = NX * NL
ROWS, DEPTH, WIDTH = 256, 1024, 768
PART = DEPTH // NM
SHARE = ROWS // NM
COLS = SHARE * NC * NY * NH
PAIRS = ROWS * NC * NY * NH
TILE = 256
SEMS = 224
QUARTER = 16
DIRECT = PART - NY * QUARTER
BLOCK = PART // NY
BLOCKS = SHARE * NY
HALF = BLOCK // 2
F32, BF16 = jnp.float32, jnp.bfloat16
MESH = pl.DeviceIdType.MESH


def dot(left, right, dims=((1,), (0,))):
    return lax.dot_general(left, right, (dims, ((), ())), preferred_element_type=F32)


def unit_of(raw):
    inverse = lax.rsqrt(jnp.sum(raw * raw, -1, keepdims=True) + EPSILON)
    return raw * inverse, inverse


def turn_of(tangent, unit, inverse):
    along = jnp.sum(unit * tangent, -1, keepdims=True)
    return (tangent - unit * along) * inverse, along


def pack_lanes(columns):
    size = columns[0].shape[0]
    lane = lax.broadcasted_iota(jnp.int32, (size, 128), 1)
    wide = jnp.zeros((size, 128), F32)
    for place, column in enumerate(columns):
        wide = jnp.where(lane == place, column, wide)
    return wide.T[0:8]


def unpack_lanes(rows):
    return jnp.concatenate([rows, jnp.zeros((128 - rows.shape[0], rows.shape[1]), F32)], 0).T


def fold(rows):
    size = rows[0].shape[1] * len(rows) // 8
    stacked = jnp.concatenate(rows, 0)
    return jnp.concatenate([stacked[:, k : k + size] for k in range(0, stacked.shape[1], size)], 0)


def unfold(block, count):
    return jnp.concatenate([block[k : k + count] for k in range(0, 8, count)], 1)


def softmax_join(slots):
    top = functools.reduce(jnp.maximum, [slot[0] for slot in slots])
    total = 0.0
    weighted = 0.0
    for slot in slots:
        factor = jnp.exp(slot[0] - top)
        total = total + factor * slot[1]
        weighted = weighted + factor * slot[2]
    return top, total, weighted


def kernel(
    feats_in, proj_in, direc_in, resid_in,
    hess_out, info_out,
    feats, direc, resid, weights, quarters, rawbuf, tanbuf, rows_u, rows_t, cols,
    scores, left_ts, right_ts, dsc, tdsc, cvec,
    row_slots, plane_stat, z_stat,
    grad_slots, plane_grad, z_grad,
    row_part, x_recv, l_recv, col_away, col_part, col_recv, y_recv, z_recv,
    grad_cols, grad_rows, tdz, part_hess, core_hess, y_hess, z_hess, hess,
    scal_m, scal_p, scal_z, norm_p, norm_m,
    send_sem, recv_sem, load_sem,
):
    dp, mp = lax.axis_index("dp"), lax.axis_index("mp")
    c, y, zh = dp % NC, (dp // NC) % NY, dp // (NC * NY)
    x, zl = mp % NX, mp // NX
    partner = (1 - zl) * NX + x
    counter = [0]

    def device(core=None, row=None, high=None, model=None):
        core, row, high = c if core is None else core, y if row is None else row, zh if high is None else high
        return {"dp": (high * NY + row) * NC + core, "mp": mp if model is None else model}

    def m_at(step):
        return ((zl + step // NX) % NL) * NX + (x + step % NX) % NX

    def m_from(step):
        return ((zl + step // NX) % NL) * NX + (x + NX - step % NX) % NX

    def x_at(step):
        return (x + step) % NX

    def y_at(step):
        return (y + step) % NY

    def h_at(step):
        return (zh + step) % NH

    def send(source, target, where):
        place = counter[0]
        counter[0] += 1
        copy = pltpu.make_async_remote_copy(
            src_ref=source, dst_ref=target, send_sem=send_sem.at[place], recv_sem=recv_sem.at[place],
            device_id=where, device_id_type=MESH,
        )
        copy.start()
        pending.append(copy)
        return copy

    pending = []

    def arrive(copies):
        for copy in copies:
            copy.wait_recv()

    def over_m(source, target):
        return [send(source(m_at(q)), target(q), device(model=m_at(q))) for q in range(1, NM)]

    def over_y(source, target):
        return [send(source(y_at(q)), target(q), device(row=y_at(q))) for q in range(1, NY)]

    def over_h(source, target):
        return [send(source(h_at(q)), target(q), device(high=h_at(q))) for q in range(1, NH)]

    def over_x(source, target):
        return [send(source(x_at(q)), target(q), device(model=zl * NX + x_at(q))) for q in range(1, NX)]

    def over_l(source, target):
        return [send(source, target, device(model=partner))]

    def over_plane(slots):
        place = slots.at[c * NY + y]
        return [
            send(place, place, device(core=(c + q // NY) % NC, row=(y + q % NY) % NY)) for q in range(1, NC * NY)
        ]

    def over_c(source, target):
        return [send(source, target, device(core=1 - c))]

    def load(source, target, place):
        copy = pltpu.make_async_copy(source, target, load_sem.at[place])
        copy.start()
        return copy

    load_direc = [load(direc_in.at[tower], direc.at[tower], tower) for tower in (1, 0)]
    load_proj = [load(proj_in.at[tower], weights.at[0, tower, mp], 2 + tower) for tower in (1, 0)]
    load_feats = [load(feats_in.at[tower], feats.at[tower], 4 + tower) for tower in (1, 0)]
    load_resid = load(resid_in, resid, 6)

    barrier = pltpu.get_barrier_semaphore()
    for q in range(1, NM):
        pl.semaphore_signal(barrier, inc=1, device_id=device(model=m_at(q)), device_id_type=MESH)
    for q in range(1, NC * NY):
        where = device(core=(c + q // NY) % NC, row=(y + q % NY) % NY)
        pl.semaphore_signal(barrier, inc=1, device_id=where, device_id_type=MESH)
    for q in range(1, NH):
        pl.semaphore_signal(barrier, inc=1, device_id=device(high=h_at(q)), device_id_type=MESH)
    load_direc[0].wait()
    weights[1, 1, pl.ds(mp, 1)] = direc[1].astype(BF16)[None]
    load_proj[0].wait()
    pl.semaphore_wait(barrier, NM + NC * NY + NH - 3)

    part = weights.at[c, 1, mp, pl.ds(pl.multiple_of(DIRECT + y * QUARTER, QUARTER), QUARTER)]
    quarter_copies = over_m(lambda m: part, lambda q: quarters.at[c, y, q - 1])
    def optical(m):
        return weights.at[c, 1, m, pl.ds(0, DIRECT)]

    def sar(m):
        return weights.at[c, 0, m]

    def spread_x(block):
        return over_x(lambda m: block, lambda q: block)

    def pass_on(blocks, low, copies):
        passed = []
        for q, copy in enumerate(copies, 1):
            copy.wait_recv()
            block = blocks(low * NX + (x + NX - q) % NX)
            passed += over_c(block, block)
        return passed

    l_copies = over_l(optical(mp), optical(mp))
    x_copies = spread_x(optical(mp))
    load_direc[1].wait()
    weights[1, 0, pl.ds(mp, 1)] = direc[0].astype(BF16)[None]
    load_proj[1].wait()
    sar_l_copies = over_l(sar(mp), sar(mp))
    arrive(quarter_copies)
    mine = quarters.at[c, y]
    row_copies = over_y(lambda r: mine, lambda q: mine)
    arrive(l_copies)
    x_relays = spread_x(optical(partner))
    passed = over_c(mine, mine) + over_c(optical(partner), optical(partner))
    passed += pass_on(optical, zl, x_copies)
    sar_x_copies = spread_x(sar(mp))
    passed += pass_on(optical, 1 - zl, x_relays)
    arrive(sar_l_copies)
    sar_x_relays = spread_x(sar(partner))
    for q, copy in enumerate(row_copies, 1):
        copy.wait_recv()
        block = quarters.at[c, (y + NY - q) % NY]
        passed += over_c(block, block)
    load_feats[0].wait()
    arrive(passed)
    for kind in range(2):
        for q in range(1, NM):
            for r in range(NY):
                weights[kind, 1, m_from(q), DIRECT + r * QUARTER : DIRECT + (r + 1) * QUARTER] = quarters[kind, r, q - 1]

    def embed(kind, tower, rows, into, first):
        for tile in range(WIDTH // TILE):
            span = slice(tile * TILE, (tile + 1) * TILE)
            total = 0.0
            for block in range(0, NM, 2):
                deep = slice(block * PART, (block + 2) * PART)
                piece = weights[kind, tower, block : block + 2, :, span].reshape(2 * PART, TILE)
                total += dot(feats[tower, rows, deep], piece)
            into[first : first + total.shape[0], span] = total

    own = pl.ds(pl.multiple_of(mp * SHARE, SHARE), SHARE)
    embed(0, 1, own, rawbuf, ROWS)
    embed(1, 1, own, tanbuf, ROWS)
    unit, inverse = unit_of(rawbuf[ROWS : ROWS + SHARE])
    turned, along = turn_of(tanbuf[ROWS : ROWS + SHARE], unit, inverse)
    cols[c, zh, y, 0] = unit.astype(BF16)
    cols[c, zh, y, 1] = turned.astype(BF16)
    slope = inverse * along

    def column_block(high, row):
        return cols.at[c, high, row]

    def column_rows(high):
        block = column_block(high, y)
        return over_c(block, block), over_y(lambda r: block, lambda q: block)

    def column_pass(high, copies):
        passed = []
        for q, copy in enumerate(copies, 1):
            copy.wait_recv()
            block = column_block(high, (y + NY - q) % NY)
            passed += over_c(block, block)
        return passed

    mine = column_block(zh, y)
    high_copies = over_h(lambda h: mine, lambda q: mine)
    col_passed, copies = column_rows(zh)
    waiting = [(zh, copies)]
    first_col = pl.multiple_of(((c * NH + zh) * NY + y) * SHARE, SHARE)
    cvec[...] = jnp.zeros_like(cvec)
    cvec[pl.ds(first_col, SHARE)] = jnp.broadcast_to(slope, (SHARE, 128))
    slope_row = cvec[...].T[0:1]
    for q in (1, 3, 2):
        high_copies[q - 1].wait_recv()
        high = (zh + NH - q) % NH
        passed, copies = column_rows(high)
        col_passed += passed
        waiting.append((high, copies))
    col_passed += column_pass(*waiting[0])
    passed = over_c(sar(partner), sar(partner))
    passed += pass_on(sar, zl, sar_x_copies)
    col_passed += column_pass(*waiting[1])
    passed += pass_on(sar, 1 - zl, sar_x_relays)
    load_feats[1].wait()
    arrive(passed)
    col_passed += column_pass(*waiting[2])
    every = slice(0, ROWS)
    embed(0, 0, every, rawbuf, 0)
    embed(1, 0, every, tanbuf, 0)
    unit, inverse = unit_of(rawbuf[every])
    turned, along = turn_of(tanbuf[every], unit, inverse)
    rows_u[...] = unit.astype(BF16)
    rows_t[...] = turned.astype(BF16)
    row_slope = inverse * along
    col_passed += column_pass(*waiting[3])
    arrive(col_passed)

    def column_tile(kind, tile):
        return cols[tile // 2, (tile % 2) * 2 : (tile % 2) * 2 + 2, :, kind].reshape(TILE, WIDTH)

    NT = ((1,), (1,))
    tiles = COLS // TILE
    for tile in range(tiles):
        span = slice(tile * TILE, (tile + 1) * TILE)
        piece = column_tile(0, tile)
        scores[:, span] = LOGIT_SCALE * dot(rows_u[...], piece, NT)
        left_ts[:, span] = LOGIT_SCALE * dot(rows_t[...], piece, NT)
    row_max = jnp.max(scores[...], 1, keepdims=True)
    col_max = jnp.max(scores[...], 0, keepdims=True)
    for tile in range(tiles):
        span = slice(tile * TILE, (tile + 1) * TILE)
        right_ts[:, span] = LOGIT_SCALE * dot(rows_u[...], column_tile(1, tile), NT)

    row_sum = jnp.zeros((ROWS, 1), F32)
    row_weighted = jnp.zeros((ROWS, 1), F32)
    col_sum, col_weighted = [], []
    for tile in range(tiles):
        span = slice(tile * TILE, (tile + 1) * TILE)
        score = scores[:, span]
        tscore = left_ts[:, span] + right_ts[:, span]
        weight = jnp.exp(score - row_max)
        row_sum += jnp.sum(weight, 1, keepdims=True)
        row_weighted += jnp.sum(weight * tscore, 1, keepdims=True)
        weight = jnp.exp(score - col_max[:, span])
        col_sum.append(jnp.sum(weight, 0, keepdims=True))
        col_weighted.append(jnp.sum(weight * tscore, 0, keepdims=True))
    load_resid.wait()
    resid_norm = jnp.sum(resid[...] * resid[...])
    direc_norm = jnp.sum(direc[...] * direc[...])
    constant = lambda value: jnp.full((ROWS, 1), value, F32)
    row_slots[pl.ds(mp, 1)] = pack_lanes(
        [row_max, row_sum, row_weighted, constant(resid_norm), constant(direc_norm)]
    )[None]
    plane_stat[pl.ds(c * NY + y, 1)] = fold(
        [col_max, jnp.concatenate(col_sum, 1), jnp.concatenate(col_weighted, 1), slope_row]
    )[None]

    def join_columns(slots, count):
        parts = [unfold(slots[k], 4) for k in range(count)]
        top, total, weighted = softmax_join([(part[0:1], part[1:2], part[2:3]) for part in parts])
        slopes = functools.reduce(jnp.add, [part[3:4] for part in parts])
        return top, total, weighted, slopes

    def sum_slots(slots, count):
        return functools.reduce(jnp.add, [slots[k] for k in range(count)])

    def spread_h(slots):
        return over_h(lambda h: slots.at[zh], lambda q: slots.at[zh])

    def spread_m(slots):
        return over_m(lambda m: slots.at[mp], lambda q: slots.at[mp])

    copies = over_plane(plane_stat)
    row_copies = spread_m(row_slots)
    arrive(copies)
    z_stat[pl.ds(zh, 1)] = fold(join_columns(plane_stat, NC * NY))[None]
    copies = spread_h(z_stat)
    arrive(row_copies)
    parts = [row_slots[k] for k in range(NM)]
    top, total, weighted = softmax_join([(part[0:1], part[1:2], part[2:3]) for part in parts])
    norms = functools.reduce(jnp.add, [part[3:5] for part in parts])
    norm_old = norms[0:1, 0:1]
    norm_direc = norms[1:2, 0:1]
    row_info = unpack_lanes(jnp.concatenate([top + jnp.log(total), weighted / total], 0))
    row_lse, row_dot = row_info[:, 0:1], row_info[:, 1:2]
    arrive(copies)
    top, total, weighted, slopes = join_columns(z_stat, NH)
    col_lse, col_dot = top + jnp.log(total), weighted / total
    col_slope = unpack_lanes(slopes)

    row_ids = lax.broadcasted_iota(jnp.int32, (ROWS, TILE), 0)
    col_ids = lax.broadcasted_iota(jnp.int32, (ROWS, TILE), 1)
    offset = mp * SHARE - first_col
    row_along = jnp.zeros((ROWS, 1), F32)
    row_turned = jnp.zeros((ROWS, 1), F32)
    col_along, col_turned = [], []
    for tile in range(tiles):
        span = slice(tile * TILE, (tile + 1) * TILE)
        score = scores[:, span]
        left, right = left_ts[:, span], right_ts[:, span]
        tscore = left + right
        row_w = jnp.exp(score - row_lse)
        col_w = jnp.exp(score - col_lse[:, span])
        place = col_ids + tile * TILE
        mine = (place >= first_col) & (place < first_col + SHARE) & (row_ids == place + offset)
        low = ((row_w + col_w - 2.0 * mine.astype(F32)) / (2.0 * PAIRS)).astype(BF16)
        dsc[:, span] = low
        tdsc[:, span] = (
            (row_w * (tscore - row_dot) + col_w * (tscore - col_dot[:, span])) / (2.0 * PAIRS)
        ).astype(BF16)
        wide = low.astype(F32)
        row_along += jnp.sum(wide * score, 1, keepdims=True)
        row_turned += jnp.sum(wide * left, 1, keepdims=True)
        col_along.append(jnp.sum(wide * score, 0, keepdims=True))
        col_turned.append(jnp.sum(wide * right, 0, keepdims=True))
    grad_slots[pl.ds(mp, 1)] = pack_lanes([row_along, row_turned])[None]
    plane_grad[pl.ds(c * NY + y, 1)] = fold([jnp.concatenate(col_along, 1), jnp.concatenate(col_turned, 1)])[None]
    grad_copies = spread_m(grad_slots)
    plane_copies = over_plane(plane_grad)

    TN = ((0,), (0,))
    cvec[...] = col_slope

    def column_terms(core, high):
        start = pl.multiple_of((core * NH + high) * BLOCKS, BLOCKS)
        d_low, t_low = dsc[:, pl.ds(start, BLOCKS)], tdsc[:, pl.ds(start, BLOCKS)]
        total = dot(t_low, rows_u[...], TN) + dot(d_low, rows_t[...], TN)
        total -= cvec[pl.ds(start, BLOCKS), 0:1] * dot(d_low, rows_u[...], TN)
        return (LOGIT_SCALE * total).reshape(NY, SHARE, WIDTH)

    steps = (2, 1, 3, 0)
    passed = []
    for place, step in enumerate(steps):
        col_away[place] = column_terms(1 - c, h_at(step))
        passed += over_c(col_away.at[place], col_recv.at[place])
    y_copies = []
    for place, step in enumerate(steps):
        terms = column_terms(c, h_at(step))
        passed[place].wait_recv()
        col_part[place] = terms + col_recv[place]
        y_copies.append(over_y(lambda r: col_part.at[place, r], lambda q: y_recv.at[place, q - 1]))

    for tile in range(WIDTH // TILE):
        span = slice(tile * TILE, (tile + 1) * TILE)
        u_piece = cols[:, :, :, 0, :, span].reshape(COLS, TILE)
        t_piece = cols[:, :, :, 1, :, span].reshape(COLS, TILE)
        total = dot(tdsc[...], u_piece) + dot(dsc[...], t_piece) - row_slope * dot(dsc[...], u_piece)
        row_part[:, :, :, span] = (LOGIT_SCALE * total).reshape(NL, NX, SHARE, TILE)
    x_copies = over_x(lambda k: row_part.at[:, k], lambda q: x_recv.at[q - 1])

    arrive(plane_copies)
    z_grad[pl.ds(zh, 1)] = sum_slots(plane_grad, NC * NY)[None]
    z_grad_copies = spread_h(z_grad)

    def column_sum(place):
        arrive(y_copies[place])
        return col_part[place, y] + y_recv[place, 0] + y_recv[place, 1] + y_recv[place, 2]

    def column_high(place):
        step = steps[place]
        col_part[place, y] = column_sum(place)
        return [send(col_part.at[place, y], z_recv.at[step - 1], device(high=h_at(step)))]

    high_copies = column_high(0)
    high_copies += column_high(1)
    arrive(x_copies)
    for low in range(NL):
        row_part[low, x] += x_recv[0, low] + x_recv[1, low] + x_recv[2, low]
    l_copies = over_l(row_part.at[1 - zl, x], l_recv)
    arrive(grad_copies)
    grad_rows[...] = unpack_lanes(sum_slots(grad_slots, NM))

    def finish(raw, tangent, value, info):
        unit, inverse = unit_of(raw)
        turned, _ = turn_of(tangent, unit, inverse)
        mixed = info[:, 1:2] + jnp.sum(unit * value, -1, keepdims=True)
        return ((value - turned * info[:, 0:1] - unit * mixed) * inverse).astype(BF16)

    def spread_tdz(tower):
        block = tdz.at[tower, mp]
        return over_m(lambda m: block, lambda q: block)

    high_copies += column_high(2)
    arrive(z_grad_copies)
    grad_cols[...] = unpack_lanes(unfold(sum_slots(z_grad, NH), 2))
    arrive(l_copies)
    tdz[0, mp] = finish(rawbuf[own], tanbuf[own], row_part[zl, x] + l_recv[...], grad_rows[own])
    sar_copies = spread_tdz(0)
    own_sum = column_sum(3)
    arrive(high_copies)
    tdz[1, mp] = finish(
        rawbuf[ROWS : ROWS + SHARE],
        tanbuf[ROWS : ROWS + SHARE],
        own_sum + z_recv[0] + z_recv[1] + z_recv[2],
        grad_cols[pl.ds(first_col, SHARE)],
    )
    optical_copies = spread_tdz(1)

    curve = 0.0
    for tower, copies in enumerate((sar_copies, optical_copies)):
        arrive(copies)
        part = dot(feats[tower, :, pl.ds(pl.multiple_of(mp * PART, PART), PART)], tdz[tower].reshape(ROWS, WIDTH), TN)
        part_hess[tower] = part.reshape(part_hess.shape[1:])
        curve += jnp.sum(direc[tower] * part)
    passed = over_c(part_hess.at[1 - c], core_hess)
    scal_m[pl.ds(mp, 1)] = jnp.full((1, 8, 128), curve, F32)
    scal_copies = spread_m(scal_m)
    arrive(passed)
    part_hess[pl.ds(c, 1)] += core_hess[...][None]
    row_copies = [
        over_y(lambda r: part_hess.at[c, r, half], lambda q: y_hess.at[half, q - 1]) for half in range(2)
    ]
    arrive(scal_copies)
    scal_p[pl.ds(c * NY + y, 1)] = sum_slots(scal_m, NM)[None]
    scal_copies = over_plane(scal_p)
    high_copies = []
    for half in range(2):
        arrive(row_copies[half])
        z_hess[half, zh] = part_hess[c, y, half] + y_hess[half, 0] + y_hess[half, 1] + y_hess[half, 2]
        block = z_hess.at[half, zh]
        high_copies.append(over_h(lambda h: block, lambda q: block))
    arrive(scal_copies)
    scal_z[pl.ds(zh, 1)] = sum_slots(scal_p, NC * NY)[None]
    scal_copies = spread_h(scal_z)

    def hess_rows(half):
        block = hess.at[c, y, half]
        return over_y(lambda r: block, lambda q: block)

    def hess_sum(half):
        arrive(high_copies[half])
        hess[c, y, half] = functools.reduce(jnp.add, [z_hess[half, k] for k in range(NH)])

    hess_sum(0)
    row_copies = [hess_rows(0)]
    arrive(scal_copies)
    curve = sum_slots(scal_z, NH)[0:1, 0:1] + DAMPING * norm_direc
    alpha = norm_old / curve
    hess_sum(1)
    piece = pl.ds(pl.multiple_of(y * BLOCK, BLOCK), BLOCK)
    after = resid[c, piece] - alpha * (hess[c, y].reshape(BLOCK, WIDTH) + DAMPING * direc[c, piece])
    norm_p[pl.ds(c * NY + y, 1)] = jnp.full((1, 8, 128), jnp.sum(after * after), F32)
    scal_copies = over_plane(norm_p)
    row_copies.append(hess_rows(1))
    passed = over_c(hess.at[c, y], hess.at[c, y])
    for half in range(2):
        for q, copy in enumerate(row_copies[half], 1):
            copy.wait_recv()
            block = hess.at[c, (y + NY - q) % NY, half]
            passed += over_c(block, block)
        if half == 0:
            arrive(scal_copies)
            norm_m[pl.ds(mp, 1)] = sum_slots(norm_p, NC * NY)[None]
            scal_copies = spread_m(norm_m)
    arrive(passed)
    store = load(hess, hess_out, 7)
    arrive(scal_copies)
    norm_new = sum_slots(norm_m, NM)[0:1, 0:1]
    first_row = lax.broadcasted_iota(jnp.int32, (8, 128), 0) == 0
    info_out[...] = jnp.where(first_row, alpha, norm_new / norm_old)
    store.wait()
    for copy in pending:
        copy.wait_send()
    assert counter[0] <= SEMS


def last_kernel(info, hess, direc, resid, solu, out_sol, out_res, out_dir):
    alpha, beta = info[0:1, 0:1], info[1:2, 0:1]
    for tower in range(2):
        direction = direc[tower]
        out_sol[tower] = solu[tower] + alpha * direction
        after = resid[tower] - alpha * (hess[tower] + DAMPING * direction)
        out_res[tower] = after
        out_dir[tower] = after + beta * direction


def body(features, projections, solution, residual, direction):
    vmem = pl.BlockSpec(memory_space=pltpu.VMEM)
    hbm = pl.BlockSpec(memory_space=pl.ANY)
    f32 = lambda *size: pltpu.VMEM(size, F32)
    bf16 = lambda *size: pltpu.VMEM(size, BF16)
    scratch = [
        bf16(2, ROWS, DEPTH), f32(2, PART, WIDTH), f32(2, PART, WIDTH),
        bf16(2, 2, NM, PART, WIDTH), bf16(2, NY, NM - 1, QUARTER, WIDTH),
        f32(ROWS + SHARE, WIDTH), f32(ROWS + SHARE, WIDTH),
        bf16(ROWS, WIDTH), bf16(ROWS, WIDTH),
        bf16(NC, NH, NY, 2, SHARE, WIDTH),
        f32(ROWS, COLS), f32(ROWS, COLS), f32(ROWS, COLS),
        bf16(ROWS, COLS), bf16(ROWS, COLS), f32(COLS, 128),
        f32(NM, 8, ROWS), f32(NC * NY, 8, COLS // 2), f32(NH, 8, COLS // 2),
        f32(NM, 8, ROWS), f32(NC * NY, 8, COLS // 4), f32(NH, 8, COLS // 4),
        f32(NL, NX, SHARE, WIDTH), f32(NX - 1, NL, SHARE, WIDTH), f32(SHARE, WIDTH),
        f32(NH, NY, SHARE, WIDTH), f32(NH, NY, SHARE, WIDTH), f32(NH, NY, SHARE, WIDTH),
        f32(NH, NY - 1, SHARE, WIDTH), f32(NH - 1, SHARE, WIDTH),
        f32(COLS, 128), f32(ROWS, 128),
        bf16(2, NM, SHARE, WIDTH),
        f32(2, NY, 2, HALF, WIDTH), f32(NY, 2, HALF, WIDTH),
        f32(2, NY - 1, HALF, WIDTH), f32(2, NH, HALF, WIDTH), f32(2, NY, 2, HALF, WIDTH),
        f32(NM, 8, 128), f32(NC * NY, 8, 128), f32(NH, 8, 128),
        f32(NC * NY, 8, 128), f32(NM, 8, 128),
        pltpu.SemaphoreType.DMA((SEMS,)), pltpu.SemaphoreType.DMA((SEMS,)), pltpu.SemaphoreType.DMA((8,)),
    ]
    hess, info = pl.pallas_call(
        kernel,
        name="cg_step",
        out_shape=(
            jax.ShapeDtypeStruct((2, NY, 2, HALF, WIDTH), F32),
            jax.ShapeDtypeStruct((8, 128), F32),
        ),
        in_specs=[hbm] * 4,
        out_specs=(hbm, vmem),
        scratch_shapes=scratch,
        compiler_params=pltpu.CompilerParams(
            collective_id=0, has_side_effects=True, vmem_limit_bytes=60 * 2**20
        ),
    )(features, projections, direction, residual)
    whole = pl.BlockSpec((2, BLOCK, WIDTH), lambda step: (0, step, 0))
    shape = jax.ShapeDtypeStruct(direction.shape, F32)
    return pl.pallas_call(
        last_kernel,
        name="updates",
        grid=(NY,),
        out_shape=(shape, shape, shape),
        in_specs=[pl.BlockSpec((8, 128), lambda step: (0, 0))] + [whole] * 4,
        out_specs=(whole, whole, whole),
    )(info, hess.reshape(direction.shape), direction, residual, solution)


def solution(mesh):
    placed = (
        P(None, "dp", None),
        P(None, "mp", None),
        P(None, "mp", None),
        P(None, "mp", None),
        P(None, "mp", None),
    )
    return jax.shard_map(
        body,
        mesh=mesh,
        in_specs=placed,
        out_specs=(P(None, "mp", None), P(None, "mp", None), P(None, "mp", None)),
        check_vma=False,
    )
```

```python
import functools

import jax
import jax.numpy as jnp
from jax import lax
from jax.experimental import pallas as pl
from jax.experimental.pallas import tpu as pltpu
from jax.sharding import PartitionSpec as P

LOGIT_SCALE = 100.0
DAMPING = 1.0
EPSILON = 1e-06

NC, NY, NH, NX, NL = 2, 4, 4, 4, 2
NM = NX * NL
ROWS, DEPTH, WIDTH = 256, 1024, 768
PART = DEPTH // NM
SHARE = ROWS // NM
COLS = SHARE * NC * NY * NH
PAIRS = ROWS * NC * NY * NH
TILE = 256
SEMS = 224
QUARTER = 16
DIRECT = PART - NY * QUARTER
BLOCK = PART // NY
BLOCKS = SHARE * NY
HALF = BLOCK // 2
F32, BF16 = jnp.float32, jnp.bfloat16
MESH = pl.DeviceIdType.MESH


def dot(left, right, dims=((1,), (0,))):
    return lax.dot_general(left, right, (dims, ((), ())), preferred_element_type=F32)


def unit_of(raw):
    inverse = lax.rsqrt(jnp.sum(raw * raw, -1, keepdims=True) + EPSILON)
    return raw * inverse, inverse


def turn_of(tangent, unit, inverse):
    along = jnp.sum(unit * tangent, -1, keepdims=True)
    return (tangent - unit * along) * inverse, along


def pack_lanes(columns):
    size = columns[0].shape[0]
    lane = lax.broadcasted_iota(jnp.int32, (size, 128), 1)
    wide = jnp.zeros((size, 128), F32)
    for place, column in enumerate(columns):
        wide = jnp.where(lane == place, column, wide)
    return wide.T[0:8]


def unpack_lanes(rows):
    return jnp.concatenate([rows, jnp.zeros((128 - rows.shape[0], rows.shape[1]), F32)], 0).T


def fold(rows):
    size = rows[0].shape[1] * len(rows) // 8
    stacked = jnp.concatenate(rows, 0)
    return jnp.concatenate([stacked[:, k : k + size] for k in range(0, stacked.shape[1], size)], 0)


def unfold(block, count):
    return jnp.concatenate([block[k : k + count] for k in range(0, 8, count)], 1)


def softmax_join(slots):
    top = functools.reduce(jnp.maximum, [slot[0] for slot in slots])
    total = 0.0
    weighted = 0.0
    for slot in slots:
        factor = jnp.exp(slot[0] - top)
        total = total + factor * slot[1]
        weighted = weighted + factor * slot[2]
    return top, total, weighted


def kernel(
    feats_in, proj_in, direc_in, resid_in,
    hess_out, info_out,
    feats, direc, resid, weights, quarters, rawbuf, tanbuf, rows_u, rows_t, cols,
    scores, left_ts, right_ts, dsc, tdsc, cvec,
    row_slots, plane_stat, z_stat,
    grad_slots, plane_grad, z_grad,
    row_part, x_recv, l_recv, col_away, col_part, col_low, col_recv, y_recv, z_recv,
    grad_cols, grad_rows, tdz, part_hess, core_hess, y_hess, z_hess, hess,
    scal_m, scal_p, scal_z, norm_p, norm_m,
    send_sem, recv_sem, load_sem,
):
    dp, mp = lax.axis_index("dp"), lax.axis_index("mp")
    c, y, zh = dp % NC, (dp // NC) % NY, dp // (NC * NY)
    x, zl = mp % NX, mp // NX
    partner = (1 - zl) * NX + x
    counter = [0]

    def device(core=None, row=None, high=None, model=None):
        core, row, high = c if core is None else core, y if row is None else row, zh if high is None else high
        return {"dp": (high * NY + row) * NC + core, "mp": mp if model is None else model}

    def m_at(step):
        return ((zl + step // NX) % NL) * NX + (x + step % NX) % NX

    def m_from(step):
        return ((zl + step // NX) % NL) * NX + (x + NX - step % NX) % NX

    def x_at(step):
        return (x + step) % NX

    def y_at(step):
        return (y + step) % NY

    def h_at(step):
        return (zh + step) % NH

    def send(source, target, where):
        place = counter[0]
        counter[0] += 1
        copy = pltpu.make_async_remote_copy(
            src_ref=source, dst_ref=target, send_sem=send_sem.at[place], recv_sem=recv_sem.at[place],
            device_id=where, device_id_type=MESH,
        )
        copy.start()
        pending.append(copy)
        return copy

    pending = []

    def arrive(copies):
        for copy in copies:
            copy.wait_recv()

    def over_m(source, target):
        return [send(source(m_at(q)), target(q), device(model=m_at(q))) for q in range(1, NM)]

    def over_y(source, target):
        return [send(source(y_at(q)), target(q), device(row=y_at(q))) for q in range(1, NY)]

    def over_h(source, target):
        return [send(source(h_at(q)), target(q), device(high=h_at(q))) for q in range(1, NH)]

    def over_x(source, target):
        return [send(source(x_at(q)), target(q), device(model=zl * NX + x_at(q))) for q in range(1, NX)]

    def over_l(source, target):
        return [send(source, target, device(model=partner))]

    def over_plane(slots):
        place = slots.at[c * NY + y]
        return [
            send(place, place, device(core=(c + q // NY) % NC, row=(y + q % NY) % NY)) for q in range(1, NC * NY)
        ]

    def over_c(source, target):
        return [send(source, target, device(core=1 - c))]

    def load(source, target, place):
        copy = pltpu.make_async_copy(source, target, load_sem.at[place])
        copy.start()
        return copy

    barrier = pltpu.get_barrier_semaphore()
    for q in (2, 1, 3):
        pl.semaphore_signal(barrier, inc=1, device_id=device(high=h_at(q)), device_id_type=MESH)
    for q in range(1, NM):
        pl.semaphore_signal(barrier, inc=1, device_id=device(model=m_at(q)), device_id_type=MESH)
    for q in range(1, NC * NY):
        where = device(core=(c + q // NY) % NC, row=(y + q % NY) % NY)
        pl.semaphore_signal(barrier, inc=1, device_id=where, device_id_type=MESH)
    load_direc = [load(direc_in.at[tower], direc.at[tower], tower) for tower in (1, 0)]
    load_proj = [load(proj_in.at[tower], weights.at[0, tower, mp], 2 + tower) for tower in (1, 0)]
    load_feats = [load(feats_in.at[tower], feats.at[tower], 4 + tower) for tower in (1, 0)]
    load_resid = load(resid_in, resid, 6)
    load_direc[0].wait()
    weights[1, 1, pl.ds(mp, 1)] = direc[1].astype(BF16)[None]
    load_proj[0].wait()
    pl.semaphore_wait(barrier, NM + NC * NY + NH - 3)

    part = weights.at[c, 1, mp, pl.ds(pl.multiple_of(DIRECT + y * QUARTER, QUARTER), QUARTER)]
    quarter_copies = over_m(lambda m: part, lambda q: quarters.at[c, y, q - 1])
    def optical(m):
        return weights.at[c, 1, m, pl.ds(0, DIRECT)]

    def sar(m):
        return weights.at[c, 0, m]

    def spread_x(block):
        return over_x(lambda m: block, lambda q: block)

    def pass_on(blocks, low, copies):
        passed = []
        for q, copy in enumerate(copies, 1):
            copy.wait_recv()
            block = blocks(low * NX + (x + NX - q) % NX)
            passed += over_c(block, block)
        return passed

    l_copies = over_l(optical(mp), optical(mp))
    x_copies = spread_x(optical(mp))
    load_direc[1].wait()
    weights[1, 0, pl.ds(mp, 1)] = direc[0].astype(BF16)[None]
    load_proj[1].wait()
    sar_l_copies = over_l(sar(mp), sar(mp))
    arrive(quarter_copies)
    mine = quarters.at[c, y]
    row_copies = over_y(lambda r: mine, lambda q: mine)
    arrive(l_copies)
    x_relays = spread_x(optical(partner))
    passed = over_c(mine, mine) + over_c(optical(partner), optical(partner))
    passed += pass_on(optical, zl, x_copies)
    sar_x_copies = spread_x(sar(mp))
    passed += pass_on(optical, 1 - zl, x_relays)
    arrive(sar_l_copies)
    sar_x_relays = spread_x(sar(partner))
    for q, copy in enumerate(row_copies, 1):
        copy.wait_recv()
        block = quarters.at[c, (y + NY - q) % NY]
        passed += over_c(block, block)
    load_feats[0].wait()
    arrive(passed)
    for kind in range(2):
        for q in range(1, NM):
            for r in range(NY):
                weights[kind, 1, m_from(q), DIRECT + r * QUARTER : DIRECT + (r + 1) * QUARTER] = quarters[kind, r, q - 1]

    def embed(kind, tower, rows, into, first):
        for tile in range(WIDTH // TILE):
            span = slice(tile * TILE, (tile + 1) * TILE)
            total = 0.0
            for block in range(0, NM, 2):
                deep = slice(block * PART, (block + 2) * PART)
                piece = weights[kind, tower, block : block + 2, :, span].reshape(2 * PART, TILE)
                total += dot(feats[tower, rows, deep], piece)
            into[first : first + total.shape[0], span] = total

    own = pl.ds(pl.multiple_of(mp * SHARE, SHARE), SHARE)
    embed(0, 1, own, rawbuf, ROWS)
    embed(1, 1, own, tanbuf, ROWS)
    unit, inverse = unit_of(rawbuf[ROWS : ROWS + SHARE])
    turned, along = turn_of(tanbuf[ROWS : ROWS + SHARE], unit, inverse)
    cols[c, zh, y, 0] = unit.astype(BF16)
    cols[c, zh, y, 1] = turned.astype(BF16)
    slope = inverse * along

    def column_block(high, row):
        return cols.at[c, high, row]

    def column_rows(high):
        block = column_block(high, y)
        return over_c(block, block), over_y(lambda r: block, lambda q: block)

    def column_pass(high, copies):
        passed = []
        for q, copy in enumerate(copies, 1):
            copy.wait_recv()
            block = column_block(high, (y + NY - q) % NY)
            passed += over_c(block, block)
        return passed

    mine = column_block(zh, y)
    high_copies = over_h(lambda h: mine, lambda q: mine)
    passed, copies = column_rows(zh)
    col_passed = [passed]
    waiting = [(zh, copies)]
    first_col = pl.multiple_of(((c * NH + zh) * NY + y) * SHARE, SHARE)
    cvec[...] = jnp.zeros_like(cvec)
    cvec[pl.ds(first_col, SHARE)] = jnp.broadcast_to(slope, (SHARE, 128))
    slope_row = cvec[...].T[0:1]
    for q in (1, 3, 2):
        high_copies[q - 1].wait_recv()
        high = (zh + NH - q) % NH
        passed, copies = column_rows(high)
        col_passed.append(passed)
        waiting.append((high, copies))
    col_passed[0] += column_pass(*waiting[0])
    passed = over_c(sar(partner), sar(partner))
    passed += pass_on(sar, zl, sar_x_copies)
    col_passed[1] += column_pass(*waiting[1])
    passed += pass_on(sar, 1 - zl, sar_x_relays)
    load_feats[1].wait()
    arrive(passed)
    col_passed[2] += column_pass(*waiting[2])
    every = slice(0, ROWS)
    embed(0, 0, every, rawbuf, 0)
    embed(1, 0, every, tanbuf, 0)
    unit, inverse = unit_of(rawbuf[every])
    turned, along = turn_of(tanbuf[every], unit, inverse)
    rows_u[...] = unit.astype(BF16)
    rows_t[...] = turned.astype(BF16)
    row_slope = inverse * along
    NT = ((1,), (1,))
    tiles = COLS // TILE
    for place, (high, copies) in enumerate(waiting):
        if place == NH - 1:
            col_passed[place] += column_pass(high, copies)
        arrive(col_passed[place])
        piece = [cols[:, high, :, kind].reshape(NC * BLOCKS, WIDTH) for kind in range(2)]
        for target, rows, kind in ((scores, rows_u, 0), (left_ts, rows_t, 0), (right_ts, rows_u, 1)):
            product = LOGIT_SCALE * dot(rows[...], piece[kind], NT)
            for core in range(NC):
                start = pl.multiple_of((core * NH + high) * BLOCKS, BLOCKS)
                target[:, pl.ds(start, BLOCKS)] = product[:, core * BLOCKS : (core + 1) * BLOCKS]
    row_max = jnp.max(scores[...], 1, keepdims=True)
    col_max = jnp.max(scores[...], 0, keepdims=True)
    row_sum = jnp.zeros((ROWS, 1), F32)
    row_weighted = jnp.zeros((ROWS, 1), F32)
    col_sum, col_weighted = [], []
    for tile in range(tiles):
        span = slice(tile * TILE, (tile + 1) * TILE)
        score = scores[:, span]
        tscore = left_ts[:, span] + right_ts[:, span]
        weight = jnp.exp(score - row_max)
        row_sum += jnp.sum(weight, 1, keepdims=True)
        row_weighted += jnp.sum(weight * tscore, 1, keepdims=True)
        weight = jnp.exp(score - col_max[:, span])
        col_sum.append(jnp.sum(weight, 0, keepdims=True))
        col_weighted.append(jnp.sum(weight * tscore, 0, keepdims=True))
    load_resid.wait()
    resid_norm = jnp.sum(resid[...] * resid[...])
    direc_norm = jnp.sum(direc[...] * direc[...])
    constant = lambda value: jnp.full((ROWS, 1), value, F32)
    row_slots[pl.ds(mp, 1)] = pack_lanes(
        [row_max, row_sum, row_weighted, constant(resid_norm), constant(direc_norm)]
    )[None]
    plane_stat[pl.ds(c * NY + y, 1)] = fold(
        [col_max, jnp.concatenate(col_sum, 1), jnp.concatenate(col_weighted, 1), slope_row]
    )[None]

    def join_columns(slots, count):
        parts = [unfold(slots[k], 4) for k in range(count)]
        top, total, weighted = softmax_join([(part[0:1], part[1:2], part[2:3]) for part in parts])
        slopes = functools.reduce(jnp.add, [part[3:4] for part in parts])
        return top, total, weighted, slopes

    def sum_slots(slots, count):
        return functools.reduce(jnp.add, [slots[k] for k in range(count)])

    def spread_h(slots):
        return over_h(lambda h: slots.at[zh], lambda q: slots.at[zh])

    def spread_m(slots):
        return over_m(lambda m: slots.at[mp], lambda q: slots.at[mp])

    copies = over_plane(plane_stat)
    row_copies = spread_m(row_slots)
    arrive(copies)
    z_stat[pl.ds(zh, 1)] = fold(join_columns(plane_stat, NC * NY))[None]
    copies = spread_h(z_stat)
    arrive(row_copies)
    parts = [row_slots[k] for k in range(NM)]
    top, total, weighted = softmax_join([(part[0:1], part[1:2], part[2:3]) for part in parts])
    norms = functools.reduce(jnp.add, [part[3:5] for part in parts])
    norm_old = norms[0:1, 0:1]
    norm_direc = norms[1:2, 0:1]
    row_info = unpack_lanes(jnp.concatenate([top + jnp.log(total), weighted / total], 0))
    row_lse, row_dot = row_info[:, 0:1], row_info[:, 1:2]
    arrive(copies)
    top, total, weighted, slopes = join_columns(z_stat, NH)
    col_lse, col_dot = top + jnp.log(total), weighted / total
    col_slope = unpack_lanes(slopes)

    row_ids = lax.broadcasted_iota(jnp.int32, (ROWS, TILE), 0)
    col_ids = lax.broadcasted_iota(jnp.int32, (ROWS, TILE), 1)
    offset = mp * SHARE - first_col
    row_along = jnp.zeros((ROWS, 1), F32)
    row_turned = jnp.zeros((ROWS, 1), F32)
    col_along, col_turned = [], []
    for tile in range(tiles):
        span = slice(tile * TILE, (tile + 1) * TILE)
        score = scores[:, span]
        left, right = left_ts[:, span], right_ts[:, span]
        tscore = left + right
        row_w = jnp.exp(score - row_lse)
        col_w = jnp.exp(score - col_lse[:, span])
        place = col_ids + tile * TILE
        mine = (place >= first_col) & (place < first_col + SHARE) & (row_ids == place + offset)
        low = ((row_w + col_w - 2.0 * mine.astype(F32)) / (2.0 * PAIRS)).astype(BF16)
        dsc[:, span] = low
        tdsc[:, span] = (
            (row_w * (tscore - row_dot) + col_w * (tscore - col_dot[:, span])) / (2.0 * PAIRS)
        ).astype(BF16)
        wide = low.astype(F32)
        row_along += jnp.sum(wide * score, 1, keepdims=True)
        row_turned += jnp.sum(wide * left, 1, keepdims=True)
        col_along.append(jnp.sum(wide * score, 0, keepdims=True))
        col_turned.append(jnp.sum(wide * right, 0, keepdims=True))
    grad_slots[pl.ds(mp, 1)] = pack_lanes([row_along, row_turned])[None]
    plane_grad[pl.ds(c * NY + y, 1)] = fold([jnp.concatenate(col_along, 1), jnp.concatenate(col_turned, 1)])[None]
    grad_copies = spread_m(grad_slots)
    plane_copies = over_plane(plane_grad)

    TN = ((0,), (0,))
    cvec[...] = col_slope

    def column_terms(core, high):
        start = pl.multiple_of((core * NH + high) * BLOCKS, BLOCKS)
        d_low, t_low = dsc[:, pl.ds(start, BLOCKS)], tdsc[:, pl.ds(start, BLOCKS)]
        total = dot(t_low, rows_u[...], TN) + dot(d_low, rows_t[...], TN)
        total -= cvec[pl.ds(start, BLOCKS), 0:1] * dot(d_low, rows_u[...], TN)
        return (LOGIT_SCALE * total).reshape(NY, SHARE, WIDTH)

    steps = (2, 1, 3, 0)
    passed = []

    def away(place):
        col_away[place] = column_terms(1 - c, h_at(steps[place]))
        passed.extend(over_c(col_away.at[place], col_recv.at[place]))

    away(0)
    away(1)
    y_copies = []
    for place, step in enumerate(steps):
        terms = column_terms(c, h_at(step))
        passed[place].wait_recv()
        terms = terms + col_recv[place]
        col_low[place] = terms.astype(BF16)
        col_part[place] = terms
        y_copies.append(over_y(lambda r: col_low.at[place, r], lambda q: y_recv.at[place, q - 1]))
        if place + 2 < NH:
            away(place + 2)

    for tile in range(WIDTH // TILE):
        span = slice(tile * TILE, (tile + 1) * TILE)
        u_piece = cols[:, :, :, 0, :, span].reshape(COLS, TILE)
        t_piece = cols[:, :, :, 1, :, span].reshape(COLS, TILE)
        total = dot(tdsc[...], u_piece) + dot(dsc[...], t_piece) - row_slope * dot(dsc[...], u_piece)
        row_part[:, :, :, span] = (LOGIT_SCALE * total).reshape(NL, NX, SHARE, TILE)
    x_copies = over_x(lambda k: row_part.at[:, k], lambda q: x_recv.at[q - 1])

    arrive(plane_copies)
    z_grad[pl.ds(zh, 1)] = sum_slots(plane_grad, NC * NY)[None]
    z_grad_copies = spread_h(z_grad)

    def column_sum(place):
        arrive(y_copies[place])
        return functools.reduce(jnp.add, [y_recv[place, q].astype(F32) for q in range(NY - 1)], col_part[place, y])

    def column_high(place):
        step = steps[place]
        col_part[place, y] = column_sum(place)
        return [send(col_part.at[place, y], z_recv.at[step - 1], device(high=h_at(step)))]

    high_copies = column_high(0)
    high_copies += column_high(1)
    arrive(x_copies)
    for low in range(NL):
        row_part[low, x] += x_recv[0, low] + x_recv[1, low] + x_recv[2, low]
    l_copies = over_l(row_part.at[1 - zl, x], l_recv)
    arrive(grad_copies)
    grad_rows[...] = unpack_lanes(sum_slots(grad_slots, NM))

    def finish(raw, tangent, value, info):
        unit, inverse = unit_of(raw)
        turned, _ = turn_of(tangent, unit, inverse)
        mixed = info[:, 1:2] + jnp.sum(unit * value, -1, keepdims=True)
        return ((value - turned * info[:, 0:1] - unit * mixed) * inverse).astype(BF16)

    def spread_tdz(tower):
        block = tdz.at[tower, mp]
        return over_m(lambda m: block, lambda q: block)

    high_copies += column_high(2)
    arrive(z_grad_copies)
    grad_cols[...] = unpack_lanes(unfold(sum_slots(z_grad, NH), 2))
    arrive(l_copies)
    tdz[0, mp] = finish(rawbuf[own], tanbuf[own], row_part[zl, x] + l_recv[...], grad_rows[own])
    sar_copies = spread_tdz(0)
    own_sum = column_sum(3)
    arrive(high_copies)
    tdz[1, mp] = finish(
        rawbuf[ROWS : ROWS + SHARE],
        tanbuf[ROWS : ROWS + SHARE],
        own_sum + z_recv[0] + z_recv[1] + z_recv[2],
        grad_cols[pl.ds(first_col, SHARE)],
    )
    optical_copies = spread_tdz(1)

    curve = 0.0
    for tower, copies in enumerate((sar_copies, optical_copies)):
        arrive(copies)
        part = dot(feats[tower, :, pl.ds(pl.multiple_of(mp * PART, PART), PART)], tdz[tower].reshape(ROWS, WIDTH), TN)
        part_hess[tower] = part.reshape(part_hess.shape[1:])
        curve += jnp.sum(direc[tower] * part)
    passed = over_c(part_hess.at[1 - c], core_hess)
    scal_m[pl.ds(mp, 1)] = jnp.full((1, 8, 128), curve, F32)
    scal_copies = spread_m(scal_m)
    arrive(passed)
    part_hess[pl.ds(c, 1)] += core_hess[...][None]
    row_copies = [
        over_y(lambda r: part_hess.at[c, r, half], lambda q: y_hess.at[half, q - 1]) for half in range(2)
    ]
    arrive(scal_copies)
    scal_p[pl.ds(c * NY + y, 1)] = sum_slots(scal_m, NM)[None]
    scal_copies = over_plane(scal_p)
    high_copies = []
    for half in range(2):
        arrive(row_copies[half])
        z_hess[half, zh] = part_hess[c, y, half] + y_hess[half, 0] + y_hess[half, 1] + y_hess[half, 2]
        block = z_hess.at[half, zh]
        high_copies.append(over_h(lambda h: block, lambda q: block))
    arrive(scal_copies)
    scal_z[pl.ds(zh, 1)] = sum_slots(scal_p, NC * NY)[None]
    scal_copies = spread_h(scal_z)

    def hess_rows(half):
        block = hess.at[c, y, half]
        return over_y(lambda r: block, lambda q: block)

    def hess_sum(half):
        arrive(high_copies[half])
        hess[c, y, half] = functools.reduce(jnp.add, [z_hess[half, k] for k in range(NH)])

    hess_sum(0)
    row_copies = [hess_rows(0)]
    arrive(scal_copies)
    curve = sum_slots(scal_z, NH)[0:1, 0:1] + DAMPING * norm_direc
    alpha = norm_old / curve
    hess_sum(1)
    piece = pl.ds(pl.multiple_of(y * BLOCK, BLOCK), BLOCK)
    after = resid[c, piece] - alpha * (hess[c, y].reshape(BLOCK, WIDTH) + DAMPING * direc[c, piece])
    norm_p[pl.ds(c * NY + y, 1)] = jnp.full((1, 8, 128), jnp.sum(after * after), F32)
    scal_copies = over_plane(norm_p)
    row_copies.append(hess_rows(1))
    passed = over_c(hess.at[c, y], hess.at[c, y])
    for half in range(2):
        for q, copy in enumerate(row_copies[half], 1):
            copy.wait_recv()
            block = hess.at[c, (y + NY - q) % NY, half]
            passed += over_c(block, block)
        if half == 0:
            arrive(scal_copies)
            norm_m[pl.ds(mp, 1)] = sum_slots(norm_p, NC * NY)[None]
            scal_copies = spread_m(norm_m)
    arrive(passed)
    store = load(hess, hess_out, 7)
    arrive(scal_copies)
    norm_new = sum_slots(norm_m, NM)[0:1, 0:1]
    first_row = lax.broadcasted_iota(jnp.int32, (8, 128), 0) == 0
    info_out[...] = jnp.where(first_row, alpha, norm_new / norm_old)
    store.wait()
    for copy in pending:
        copy.wait_send()
    assert counter[0] <= SEMS


def last_kernel(info, hess, direc, resid, solu, out_sol, out_res, out_dir, sol, res, way, store_sem):
    alpha, beta = info[0:1, 0:1], info[1:2, 0:1]
    stores = []

    def store(source, target, tower):
        copy = pltpu.make_async_copy(source.at[tower], target.at[tower], store_sem.at[len(stores)])
        copy.start()
        stores.append(copy)

    for tower in range(2):
        direction = direc[tower]
        sol[tower] = solu[tower] + alpha * direction
        store(sol, out_sol, tower)
        after = resid[tower] - alpha * (hess[tower] + DAMPING * direction)
        res[tower] = after
        store(res, out_res, tower)
        way[tower] = after + beta * direction
        store(way, out_dir, tower)
    for copy in stores:
        copy.wait()


def body(features, projections, solution, residual, direction):
    vmem = pl.BlockSpec(memory_space=pltpu.VMEM)
    hbm = pl.BlockSpec(memory_space=pltpu.HBM)
    f32 = lambda *size: pltpu.VMEM(size, F32)
    bf16 = lambda *size: pltpu.VMEM(size, BF16)
    scratch = [
        bf16(2, ROWS, DEPTH), f32(2, PART, WIDTH), f32(2, PART, WIDTH),
        bf16(2, 2, NM, PART, WIDTH), bf16(2, NY, NM - 1, QUARTER, WIDTH),
        f32(ROWS + SHARE, WIDTH), f32(ROWS + SHARE, WIDTH),
        bf16(ROWS, WIDTH), bf16(ROWS, WIDTH),
        bf16(NC, NH, NY, 2, SHARE, WIDTH),
        f32(ROWS, COLS), f32(ROWS, COLS), f32(ROWS, COLS),
        bf16(ROWS, COLS), bf16(ROWS, COLS), f32(COLS, 128),
        f32(NM, 8, ROWS), f32(NC * NY, 8, COLS // 2), f32(NH, 8, COLS // 2),
        f32(NM, 8, ROWS), f32(NC * NY, 8, COLS // 4), f32(NH, 8, COLS // 4),
        f32(NL, NX, SHARE, WIDTH), f32(NX - 1, NL, SHARE, WIDTH), f32(SHARE, WIDTH),
        f32(NH, NY, SHARE, WIDTH), f32(NH, NY, SHARE, WIDTH), bf16(NH, NY, SHARE, WIDTH),
        f32(NH, NY, SHARE, WIDTH), bf16(NH, NY - 1, SHARE, WIDTH), f32(NH - 1, SHARE, WIDTH),
        f32(COLS, 128), f32(ROWS, 128),
        bf16(2, NM, SHARE, WIDTH),
        f32(2, NY, 2, HALF, WIDTH), f32(NY, 2, HALF, WIDTH),
        f32(2, NY - 1, HALF, WIDTH), f32(2, NH, HALF, WIDTH), f32(2, NY, 2, HALF, WIDTH),
        f32(NM, 8, 128), f32(NC * NY, 8, 128), f32(NH, 8, 128),
        f32(NC * NY, 8, 128), f32(NM, 8, 128),
        pltpu.SemaphoreType.DMA((SEMS,)), pltpu.SemaphoreType.DMA((SEMS,)), pltpu.SemaphoreType.DMA((8,)),
    ]
    hess, info = pl.pallas_call(
        kernel,
        name="cg_step",
        out_shape=(
            jax.ShapeDtypeStruct((2, NY, 2, HALF, WIDTH), F32),
            jax.ShapeDtypeStruct((8, 128), F32),
        ),
        in_specs=[hbm] * 4,
        out_specs=(pl.BlockSpec(memory_space=pl.ANY), vmem),
        scratch_shapes=scratch,
        compiler_params=pltpu.CompilerParams(
            collective_id=0, has_side_effects=True, vmem_limit_bytes=58 * 2**20
        ),
    )(features, projections, direction, residual)
    shape = jax.ShapeDtypeStruct(direction.shape, F32)
    return pl.pallas_call(
        last_kernel,
        name="updates",
        out_shape=(shape, shape, shape),
        in_specs=[vmem] * 5,
        out_specs=(hbm, hbm, hbm),
        scratch_shapes=[f32(2, PART, WIDTH)] * 3 + [pltpu.SemaphoreType.DMA((6,))],
        compiler_params=pltpu.CompilerParams(vmem_limit_bytes=16 * 2**20),
    )(info, hess.reshape(direction.shape), direction, residual, solution)


def solution(mesh):
    placed = (
        P(None, "dp", None),
        P(None, "mp", None),
        P(None, "mp", None),
        P(None, "mp", None),
        P(None, "mp", None),
    )
    return jax.shard_map(
        body,
        mesh=mesh,
        in_specs=placed,
        out_specs=(P(None, "mp", None), P(None, "mp", None), P(None, "mp", None)),
        check_vma=False,
    )
```

```python
import functools

import jax
import jax.numpy as jnp
from jax import lax
from jax.experimental import pallas as pl
from jax.experimental.pallas import tpu as pltpu
from jax.sharding import PartitionSpec as P

LOGIT_SCALE = 100.0
DAMPING = 1.0
EPSILON = 1e-06

NC, NY, NH, NX, NL = 2, 4, 4, 4, 2
NM = NX * NL
ROWS, DEPTH, WIDTH = 256, 1024, 768
PART = DEPTH // NM
SHARE = ROWS // NM
COLS = SHARE * NC * NY * NH
PAIRS = ROWS * NC * NY * NH
TILE = 256
SEMS = 224
QUARTER = 16
DIRECT = PART - NY * QUARTER
BLOCK = PART // NY
BLOCKS = SHARE * NY
WIDE = WIDTH // 2
F32, BF16 = jnp.float32, jnp.bfloat16
MESH = pl.DeviceIdType.MESH


def dot(left, right, dims=((1,), (0,))):
    return lax.dot_general(left, right, (dims, ((), ())), preferred_element_type=F32)


def unit_of(raw):
    inverse = lax.rsqrt(jnp.sum(raw * raw, -1, keepdims=True) + EPSILON)
    return raw * inverse, inverse


def turn_of(tangent, unit, inverse):
    along = jnp.sum(unit * tangent, -1, keepdims=True)
    return (tangent - unit * along) * inverse, along


def pack_lanes(columns):
    size = columns[0].shape[0]
    lane = lax.broadcasted_iota(jnp.int32, (size, 128), 1)
    wide = jnp.zeros((size, 128), F32)
    for place, column in enumerate(columns):
        wide = jnp.where(lane == place, column, wide)
    return wide.T[0:8]


def unpack_lanes(rows):
    return jnp.concatenate([rows, jnp.zeros((128 - rows.shape[0], rows.shape[1]), F32)], 0).T


def fold(rows):
    size = rows[0].shape[1] * len(rows) // 8
    stacked = jnp.concatenate(rows, 0)
    return jnp.concatenate([stacked[:, k : k + size] for k in range(0, stacked.shape[1], size)], 0)


def unfold(block, count):
    return jnp.concatenate([block[k : k + count] for k in range(0, 8, count)], 1)


def softmax_join(slots):
    top = functools.reduce(jnp.maximum, [slot[0] for slot in slots])
    total = 0.0
    weighted = 0.0
    for slot in slots:
        factor = jnp.exp(slot[0] - top)
        total = total + factor * slot[1]
        weighted = weighted + factor * slot[2]
    return top, total, weighted


def kernel(
    feats_in, proj_in, direc_in, resid_in,
    hess_out,
    feats, direc, resid, weights, quarters, rawbuf, tanbuf, rows_u, rows_t, cols,
    scores, left_ts, right_ts, dsc, tdsc, cvec,
    row_slots, plane_stat, z_stat,
    grad_slots, plane_grad, z_grad,
    row_part, x_recv, l_recv, col_away, col_part, col_low, col_recv, y_recv, z_recv,
    grad_cols, grad_rows, tdz, part_hess, core_hess, y_hess, z_hess, hess,
    scal_m, scal_p, scal_z, norm_p, norm_m, info,
    send_sem, recv_sem, load_sem,
):
    dp, mp = lax.axis_index("dp"), lax.axis_index("mp")
    c, y, zh = dp % NC, (dp // NC) % NY, dp // (NC * NY)
    x, zl = mp % NX, mp // NX
    partner = (1 - zl) * NX + x
    counter = [0]

    def device(core=None, row=None, high=None, model=None):
        core, row, high = c if core is None else core, y if row is None else row, zh if high is None else high
        return {"dp": (high * NY + row) * NC + core, "mp": mp if model is None else model}

    def m_at(step):
        return ((zl + step // NX) % NL) * NX + (x + step % NX) % NX

    def m_from(step):
        return ((zl + step // NX) % NL) * NX + (x + NX - step % NX) % NX

    def x_at(step):
        return (x + step) % NX

    def y_at(step):
        return (y + step) % NY

    def h_at(step):
        return (zh + step) % NH

    def send(source, target, where):
        place = counter[0]
        counter[0] += 1
        copy = pltpu.make_async_remote_copy(
            src_ref=source, dst_ref=target, send_sem=send_sem.at[place], recv_sem=recv_sem.at[place],
            device_id=where, device_id_type=MESH,
        )
        copy.start()
        pending.append(copy)
        return copy

    pending = []

    def arrive(copies):
        for copy in copies:
            copy.wait_recv()

    def over_m(source, target):
        return [send(source(m_at(q)), target(q), device(model=m_at(q))) for q in range(1, NM)]

    def over_y(source, target):
        return [send(source(y_at(q)), target(q), device(row=y_at(q))) for q in range(1, NY)]

    def over_h(source, target):
        copies = {q: send(source(h_at(q)), target(q), device(high=h_at(q))) for q in (2, 1, 3)}
        return [copies[q] for q in range(1, NH)]

    def over_x(source, target):
        return [send(source(x_at(q)), target(q), device(model=zl * NX + x_at(q))) for q in range(1, NX)]

    def over_l(source, target):
        return [send(source, target, device(model=partner))]

    def over_plane(slots):
        place = slots.at[c * NY + y]
        return [
            send(place, place, device(core=(c + q // NY) % NC, row=(y + q % NY) % NY)) for q in range(1, NC * NY)
        ]

    def over_c(source, target):
        return [send(source, target, device(core=1 - c))]

    def load(source, target, place):
        copy = pltpu.make_async_copy(source, target, load_sem.at[place])
        copy.start()
        return copy

    barrier = pltpu.get_barrier_semaphore()
    for q in (2, 1, 3):
        pl.semaphore_signal(barrier, inc=1, device_id=device(high=h_at(q)), device_id_type=MESH)
    for q in range(1, NM):
        pl.semaphore_signal(barrier, inc=1, device_id=device(model=m_at(q)), device_id_type=MESH)
    for q in range(1, NC * NY):
        where = device(core=(c + q // NY) % NC, row=(y + q % NY) % NY)
        pl.semaphore_signal(barrier, inc=1, device_id=where, device_id_type=MESH)
    load_direc = [load(direc_in.at[tower], direc.at[tower], tower) for tower in (1, 0)]
    load_proj = [load(proj_in.at[tower], weights.at[0, tower, mp], 2 + tower) for tower in (1, 0)]
    load_feats = [load(feats_in.at[tower], feats.at[tower], 4 + tower) for tower in (1, 0)]
    load_resid = load(resid_in, resid, 6)
    load_direc[0].wait()
    weights[1, 1, pl.ds(mp, 1)] = direc[1].astype(BF16)[None]
    load_proj[0].wait()
    pl.semaphore_wait(barrier, NM + NC * NY + NH - 3)

    part = weights.at[c, 1, mp, pl.ds(pl.multiple_of(DIRECT + y * QUARTER, QUARTER), QUARTER)]
    quarter_copies = over_m(lambda m: part, lambda q: quarters.at[c, y, q - 1])
    def optical(m):
        return weights.at[c, 1, m, pl.ds(0, DIRECT)]

    def sar(m):
        return weights.at[c, 0, m]

    def spread_x(block):
        return over_x(lambda m: block, lambda q: block)

    def pass_on(blocks, low, copies):
        passed = []
        for q, copy in enumerate(copies, 1):
            copy.wait_recv()
            block = blocks(low * NX + (x + NX - q) % NX)
            passed += over_c(block, block)
        return passed

    l_copies = over_l(optical(mp), optical(mp))
    x_copies = spread_x(optical(mp))
    load_direc[1].wait()
    weights[1, 0, pl.ds(mp, 1)] = direc[0].astype(BF16)[None]
    load_proj[1].wait()
    sar_l_copies = over_l(sar(mp), sar(mp))
    arrive(quarter_copies)
    mine = quarters.at[c, y]
    row_copies = over_y(lambda r: mine, lambda q: mine)
    arrive(l_copies)
    x_relays = spread_x(optical(partner))
    passed = over_c(mine, mine) + over_c(optical(partner), optical(partner))
    passed += pass_on(optical, zl, x_copies)
    sar_x_copies = spread_x(sar(mp))
    passed += pass_on(optical, 1 - zl, x_relays)
    arrive(sar_l_copies)
    sar_x_relays = spread_x(sar(partner))
    for q, copy in enumerate(row_copies, 1):
        copy.wait_recv()
        block = quarters.at[c, (y + NY - q) % NY]
        passed += over_c(block, block)
    load_feats[0].wait()
    arrive(passed)
    for kind in range(2):
        for q in range(1, NM):
            for r in range(NY):
                weights[kind, 1, m_from(q), DIRECT + r * QUARTER : DIRECT + (r + 1) * QUARTER] = quarters[kind, r, q - 1]

    def embed(kind, tower, rows, into, first):
        for tile in range(WIDTH // TILE):
            span = slice(tile * TILE, (tile + 1) * TILE)
            total = 0.0
            for block in range(0, NM, 2):
                deep = slice(block * PART, (block + 2) * PART)
                piece = weights[kind, tower, block : block + 2, :, span].reshape(2 * PART, TILE)
                total += dot(feats[tower, rows, deep], piece)
            into[first : first + total.shape[0], span] = total

    own = pl.ds(pl.multiple_of(mp * SHARE, SHARE), SHARE)
    embed(0, 1, own, rawbuf, ROWS)
    embed(1, 1, own, tanbuf, ROWS)
    unit, inverse = unit_of(rawbuf[ROWS : ROWS + SHARE])
    turned, along = turn_of(tanbuf[ROWS : ROWS + SHARE], unit, inverse)
    cols[c, zh, y, 0] = unit.astype(BF16)
    cols[c, zh, y, 1] = turned.astype(BF16)
    slope = inverse * along

    def column_block(high, row):
        return cols.at[c, high, row]

    def column_rows(high):
        block = column_block(high, y)
        return over_c(block, block), over_y(lambda r: block, lambda q: block)

    def column_pass(high, copies):
        passed = []
        for q, copy in enumerate(copies, 1):
            copy.wait_recv()
            block = column_block(high, (y + NY - q) % NY)
            passed += over_c(block, block)
        return passed

    mine = column_block(zh, y)
    high_copies = over_h(lambda h: mine, lambda q: mine)
    passed, copies = column_rows(zh)
    col_passed = [passed]
    waiting = [(zh, copies)]
    first_col = pl.multiple_of(((c * NH + zh) * NY + y) * SHARE, SHARE)
    cvec[...] = jnp.zeros_like(cvec)
    cvec[pl.ds(first_col, SHARE)] = jnp.broadcast_to(slope, (SHARE, 128))
    slope_row = cvec[...].T[0:1]
    for q in (1, 3, 2):
        high_copies[q - 1].wait_recv()
        high = (zh + NH - q) % NH
        passed, copies = column_rows(high)
        col_passed.append(passed)
        waiting.append((high, copies))
    col_passed[0] += column_pass(*waiting[0])
    passed = over_c(sar(partner), sar(partner))
    passed += pass_on(sar, zl, sar_x_copies)
    col_passed[1] += column_pass(*waiting[1])
    passed += pass_on(sar, 1 - zl, sar_x_relays)
    load_feats[1].wait()
    arrive(passed)
    col_passed[2] += column_pass(*waiting[2])
    every = slice(0, ROWS)
    embed(0, 0, every, rawbuf, 0)
    embed(1, 0, every, tanbuf, 0)
    unit, inverse = unit_of(rawbuf[every])
    turned, along = turn_of(tanbuf[every], unit, inverse)
    rows_u[...] = unit.astype(BF16)
    rows_t[...] = turned.astype(BF16)
    row_slope = inverse * along
    NT = ((1,), (1,))
    tiles = COLS // TILE
    for place, (high, copies) in enumerate(waiting):
        if place == NH - 1:
            col_passed[place] += column_pass(high, copies)
        arrive(col_passed[place])
        piece = [cols[:, high, :, kind].reshape(NC * BLOCKS, WIDTH) for kind in range(2)]
        for target, rows, kind in ((scores, rows_u, 0), (left_ts, rows_t, 0), (right_ts, rows_u, 1)):
            product = LOGIT_SCALE * dot(rows[...], piece[kind], NT)
            for core in range(NC):
                start = pl.multiple_of((core * NH + high) * BLOCKS, BLOCKS)
                target[:, pl.ds(start, BLOCKS)] = product[:, core * BLOCKS : (core + 1) * BLOCKS]
    row_max = jnp.max(scores[...], 1, keepdims=True)
    col_max = jnp.max(scores[...], 0, keepdims=True)
    row_sum = jnp.zeros((ROWS, 1), F32)
    row_weighted = jnp.zeros((ROWS, 1), F32)
    col_sum, col_weighted = [], []
    for tile in range(tiles):
        span = slice(tile * TILE, (tile + 1) * TILE)
        score = scores[:, span]
        tscore = left_ts[:, span] + right_ts[:, span]
        weight = jnp.exp(score - row_max)
        row_sum += jnp.sum(weight, 1, keepdims=True)
        row_weighted += jnp.sum(weight * tscore, 1, keepdims=True)
        weight = jnp.exp(score - col_max[:, span])
        col_sum.append(jnp.sum(weight, 0, keepdims=True))
        col_weighted.append(jnp.sum(weight * tscore, 0, keepdims=True))
    load_resid.wait()
    resid_norm = jnp.sum(resid[...] * resid[...])
    direc_norm = jnp.sum(direc[...] * direc[...])
    constant = lambda value: jnp.full((ROWS, 1), value, F32)
    row_slots[pl.ds(mp, 1)] = pack_lanes(
        [row_max, row_sum, row_weighted, constant(resid_norm), constant(direc_norm)]
    )[None]
    plane_stat[pl.ds(c * NY + y, 1)] = fold(
        [col_max, jnp.concatenate(col_sum, 1), jnp.concatenate(col_weighted, 1), slope_row]
    )[None]

    def join_columns(slots, count):
        parts = [unfold(slots[k], 4) for k in range(count)]
        top, total, weighted = softmax_join([(part[0:1], part[1:2], part[2:3]) for part in parts])
        slopes = functools.reduce(jnp.add, [part[3:4] for part in parts])
        return top, total, weighted, slopes

    def sum_slots(slots, count):
        return functools.reduce(jnp.add, [slots[k] for k in range(count)])

    def spread_h(slots):
        return over_h(lambda h: slots.at[zh], lambda q: slots.at[zh])

    def spread_m(slots):
        return over_m(lambda m: slots.at[mp], lambda q: slots.at[mp])

    copies = over_plane(plane_stat)
    row_copies = spread_m(row_slots)
    arrive(copies)
    z_stat[pl.ds(zh, 1)] = fold(join_columns(plane_stat, NC * NY))[None]
    copies = spread_h(z_stat)
    arrive(row_copies)
    parts = [row_slots[k] for k in range(NM)]
    top, total, weighted = softmax_join([(part[0:1], part[1:2], part[2:3]) for part in parts])
    norms = functools.reduce(jnp.add, [part[3:5] for part in parts])
    norm_old = norms[0:1, 0:1]
    norm_direc = norms[1:2, 0:1]
    row_info = unpack_lanes(jnp.concatenate([top + jnp.log(total), weighted / total], 0))
    row_lse, row_dot = row_info[:, 0:1], row_info[:, 1:2]
    arrive(copies)
    top, total, weighted, slopes = join_columns(z_stat, NH)
    col_lse, col_dot = top + jnp.log(total), weighted / total
    col_slope = unpack_lanes(slopes)

    row_ids = lax.broadcasted_iota(jnp.int32, (ROWS, TILE), 0)
    col_ids = lax.broadcasted_iota(jnp.int32, (ROWS, TILE), 1)
    offset = mp * SHARE - first_col
    row_along = jnp.zeros((ROWS, 1), F32)
    row_turned = jnp.zeros((ROWS, 1), F32)
    col_along, col_turned = [], []
    for tile in range(tiles):
        span = slice(tile * TILE, (tile + 1) * TILE)
        score = scores[:, span]
        left, right = left_ts[:, span], right_ts[:, span]
        tscore = left + right
        row_w = jnp.exp(score - row_lse)
        col_w = jnp.exp(score - col_lse[:, span])
        place = col_ids + tile * TILE
        mine = (place >= first_col) & (place < first_col + SHARE) & (row_ids == place + offset)
        low = ((row_w + col_w - 2.0 * mine.astype(F32)) / (2.0 * PAIRS)).astype(BF16)
        dsc[:, span] = low
        tdsc[:, span] = (
            (row_w * (tscore - row_dot) + col_w * (tscore - col_dot[:, span])) / (2.0 * PAIRS)
        ).astype(BF16)
        wide = low.astype(F32)
        row_along += jnp.sum(wide * score, 1, keepdims=True)
        row_turned += jnp.sum(wide * left, 1, keepdims=True)
        col_along.append(jnp.sum(wide * score, 0, keepdims=True))
        col_turned.append(jnp.sum(wide * right, 0, keepdims=True))
    grad_slots[pl.ds(mp, 1)] = pack_lanes([row_along, row_turned])[None]
    plane_grad[pl.ds(c * NY + y, 1)] = fold([jnp.concatenate(col_along, 1), jnp.concatenate(col_turned, 1)])[None]
    grad_copies = spread_m(grad_slots)
    plane_copies = over_plane(plane_grad)

    TN = ((0,), (0,))
    cvec[...] = col_slope

    def column_terms(core, high):
        start = pl.multiple_of((core * NH + high) * BLOCKS, BLOCKS)
        d_low, t_low = dsc[:, pl.ds(start, BLOCKS)], tdsc[:, pl.ds(start, BLOCKS)]
        total = dot(t_low, rows_u[...], TN) + dot(d_low, rows_t[...], TN)
        total -= cvec[pl.ds(start, BLOCKS), 0:1] * dot(d_low, rows_u[...], TN)
        return (LOGIT_SCALE * total).reshape(NY, SHARE, WIDTH)

    steps = (2, 1, 3, 0)
    passed = []

    def away(place):
        col_away[place] = column_terms(1 - c, h_at(steps[place]))
        passed.extend(over_c(col_away.at[place], col_recv.at[place]))

    away(0)
    away(1)

    for tile in range(WIDTH // TILE):
        span = slice(tile * TILE, (tile + 1) * TILE)
        u_piece = cols[:, :, :, 0, :, span].reshape(COLS, TILE)
        t_piece = cols[:, :, :, 1, :, span].reshape(COLS, TILE)
        total = dot(tdsc[...], u_piece) + dot(dsc[...], t_piece) - row_slope * dot(dsc[...], u_piece)
        row_part[:, :, :, span] = (LOGIT_SCALE * total).reshape(NL, NX, SHARE, TILE)
    x_copies = over_x(lambda k: row_part.at[:, k], lambda q: x_recv.at[q - 1])

    y_copies = []
    for place, step in enumerate(steps):
        terms = column_terms(c, h_at(step))
        passed[place].wait_recv()
        terms = terms + col_recv[place]
        col_low[place] = terms.astype(BF16)
        col_part[place] = terms
        y_copies.append(over_y(lambda r: col_low.at[place, r], lambda q: y_recv.at[place, q - 1]))
        if place + 2 < NH:
            away(place + 2)

    arrive(plane_copies)
    z_grad[pl.ds(zh, 1)] = sum_slots(plane_grad, NC * NY)[None]
    z_grad_copies = spread_h(z_grad)

    def column_sum(place):
        arrive(y_copies[place])
        return functools.reduce(jnp.add, [y_recv[place, q].astype(F32) for q in range(NY - 1)], col_part[place, y])

    def column_high(place):
        step = steps[place]
        col_part[place, y] = column_sum(place)
        return [send(col_part.at[place, y], z_recv.at[step - 1], device(high=h_at(step)))]

    high_copies = column_high(0)
    high_copies += column_high(1)
    high_copies += column_high(2)
    arrive(x_copies)
    for low in range(NL):
        row_part[low, x] += x_recv[0, low] + x_recv[1, low] + x_recv[2, low]
    l_copies = over_l(row_part.at[1 - zl, x], l_recv)
    arrive(grad_copies)
    grad_rows[...] = unpack_lanes(sum_slots(grad_slots, NM))

    def finish(raw, tangent, value, terms):
        unit, inverse = unit_of(raw)
        turned, _ = turn_of(tangent, unit, inverse)
        mixed = terms[:, 1:2] + jnp.sum(unit * value, -1, keepdims=True)
        return ((value - turned * terms[:, 0:1] - unit * mixed) * inverse).astype(BF16)

    def spread_tdz(tower):
        block = tdz.at[tower, mp]
        return over_m(lambda m: block, lambda q: block)

    arrive(l_copies)
    tdz[0, mp] = finish(rawbuf[own], tanbuf[own], row_part[zl, x] + l_recv[...], grad_rows[own])
    sar_copies = spread_tdz(0)
    arrive(z_grad_copies)
    grad_cols[...] = unpack_lanes(unfold(sum_slots(z_grad, NH), 2))
    own_sum = column_sum(3)
    arrive(high_copies)
    tdz[1, mp] = finish(
        rawbuf[ROWS : ROWS + SHARE],
        tanbuf[ROWS : ROWS + SHARE],
        own_sum + z_recv[0] + z_recv[1] + z_recv[2],
        grad_cols[pl.ds(first_col, SHARE)],
    )
    optical_copies = spread_tdz(1)

    lanes = pl.ds(pl.multiple_of(c * WIDE, 128), WIDE)
    block_rows = pl.ds(pl.multiple_of(y * BLOCK, BLOCK), BLOCK)

    def hess_terms(tower):
        part = dot(feats[tower, :, pl.ds(pl.multiple_of(mp * PART, PART), PART)], tdz[tower].reshape(ROWS, WIDTH), TN)
        for half in range(2):
            part_hess[tower, half] = part[:, half * WIDE : (half + 1) * WIDE].reshape(NY, BLOCK, WIDE)
        return jnp.sum(direc[tower] * part), over_c(part_hess.at[tower, 1 - c], core_hess.at[tower])

    def hess_rows(tower, copies):
        arrive(copies)
        part_hess[tower, c] += core_hess[tower]
        return over_y(lambda r: part_hess.at[tower, c, r], lambda q: y_hess.at[tower, q - 1])

    def hess_high(tower, copies):
        arrive(copies)
        z_hess[tower, zh] = part_hess[tower, c, y] + y_hess[tower, 0] + y_hess[tower, 1] + y_hess[tower, 2]
        block = z_hess.at[tower, zh]
        return over_h(lambda h: block, lambda q: block)

    def hess_sum(tower, copies):
        arrive(copies)
        hess[tower, c, block_rows] = functools.reduce(jnp.add, [z_hess[tower, k] for k in range(NH)])

    def hess_back(tower):
        block = hess.at[tower, c, block_rows]
        return over_c(block, block), over_y(lambda r: block, lambda q: block)

    def hess_pass(tower, copies):
        passed = []
        for q, copy in enumerate(copies, 1):
            copy.wait_recv()
            row = (y + NY - q) % NY
            block = hess.at[tower, c, pl.ds(pl.multiple_of(row * BLOCK, BLOCK), BLOCK)]
            passed += over_c(block, block)
        return passed

    arrive(sar_copies)
    first_curve, core_first = hess_terms(0)
    row_first = hess_rows(0, core_first)
    arrive(optical_copies)
    curve, core_second = hess_terms(1)
    scal_m[pl.ds(mp, 1)] = jnp.full((1, 8, 128), first_curve + curve, F32)
    scal_copies = spread_m(scal_m)
    row_second = hess_rows(1, core_second)
    high_first = hess_high(0, row_first)
    arrive(scal_copies)
    scal_p[pl.ds(c * NY + y, 1)] = sum_slots(scal_m, NM)[None]
    scal_copies = over_plane(scal_p)
    high_second = hess_high(1, row_second)
    arrive(scal_copies)
    scal_z[pl.ds(zh, 1)] = sum_slots(scal_p, NC * NY)[None]
    scal_copies = spread_h(scal_z)
    hess_sum(0, high_first)
    passed, back_first = hess_back(0)
    arrive(scal_copies)
    curve = sum_slots(scal_z, NH)[0:1, 0:1] + DAMPING * norm_direc
    alpha = norm_old / curve
    hess_sum(1, high_second)
    total = 0.0
    for tower in range(2):
        after = resid[tower, block_rows, lanes]
        after -= alpha * (hess[tower, c, block_rows] + DAMPING * direc[tower, block_rows, lanes])
        total += jnp.sum(after * after)
    norm_p[pl.ds(c * NY + y, 1)] = jnp.full((1, 8, 128), total, F32)
    scal_copies = over_plane(norm_p)
    more, back_second = hess_back(1)
    passed += more
    passed += hess_pass(0, back_first)
    arrive(scal_copies)
    norm_m[pl.ds(mp, 1)] = sum_slots(norm_p, NC * NY)[None]
    scal_copies = spread_m(norm_m)
    passed += hess_pass(1, back_second)
    arrive(passed)
    stores = []
    for tower in range(2):
        for half in range(2):
            target = hess_out.at[tower * PART : (tower + 1) * PART, half * WIDE : (half + 1) * WIDE]
            stores.append(load(hess.at[tower, half], target, 7 + 2 * tower + half))
    arrive(scal_copies)
    norm_new = sum_slots(norm_m, NM)[0:1, 0:1]
    first_row = lax.broadcasted_iota(jnp.int32, (8, WIDTH), 0) == 0
    info[...] = jnp.where(first_row, alpha, norm_new / norm_old)
    stores.append(load(info, hess_out.at[2 * PART : 2 * PART + 8], 11))
    for store in stores:
        store.wait()
    for copy in pending:
        copy.wait_send()
    assert counter[0] <= SEMS


def last_kernel(hess, direc, resid, solu, out_sol, out_res, out_dir, sol, res, way, store_sem):
    alpha, beta = hess[2 * PART : 2 * PART + 1, 0:1], hess[2 * PART + 1 : 2 * PART + 2, 0:1]
    stores = []

    def store(source, target, tower):
        copy = pltpu.make_async_copy(source.at[tower], target.at[tower], store_sem.at[len(stores)])
        copy.start()
        stores.append(copy)

    for tower in range(2):
        direction = direc[tower]
        sol[tower] = solu[tower] + alpha * direction
        store(sol, out_sol, tower)
        part = hess[tower * PART : (tower + 1) * PART]
        after = resid[tower] - alpha * (part + DAMPING * direction)
        res[tower] = after
        store(res, out_res, tower)
        way[tower] = after + beta * direction
        store(way, out_dir, tower)
    for copy in stores:
        copy.wait()


def body(features, projections, solution, residual, direction):
    vmem = pl.BlockSpec(memory_space=pltpu.VMEM)
    hbm = pl.BlockSpec(memory_space=pltpu.HBM)
    f32 = lambda *size: pltpu.VMEM(size, F32)
    bf16 = lambda *size: pltpu.VMEM(size, BF16)
    scratch = [
        bf16(2, ROWS, DEPTH), f32(2, PART, WIDTH), f32(2, PART, WIDTH),
        bf16(2, 2, NM, PART, WIDTH), bf16(2, NY, NM - 1, QUARTER, WIDTH),
        f32(ROWS + SHARE, WIDTH), f32(ROWS + SHARE, WIDTH),
        bf16(ROWS, WIDTH), bf16(ROWS, WIDTH),
        bf16(NC, NH, NY, 2, SHARE, WIDTH),
        f32(ROWS, COLS), f32(ROWS, COLS), f32(ROWS, COLS),
        bf16(ROWS, COLS), bf16(ROWS, COLS), f32(COLS, 128),
        f32(NM, 8, ROWS), f32(NC * NY, 8, COLS // 2), f32(NH, 8, COLS // 2),
        f32(NM, 8, ROWS), f32(NC * NY, 8, COLS // 4), f32(NH, 8, COLS // 4),
        f32(NL, NX, SHARE, WIDTH), f32(NX - 1, NL, SHARE, WIDTH), f32(SHARE, WIDTH),
        f32(NH, NY, SHARE, WIDTH), f32(NH, NY, SHARE, WIDTH), bf16(NH, NY, SHARE, WIDTH),
        f32(NH, NY, SHARE, WIDTH), bf16(NH, NY - 1, SHARE, WIDTH), f32(NH - 1, SHARE, WIDTH),
        f32(COLS, 128), f32(ROWS, 128),
        bf16(2, NM, SHARE, WIDTH),
        f32(2, 2, NY, BLOCK, WIDE), f32(2, NY, BLOCK, WIDE),
        f32(2, NY - 1, BLOCK, WIDE), f32(2, NH, BLOCK, WIDE), f32(2, 2, PART, WIDE),
        f32(NM, 8, 128), f32(NC * NY, 8, 128), f32(NH, 8, 128),
        f32(NC * NY, 8, 128), f32(NM, 8, 128), f32(8, WIDTH),
        pltpu.SemaphoreType.DMA((SEMS,)), pltpu.SemaphoreType.DMA((SEMS,)), pltpu.SemaphoreType.DMA((12,)),
    ]
    hess = pl.pallas_call(
        kernel,
        name="cg_step",
        out_shape=jax.ShapeDtypeStruct((2 * PART + 8, WIDTH), F32),
        in_specs=[hbm] * 4,
        out_specs=pl.BlockSpec(memory_space=pl.ANY),
        scratch_shapes=scratch,
        compiler_params=pltpu.CompilerParams(
            collective_id=0, has_side_effects=True, vmem_limit_bytes=58 * 2**20
        ),
    )(features, projections, direction, residual)
    shape = jax.ShapeDtypeStruct(direction.shape, F32)
    return pl.pallas_call(
        last_kernel,
        name="updates",
        out_shape=(shape, shape, shape),
        in_specs=[vmem] * 4,
        out_specs=(hbm, hbm, hbm),
        scratch_shapes=[f32(2, PART, WIDTH)] * 3 + [pltpu.SemaphoreType.DMA((6,))],
        compiler_params=pltpu.CompilerParams(vmem_limit_bytes=16 * 2**20),
    )(hess, direction, residual, solution)


def solution(mesh):
    placed = (
        P(None, "dp", None),
        P(None, "mp", None),
        P(None, "mp", None),
        P(None, "mp", None),
        P(None, "mp", None),
    )
    return jax.shard_map(
        body,
        mesh=mesh,
        in_specs=placed,
        out_specs=(P(None, "mp", None), P(None, "mp", None), P(None, "mp", None)),
        check_vma=False,
    )
```

```python
import functools

import jax
import jax.numpy as jnp
from jax import lax
from jax.experimental import pallas as pl
from jax.experimental.pallas import tpu as pltpu
from jax.sharding import PartitionSpec as P

LOGIT_SCALE = 100.0
DAMPING = 1.0
EPSILON = 1e-06

NC, NY, NH, NX, NL = 2, 4, 4, 4, 2
NM = NX * NL
ROWS, DEPTH, WIDTH = 256, 1024, 768
PART = DEPTH // NM
SHARE = ROWS // NM
COLS = SHARE * NC * NY * NH
PAIRS = ROWS * NC * NY * NH
TILE = 256
SEMS = 224
QUARTER = 16
DIRECT = PART - NY * QUARTER
BLOCK = PART // NY
BLOCKS = SHARE * NY
WIDE = WIDTH // 2
F32, BF16 = jnp.float32, jnp.bfloat16
MESH = pl.DeviceIdType.MESH


def dot(left, right, dims=((1,), (0,))):
    return lax.dot_general(left, right, (dims, ((), ())), preferred_element_type=F32)


def unit_of(raw):
    inverse = lax.rsqrt(jnp.sum(raw * raw, -1, keepdims=True) + EPSILON)
    return raw * inverse, inverse


def turn_of(tangent, unit, inverse):
    along = jnp.sum(unit * tangent, -1, keepdims=True)
    return (tangent - unit * along) * inverse, along


def pack_lanes(columns):
    size = columns[0].shape[0]
    lane = lax.broadcasted_iota(jnp.int32, (size, 128), 1)
    wide = jnp.zeros((size, 128), F32)
    for place, column in enumerate(columns):
        wide = jnp.where(lane == place, column, wide)
    return wide.T[0:8]


def unpack_lanes(rows):
    return jnp.concatenate([rows, jnp.zeros((128 - rows.shape[0], rows.shape[1]), F32)], 0).T


def fold(rows):
    size = rows[0].shape[1] * len(rows) // 8
    stacked = jnp.concatenate(rows, 0)
    return jnp.concatenate([stacked[:, k : k + size] for k in range(0, stacked.shape[1], size)], 0)


def unfold(block, count):
    return jnp.concatenate([block[k : k + count] for k in range(0, 8, count)], 1)


def softmax_join(slots):
    top = functools.reduce(jnp.maximum, [slot[0] for slot in slots])
    total = 0.0
    weighted = 0.0
    for slot in slots:
        factor = jnp.exp(slot[0] - top)
        total = total + factor * slot[1]
        weighted = weighted + factor * slot[2]
    return top, total, weighted


def kernel(
    feats_in, proj_in, direc_in, resid_in,
    hess_out,
    feats, direc, resid, weights, quarters, rawbuf, tanbuf, rows_u, rows_t, cols,
    scores, left_ts, right_ts, dsc, tdsc, cvec,
    row_slots, plane_stat, z_stat,
    grad_slots, plane_grad, z_grad,
    row_part, x_recv, l_recv, col_away, col_part, col_low, col_recv, y_recv, z_recv,
    grad_cols, grad_rows, tdz, part_hess, core_hess, y_hess, z_hess, hess,
    norm_p, norm_m, info,
    send_sem, recv_sem, load_sem,
):
    dp, mp = lax.axis_index("dp"), lax.axis_index("mp")
    c, y, zh = dp % NC, (dp // NC) % NY, dp // (NC * NY)
    x, zl = mp % NX, mp // NX
    partner = (1 - zl) * NX + x
    counter = [0]

    def device(core=None, row=None, high=None, model=None):
        core, row, high = c if core is None else core, y if row is None else row, zh if high is None else high
        return {"dp": (high * NY + row) * NC + core, "mp": mp if model is None else model}

    def m_at(step):
        return ((zl + step // NX) % NL) * NX + (x + step % NX) % NX

    def m_from(step):
        return ((zl + step // NX) % NL) * NX + (x + NX - step % NX) % NX

    def x_at(step):
        return (x + step) % NX

    def y_at(step):
        return (y + step) % NY

    def h_at(step):
        return (zh + step) % NH

    def send(source, target, where):
        place = counter[0]
        counter[0] += 1
        copy = pltpu.make_async_remote_copy(
            src_ref=source, dst_ref=target, send_sem=send_sem.at[place], recv_sem=recv_sem.at[place],
            device_id=where, device_id_type=MESH,
        )
        copy.start()
        pending.append(copy)
        return copy

    pending = []

    def arrive(copies):
        for copy in copies:
            copy.wait_recv()

    def over_m(source, target):
        return [send(source(m_at(q)), target(q), device(model=m_at(q))) for q in range(1, NM)]

    def over_y(source, target):
        return [send(source(y_at(q)), target(q), device(row=y_at(q))) for q in range(1, NY)]

    def over_h(source, target):
        copies = {q: send(source(h_at(q)), target(q), device(high=h_at(q))) for q in (2, 1, 3)}
        return [copies[q] for q in range(1, NH)]

    def over_x(source, target):
        return [send(source(x_at(q)), target(q), device(model=zl * NX + x_at(q))) for q in range(1, NX)]

    def over_l(source, target):
        return [send(source, target, device(model=partner))]

    def over_plane(slots):
        place = slots.at[c * NY + y]
        return [
            send(place, place, device(core=(c + q // NY) % NC, row=(y + q % NY) % NY)) for q in range(1, NC * NY)
        ]

    def over_c(source, target):
        return [send(source, target, device(core=1 - c))]

    def load(source, target, place):
        copy = pltpu.make_async_copy(source, target, load_sem.at[place])
        copy.start()
        return copy

    barrier = pltpu.get_barrier_semaphore()
    for q in (2, 1, 3):
        pl.semaphore_signal(barrier, inc=1, device_id=device(high=h_at(q)), device_id_type=MESH)
    for q in range(1, NM):
        pl.semaphore_signal(barrier, inc=1, device_id=device(model=m_at(q)), device_id_type=MESH)
    for q in range(1, NC * NY):
        where = device(core=(c + q // NY) % NC, row=(y + q % NY) % NY)
        pl.semaphore_signal(barrier, inc=1, device_id=where, device_id_type=MESH)
    load_direc = [load(direc_in.at[tower], direc.at[tower], tower) for tower in (1, 0)]
    load_proj = [load(proj_in.at[tower], weights.at[0, tower, mp], 2 + tower) for tower in (1, 0)]
    load_feats = [load(feats_in.at[tower], feats.at[tower], 4 + tower) for tower in (1, 0)]
    load_resid = load(resid_in, resid, 6)
    load_direc[0].wait()
    weights[1, 1, pl.ds(mp, 1)] = direc[1].astype(BF16)[None]
    load_proj[0].wait()
    pl.semaphore_wait(barrier, NM + NC * NY + NH - 3)

    part = weights.at[c, 1, mp, pl.ds(pl.multiple_of(DIRECT + y * QUARTER, QUARTER), QUARTER)]
    quarter_copies = over_m(lambda m: part, lambda q: quarters.at[c, y, q - 1])
    def optical(m):
        return weights.at[c, 1, m, pl.ds(0, DIRECT)]

    def sar(m):
        return weights.at[c, 0, m]

    def spread_x(block):
        return over_x(lambda m: block, lambda q: block)

    def pass_on(blocks, low, copies):
        passed = []
        for q, copy in enumerate(copies, 1):
            copy.wait_recv()
            block = blocks(low * NX + (x + NX - q) % NX)
            passed += over_c(block, block)
        return passed

    l_copies = over_l(optical(mp), optical(mp))
    x_copies = spread_x(optical(mp))
    load_direc[1].wait()
    weights[1, 0, pl.ds(mp, 1)] = direc[0].astype(BF16)[None]
    load_proj[1].wait()
    sar_l_copies = over_l(sar(mp), sar(mp))
    arrive(quarter_copies)
    mine = quarters.at[c, y]
    row_copies = over_y(lambda r: mine, lambda q: mine)
    arrive(l_copies)
    x_relays = spread_x(optical(partner))
    passed = over_c(mine, mine) + over_c(optical(partner), optical(partner))
    passed += pass_on(optical, zl, x_copies)
    sar_x_copies = spread_x(sar(mp))
    passed += pass_on(optical, 1 - zl, x_relays)
    arrive(sar_l_copies)
    sar_x_relays = spread_x(sar(partner))
    for q, copy in enumerate(row_copies, 1):
        copy.wait_recv()
        block = quarters.at[c, (y + NY - q) % NY]
        passed += over_c(block, block)
    load_feats[0].wait()
    arrive(passed)
    for kind in range(2):
        for q in range(1, NM):
            for r in range(NY):
                weights[kind, 1, m_from(q), DIRECT + r * QUARTER : DIRECT + (r + 1) * QUARTER] = quarters[kind, r, q - 1]

    def embed(kind, tower, rows, into, first):
        for tile in range(WIDTH // TILE):
            span = slice(tile * TILE, (tile + 1) * TILE)
            total = 0.0
            for block in range(0, NM, 2):
                deep = slice(block * PART, (block + 2) * PART)
                piece = weights[kind, tower, block : block + 2, :, span].reshape(2 * PART, TILE)
                total += dot(feats[tower, rows, deep], piece)
            into[first : first + total.shape[0], span] = total

    own = pl.ds(pl.multiple_of(mp * SHARE, SHARE), SHARE)
    embed(0, 1, own, rawbuf, ROWS)
    embed(1, 1, own, tanbuf, ROWS)
    unit, inverse = unit_of(rawbuf[ROWS : ROWS + SHARE])
    turned, along = turn_of(tanbuf[ROWS : ROWS + SHARE], unit, inverse)
    cols[c, zh, y, 0] = unit.astype(BF16)
    cols[c, zh, y, 1] = turned.astype(BF16)
    slope = inverse * along

    def column_block(high, row):
        return cols.at[c, high, row]

    def column_rows(high):
        block = column_block(high, y)
        return over_c(block, block), over_y(lambda r: block, lambda q: block)

    def column_pass(high, copies):
        passed = []
        for q, copy in enumerate(copies, 1):
            copy.wait_recv()
            block = column_block(high, (y + NY - q) % NY)
            passed += over_c(block, block)
        return passed

    mine = column_block(zh, y)
    high_copies = over_h(lambda h: mine, lambda q: mine)
    passed, copies = column_rows(zh)
    col_passed = [passed]
    waiting = [(zh, copies)]
    first_col = pl.multiple_of(((c * NH + zh) * NY + y) * SHARE, SHARE)
    cvec[...] = jnp.zeros_like(cvec)
    cvec[pl.ds(first_col, SHARE)] = jnp.broadcast_to(slope, (SHARE, 128))
    slope_row = cvec[...].T[0:1]
    for q in (1, 3, 2):
        high_copies[q - 1].wait_recv()
        high = (zh + NH - q) % NH
        passed, copies = column_rows(high)
        col_passed.append(passed)
        waiting.append((high, copies))
    col_passed[0] += column_pass(*waiting[0])
    passed = over_c(sar(partner), sar(partner))
    passed += pass_on(sar, zl, sar_x_copies)
    col_passed[1] += column_pass(*waiting[1])
    passed += pass_on(sar, 1 - zl, sar_x_relays)
    load_feats[1].wait()
    arrive(passed)
    col_passed[2] += column_pass(*waiting[2])
    every = slice(0, ROWS)
    embed(0, 0, every, rawbuf, 0)
    embed(1, 0, every, tanbuf, 0)
    unit, inverse = unit_of(rawbuf[every])
    turned, along = turn_of(tanbuf[every], unit, inverse)
    rows_u[...] = unit.astype(BF16)
    rows_t[...] = turned.astype(BF16)
    row_slope = inverse * along
    NT = ((1,), (1,))
    tiles = COLS // TILE
    for place, (high, copies) in enumerate(waiting):
        if place == NH - 1:
            col_passed[place] += column_pass(high, copies)
        arrive(col_passed[place])
        piece = [cols[:, high, :, kind].reshape(NC * BLOCKS, WIDTH) for kind in range(2)]
        for target, rows, kind in ((scores, rows_u, 0), (left_ts, rows_t, 0), (right_ts, rows_u, 1)):
            product = LOGIT_SCALE * dot(rows[...], piece[kind], NT)
            for core in range(NC):
                start = pl.multiple_of((core * NH + high) * BLOCKS, BLOCKS)
                target[:, pl.ds(start, BLOCKS)] = product[:, core * BLOCKS : (core + 1) * BLOCKS]
    row_max = jnp.max(scores[...], 1, keepdims=True)
    col_max = jnp.max(scores[...], 0, keepdims=True)
    row_sum = jnp.zeros((ROWS, 1), F32)
    row_weighted = jnp.zeros((ROWS, 1), F32)
    col_sum, col_weighted = [], []
    for tile in range(tiles):
        span = slice(tile * TILE, (tile + 1) * TILE)
        score = scores[:, span]
        tscore = left_ts[:, span] + right_ts[:, span]
        weight = jnp.exp(score - row_max)
        row_sum += jnp.sum(weight, 1, keepdims=True)
        row_weighted += jnp.sum(weight * tscore, 1, keepdims=True)
        weight = jnp.exp(score - col_max[:, span])
        col_sum.append(jnp.sum(weight, 0, keepdims=True))
        col_weighted.append(jnp.sum(weight * tscore, 0, keepdims=True))
    load_resid.wait()
    resid_norm = jnp.sum(resid[...] * resid[...])
    constant = lambda value: jnp.full((ROWS, 1), value, F32)
    row_slots[pl.ds(mp, 1)] = pack_lanes(
        [row_max, row_sum, row_weighted, constant(resid_norm)]
    )[None]
    plane_stat[pl.ds(c * NY + y, 1)] = fold(
        [col_max, jnp.concatenate(col_sum, 1), jnp.concatenate(col_weighted, 1), slope_row]
    )[None]

    def join_columns(slots, count):
        parts = [unfold(slots[k], 4) for k in range(count)]
        top, total, weighted = softmax_join([(part[0:1], part[1:2], part[2:3]) for part in parts])
        slopes = functools.reduce(jnp.add, [part[3:4] for part in parts])
        return top, total, weighted, slopes

    def sum_slots(slots, count):
        return functools.reduce(jnp.add, [slots[k] for k in range(count)])

    def spread_h(slots):
        return over_h(lambda h: slots.at[zh], lambda q: slots.at[zh])

    def spread_m(slots):
        return over_m(lambda m: slots.at[mp], lambda q: slots.at[mp])

    copies = over_plane(plane_stat)
    row_copies = spread_m(row_slots)
    arrive(copies)
    z_stat[pl.ds(zh, 1)] = fold(join_columns(plane_stat, NC * NY))[None]
    copies = spread_h(z_stat)
    arrive(row_copies)
    parts = [row_slots[k] for k in range(NM)]
    top, total, weighted = softmax_join([(part[0:1], part[1:2], part[2:3]) for part in parts])
    norms = functools.reduce(jnp.add, [part[3:4] for part in parts])
    norm_old = norms[0:1, 0:1]
    row_info = unpack_lanes(jnp.concatenate([top + jnp.log(total), weighted / total], 0))
    row_lse, row_dot = row_info[:, 0:1], row_info[:, 1:2]
    arrive(copies)
    top, total, weighted, slopes = join_columns(z_stat, NH)
    col_lse, col_dot = top + jnp.log(total), weighted / total
    col_slope = unpack_lanes(slopes)

    row_ids = lax.broadcasted_iota(jnp.int32, (ROWS, TILE), 0)
    col_ids = lax.broadcasted_iota(jnp.int32, (ROWS, TILE), 1)
    offset = mp * SHARE - first_col
    row_along = jnp.zeros((ROWS, 1), F32)
    row_turned = jnp.zeros((ROWS, 1), F32)
    col_along, col_turned = [], []
    for tile in range(tiles):
        span = slice(tile * TILE, (tile + 1) * TILE)
        score = scores[:, span]
        left, right = left_ts[:, span], right_ts[:, span]
        tscore = left + right
        row_w = jnp.exp(score - row_lse)
        col_w = jnp.exp(score - col_lse[:, span])
        place = col_ids + tile * TILE
        mine = (place >= first_col) & (place < first_col + SHARE) & (row_ids == place + offset)
        low = ((row_w + col_w - 2.0 * mine.astype(F32)) / (2.0 * PAIRS)).astype(BF16)
        dsc[:, span] = low
        tdsc[:, span] = (
            (row_w * (tscore - row_dot) + col_w * (tscore - col_dot[:, span])) / (2.0 * PAIRS)
        ).astype(BF16)
        wide = low.astype(F32)
        row_along += jnp.sum(wide * score, 1, keepdims=True)
        row_turned += jnp.sum(wide * left, 1, keepdims=True)
        col_along.append(jnp.sum(wide * score, 0, keepdims=True))
        col_turned.append(jnp.sum(wide * right, 0, keepdims=True))
    grad_slots[pl.ds(mp, 1)] = pack_lanes([row_along, row_turned])[None]
    plane_grad[pl.ds(c * NY + y, 1)] = fold([jnp.concatenate(col_along, 1), jnp.concatenate(col_turned, 1)])[None]
    grad_copies = spread_m(grad_slots)
    plane_copies = over_plane(plane_grad)

    TN = ((0,), (0,))
    cvec[...] = col_slope

    def column_terms(core, high):
        start = pl.multiple_of((core * NH + high) * BLOCKS, BLOCKS)
        d_low, t_low = dsc[:, pl.ds(start, BLOCKS)], tdsc[:, pl.ds(start, BLOCKS)]
        total = dot(t_low, rows_u[...], TN) + dot(d_low, rows_t[...], TN)
        total -= cvec[pl.ds(start, BLOCKS), 0:1] * dot(d_low, rows_u[...], TN)
        return (LOGIT_SCALE * total).reshape(NY, SHARE, WIDTH)

    steps = (2, 1, 3, 0)
    passed = []

    def away(place):
        col_away[place] = column_terms(1 - c, h_at(steps[place]))
        passed.extend(over_c(col_away.at[place], col_recv.at[place]))

    away(0)
    away(1)

    for tile in range(WIDTH // TILE):
        span = slice(tile * TILE, (tile + 1) * TILE)
        u_piece = cols[:, :, :, 0, :, span].reshape(COLS, TILE)
        t_piece = cols[:, :, :, 1, :, span].reshape(COLS, TILE)
        total = dot(tdsc[...], u_piece) + dot(dsc[...], t_piece) - row_slope * dot(dsc[...], u_piece)
        row_part[:, :, :, span] = (LOGIT_SCALE * total).reshape(NL, NX, SHARE, TILE)
    x_copies = over_x(lambda k: row_part.at[:, k], lambda q: x_recv.at[q - 1])

    y_copies = []
    for place, step in enumerate(steps):
        terms = column_terms(c, h_at(step))
        passed[place].wait_recv()
        terms = terms + col_recv[place]
        col_low[place] = terms.astype(BF16)
        col_part[place] = terms
        y_copies.append(over_y(lambda r: col_low.at[place, r], lambda q: y_recv.at[place, q - 1]))
        if place + 2 < NH:
            away(place + 2)

    arrive(plane_copies)
    z_grad[pl.ds(zh, 1)] = sum_slots(plane_grad, NC * NY)[None]
    z_grad_copies = spread_h(z_grad)

    def column_sum(place):
        arrive(y_copies[place])
        return functools.reduce(jnp.add, [y_recv[place, q].astype(F32) for q in range(NY - 1)], col_part[place, y])

    def column_high(place):
        step = steps[place]
        col_part[place, y] = column_sum(place)
        return [send(col_part.at[place, y], z_recv.at[step - 1], device(high=h_at(step)))]

    high_copies = column_high(0)
    high_copies += column_high(1)
    high_copies += column_high(2)
    arrive(x_copies)
    for low in range(NL):
        row_part[low, x] += x_recv[0, low] + x_recv[1, low] + x_recv[2, low]
    l_copies = over_l(row_part.at[1 - zl, x], l_recv)
    arrive(grad_copies)
    grad_rows[...] = unpack_lanes(sum_slots(grad_slots, NM))

    def finish(raw, tangent, value, terms):
        unit, inverse = unit_of(raw)
        turned, _ = turn_of(tangent, unit, inverse)
        mixed = terms[:, 1:2] + jnp.sum(unit * value, -1, keepdims=True)
        return ((value - turned * terms[:, 0:1] - unit * mixed) * inverse).astype(BF16)

    def spread_tdz(tower):
        block = tdz.at[tower, mp]
        return over_m(lambda m: block, lambda q: block)

    arrive(l_copies)
    tdz[0, mp] = finish(rawbuf[own], tanbuf[own], row_part[zl, x] + l_recv[...], grad_rows[own])
    sar_copies = spread_tdz(0)
    arrive(z_grad_copies)
    grad_cols[...] = unpack_lanes(unfold(sum_slots(z_grad, NH), 2))
    own_sum = column_sum(3)
    arrive(high_copies)
    tdz[1, mp] = finish(
        rawbuf[ROWS : ROWS + SHARE],
        tanbuf[ROWS : ROWS + SHARE],
        own_sum + z_recv[0] + z_recv[1] + z_recv[2],
        grad_cols[pl.ds(first_col, SHARE)],
    )
    optical_copies = spread_tdz(1)

    lanes = pl.ds(pl.multiple_of(c * WIDE, 128), WIDE)
    block_rows = pl.ds(pl.multiple_of(y * BLOCK, BLOCK), BLOCK)

    def hess_terms(tower):
        part = dot(feats[tower, :, pl.ds(pl.multiple_of(mp * PART, PART), PART)], tdz[tower].reshape(ROWS, WIDTH), TN)
        for half in range(2):
            part_hess[tower, half] = part[:, half * WIDE : (half + 1) * WIDE].reshape(NY, BLOCK, WIDE)
        return over_c(part_hess.at[tower, 1 - c], core_hess.at[tower])

    def hess_rows(tower, copies):
        arrive(copies)
        part_hess[tower, c] += core_hess[tower]
        return over_y(lambda r: part_hess.at[tower, c, r], lambda q: y_hess.at[tower, q - 1])

    def hess_high(tower, copies):
        arrive(copies)
        z_hess[tower, zh] = part_hess[tower, c, y] + y_hess[tower, 0] + y_hess[tower, 1] + y_hess[tower, 2]
        block = z_hess.at[tower, zh]
        return over_h(lambda h: block, lambda q: block)

    def hess_sum(tower, copies):
        arrive(copies)
        hess[tower, c, block_rows] = functools.reduce(jnp.add, [z_hess[tower, k] for k in range(NH)])

    def hess_back(tower):
        block = hess.at[tower, c, block_rows]
        return over_c(block, block), over_y(lambda r: block, lambda q: block)

    def hess_pass(tower, copies):
        passed = []
        for q, copy in enumerate(copies, 1):
            copy.wait_recv()
            row = (y + NY - q) % NY
            block = hess.at[tower, c, pl.ds(pl.multiple_of(row * BLOCK, BLOCK), BLOCK)]
            passed += over_c(block, block)
        return passed

    def hess_inner(tower):
        old = resid[tower, block_rows, lanes]
        along = direc[tower, block_rows, lanes]
        new = hess[tower, c, block_rows] + DAMPING * along
        return [jnp.sum(along * new), jnp.sum(old * new), jnp.sum(new * new)]

    arrive(sar_copies)
    core_first = hess_terms(0)
    row_first = hess_rows(0, core_first)
    arrive(optical_copies)
    core_second = hess_terms(1)
    high_first = hess_high(0, row_first)
    row_second = hess_rows(1, core_second)
    high_second = hess_high(1, row_second)
    hess_sum(0, high_first)
    passed, back_first = hess_back(0)
    inner = hess_inner(0)
    hess_sum(1, high_second)
    inner = [first + second for first, second in zip(inner, hess_inner(1))]
    place = lax.broadcasted_iota(jnp.int32, (1, 8, 128), 1)
    norm_p[pl.ds(c * NY + y, 1)] = jnp.where(place == 0, inner[0], jnp.where(place == 1, inner[1], inner[2]))
    scal_copies = over_plane(norm_p)
    more, back_second = hess_back(1)
    passed += more
    passed += hess_pass(0, back_first)
    arrive(scal_copies)
    norm_m[pl.ds(mp, 1)] = sum_slots(norm_p, NC * NY)[None]
    scal_copies = spread_m(norm_m)
    passed += hess_pass(1, back_second)
    arrive(passed)
    stores = []
    for tower in range(2):
        for half in range(2):
            target = hess_out.at[tower * PART : (tower + 1) * PART, half * WIDE : (half + 1) * WIDE]
            stores.append(load(hess.at[tower, half], target, 7 + 2 * tower + half))
    arrive(scal_copies)
    sums = sum_slots(norm_m, NM)
    alpha = norm_old / sums[0:1, 0:1]
    norm_new = norm_old - 2.0 * alpha * sums[1:2, 0:1] + alpha * alpha * sums[2:3, 0:1]
    first_row = lax.broadcasted_iota(jnp.int32, (8, WIDTH), 0) == 0
    info[...] = jnp.where(first_row, alpha, norm_new / norm_old)
    stores.append(load(info, hess_out.at[2 * PART : 2 * PART + 8], 11))
    for store in stores:
        store.wait()
    for copy in pending:
        copy.wait_send()
    assert counter[0] <= SEMS


def last_kernel(hess, direc, resid, solu, out_sol, out_res, out_dir, sol, res, way, store_sem):
    alpha, beta = hess[2 * PART : 2 * PART + 1, 0:1], hess[2 * PART + 1 : 2 * PART + 2, 0:1]
    stores = []

    def store(source, target, tower):
        copy = pltpu.make_async_copy(source.at[tower], target.at[tower], store_sem.at[len(stores)])
        copy.start()
        stores.append(copy)

    for tower in range(2):
        direction = direc[tower]
        sol[tower] = solu[tower] + alpha * direction
        store(sol, out_sol, tower)
        part = hess[tower * PART : (tower + 1) * PART]
        after = resid[tower] - alpha * (part + DAMPING * direction)
        res[tower] = after
        store(res, out_res, tower)
        way[tower] = after + beta * direction
        store(way, out_dir, tower)
    for copy in stores:
        copy.wait()


def body(features, projections, solution, residual, direction):
    vmem = pl.BlockSpec(memory_space=pltpu.VMEM)
    hbm = pl.BlockSpec(memory_space=pltpu.HBM)
    f32 = lambda *size: pltpu.VMEM(size, F32)
    bf16 = lambda *size: pltpu.VMEM(size, BF16)
    scratch = [
        bf16(2, ROWS, DEPTH), f32(2, PART, WIDTH), f32(2, PART, WIDTH),
        bf16(2, 2, NM, PART, WIDTH), bf16(2, NY, NM - 1, QUARTER, WIDTH),
        f32(ROWS + SHARE, WIDTH), f32(ROWS + SHARE, WIDTH),
        bf16(ROWS, WIDTH), bf16(ROWS, WIDTH),
        bf16(NC, NH, NY, 2, SHARE, WIDTH),
        f32(ROWS, COLS), f32(ROWS, COLS), f32(ROWS, COLS),
        bf16(ROWS, COLS), bf16(ROWS, COLS), f32(COLS, 128),
        f32(NM, 8, ROWS), f32(NC * NY, 8, COLS // 2), f32(NH, 8, COLS // 2),
        f32(NM, 8, ROWS), f32(NC * NY, 8, COLS // 4), f32(NH, 8, COLS // 4),
        f32(NL, NX, SHARE, WIDTH), f32(NX - 1, NL, SHARE, WIDTH), f32(SHARE, WIDTH),
        f32(NH, NY, SHARE, WIDTH), f32(NH, NY, SHARE, WIDTH), bf16(NH, NY, SHARE, WIDTH),
        f32(NH, NY, SHARE, WIDTH), bf16(NH, NY - 1, SHARE, WIDTH), f32(NH - 1, SHARE, WIDTH),
        f32(COLS, 128), f32(ROWS, 128),
        bf16(2, NM, SHARE, WIDTH),
        f32(2, 2, NY, BLOCK, WIDE), f32(2, NY, BLOCK, WIDE),
        f32(2, NY - 1, BLOCK, WIDE), f32(2, NH, BLOCK, WIDE), f32(2, 2, PART, WIDE),
        f32(NC * NY, 8, 128), f32(NM, 8, 128), f32(8, WIDTH),
        pltpu.SemaphoreType.DMA((SEMS,)), pltpu.SemaphoreType.DMA((SEMS,)), pltpu.SemaphoreType.DMA((12,)),
    ]
    hess = pl.pallas_call(
        kernel,
        name="cg_step",
        out_shape=jax.ShapeDtypeStruct((2 * PART + 8, WIDTH), F32),
        in_specs=[hbm] * 4,
        out_specs=pl.BlockSpec(memory_space=pl.ANY),
        scratch_shapes=scratch,
        compiler_params=pltpu.CompilerParams(
            collective_id=0, has_side_effects=True, vmem_limit_bytes=58 * 2**20
        ),
    )(features, projections, direction, residual)
    shape = jax.ShapeDtypeStruct(direction.shape, F32)
    return pl.pallas_call(
        last_kernel,
        name="updates",
        out_shape=(shape, shape, shape),
        in_specs=[vmem] * 4,
        out_specs=(hbm, hbm, hbm),
        scratch_shapes=[f32(2, PART, WIDTH)] * 3 + [pltpu.SemaphoreType.DMA((6,))],
        compiler_params=pltpu.CompilerParams(vmem_limit_bytes=16 * 2**20),
    )(hess, direction, residual, solution)


def solution(mesh):
    placed = (
        P(None, "dp", None),
        P(None, "mp", None),
        P(None, "mp", None),
        P(None, "mp", None),
        P(None, "mp", None),
    )
    return jax.shard_map(
        body,
        mesh=mesh,
        in_specs=placed,
        out_specs=(P(None, "mp", None), P(None, "mp", None), P(None, "mp", None)),
        check_vma=False,
    )
```

```python
import functools

import jax
import jax.numpy as jnp
from jax import lax
from jax.experimental import pallas as pl
from jax.experimental.pallas import tpu as pltpu
from jax.sharding import PartitionSpec as P

LOGIT_SCALE = 100.0
DAMPING = 1.0
EPSILON = 1e-06

NC, NY, NH, NX, NL = 2, 4, 4, 4, 2
NM = NX * NL
ROWS, DEPTH, WIDTH = 256, 1024, 768
PART = DEPTH // NM
SHARE = ROWS // NM
COLS = SHARE * NC * NY * NH
PAIRS = ROWS * NC * NY * NH
TILE = 256
SEMS = 288
QUARTER = 16
DIRECT = PART - NY * QUARTER
BLOCK = PART // NY
BLOCKS = SHARE * NY
WIDE = WIDTH // 2
F32, BF16 = jnp.float32, jnp.bfloat16
MESH = pl.DeviceIdType.MESH


def dot(left, right, dims=((1,), (0,))):
    return lax.dot_general(left, right, (dims, ((), ())), preferred_element_type=F32)


def unit_of(raw):
    inverse = lax.rsqrt(jnp.sum(raw * raw, -1, keepdims=True) + EPSILON)
    return raw * inverse, inverse


def turn_of(tangent, unit, inverse):
    along = jnp.sum(unit * tangent, -1, keepdims=True)
    return (tangent - unit * along) * inverse, along


def pack_lanes(columns):
    size = columns[0].shape[0]
    lane = lax.broadcasted_iota(jnp.int32, (size, 128), 1)
    wide = jnp.zeros((size, 128), F32)
    for place, column in enumerate(columns):
        wide = jnp.where(lane == place, column, wide)
    return wide.T[0:8]


def unpack_lanes(rows):
    return jnp.concatenate([rows, jnp.zeros((128 - rows.shape[0], rows.shape[1]), F32)], 0).T


def fold(rows):
    size = rows[0].shape[1] * len(rows) // 8
    stacked = jnp.concatenate(rows, 0)
    return jnp.concatenate([stacked[:, k : k + size] for k in range(0, stacked.shape[1], size)], 0)


def unfold(block, count):
    return jnp.concatenate([block[k : k + count] for k in range(0, 8, count)], 1)


def softmax_join(slots):
    top = functools.reduce(jnp.maximum, [slot[0] for slot in slots])
    total = 0.0
    weighted = 0.0
    for slot in slots:
        factor = jnp.exp(slot[0] - top)
        total = total + factor * slot[1]
        weighted = weighted + factor * slot[2]
    return top, total, weighted


def kernel(
    feats_in, proj_in, direc_in, resid_in,
    hess_out,
    feats, direc, resid, weights, quarters, rawbuf, tanbuf, rows_u, rows_t, cols,
    scores, left_ts, right_ts, dsc, tdsc, cvec,
    row_slots, plane_stat, z_stat,
    grad_slots, plane_grad, z_grad,
    row_part, x_recv, l_recv, col_away, col_part, col_low, col_recv, y_recv, z_recv,
    grad_cols, grad_rows, tdz, part_hess, core_hess, y_hess, z_hess, hess,
    norm_p, norm_m, info,
    send_sem, recv_sem, load_sem,
):
    dp, mp = lax.axis_index("dp"), lax.axis_index("mp")
    c, y, zh = dp % NC, (dp // NC) % NY, dp // (NC * NY)
    x, zl = mp % NX, mp // NX
    partner = (1 - zl) * NX + x
    counter = [0]

    def device(core=None, row=None, high=None, model=None):
        core, row, high = c if core is None else core, y if row is None else row, zh if high is None else high
        return {"dp": (high * NY + row) * NC + core, "mp": mp if model is None else model}

    def m_at(step):
        return ((zl + step // NX) % NL) * NX + (x + step % NX) % NX

    def m_from(step):
        return ((zl + step // NX) % NL) * NX + (x + NX - step % NX) % NX

    def x_at(step):
        return (x + step) % NX

    def y_at(step):
        return (y + step) % NY

    def h_at(step):
        return (zh + step) % NH

    def send(source, target, where):
        place = counter[0]
        counter[0] += 1
        copy = pltpu.make_async_remote_copy(
            src_ref=source, dst_ref=target, send_sem=send_sem.at[place], recv_sem=recv_sem.at[place],
            device_id=where, device_id_type=MESH,
        )
        copy.start()
        pending.append(copy)
        return copy

    pending = []

    def arrive(copies):
        for copy in copies:
            copy.wait_recv()

    def over_m(source, target):
        return [send(source(m_at(q)), target(q), device(model=m_at(q))) for q in range(1, NM)]

    def over_y(source, target):
        return [send(source(y_at(q)), target(q), device(row=y_at(q))) for q in range(1, NY)]

    def over_h(source, target):
        copies = {q: send(source(h_at(q)), target(q), device(high=h_at(q))) for q in (2, 1, 3)}
        return [copies[q] for q in range(1, NH)]

    def over_x(source, target):
        return [send(source(x_at(q)), target(q), device(model=zl * NX + x_at(q))) for q in range(1, NX)]

    def over_l(source, target):
        return [send(source, target, device(model=partner))]

    def over_plane(slots):
        place = slots.at[c * NY + y]
        return [
            send(place, place, device(core=(c + q // NY) % NC, row=(y + q % NY) % NY)) for q in range(1, NC * NY)
        ]

    def over_c(source, target):
        return [send(source, target, device(core=1 - c))]

    def load(source, target, place):
        copy = pltpu.make_async_copy(source, target, load_sem.at[place])
        copy.start()
        return copy

    barrier = pltpu.get_barrier_semaphore()
    for q in (2, 1, 3):
        pl.semaphore_signal(barrier, inc=1, device_id=device(high=h_at(q)), device_id_type=MESH)
    for q in range(1, NM):
        pl.semaphore_signal(barrier, inc=1, device_id=device(model=m_at(q)), device_id_type=MESH)
    for q in range(1, NC * NY):
        where = device(core=(c + q // NY) % NC, row=(y + q % NY) % NY)
        pl.semaphore_signal(barrier, inc=1, device_id=where, device_id_type=MESH)
    load_direc = [load(direc_in.at[tower], direc.at[tower], tower) for tower in (1, 0)]
    load_proj = [
        [
            load(
                proj_in.at[tower, :, half * WIDE : (half + 1) * WIDE],
                weights.at[0, tower, half, mp],
                12 + 2 * tower + half,
            )
            for half in range(2)
        ]
        for tower in (1, 0)
    ]
    load_feats = [load(feats_in.at[tower], feats.at[tower], 4 + tower) for tower in (1, 0)]
    load_resid = load(resid_in, resid, 6)
    def own_direction(tower):
        for half in range(2):
            piece = direc[tower, :, half * WIDE : (half + 1) * WIDE].astype(BF16)
            weights[1, tower, half, pl.ds(mp, 1)] = piece[None]

    for copy in load_proj[0]:
        copy.wait()
    load_direc[0].wait()
    own_direction(1)
    pl.semaphore_wait(barrier, NM + NC * NY + NH - 3)

    def optical(kind):
        return lambda m: weights.at[kind, 1, c, m, pl.ds(0, DIRECT)]

    def sar(kind):
        return lambda m: weights.at[kind, 0, c, m]

    def spread_x(block):
        return over_x(lambda m: block, lambda q: block)

    def pass_on(blocks, low, copies):
        passed = []
        for q, copy in enumerate(copies, 1):
            copy.wait_recv()
            block = blocks(low * NX + (x + NX - q) % NX)
            passed += over_c(block, block)
        return passed

    def quarter_start(kind):
        part = weights.at[kind, 1, c, mp, pl.ds(pl.multiple_of(DIRECT + y * QUARTER, QUARTER), QUARTER)]
        return over_m(lambda m: part, lambda q: quarters.at[kind, c, y, q - 1])

    def quarter_rows(kind, copies):
        arrive(copies)
        block = quarters.at[kind, c, y]
        return over_c(block, block), over_y(lambda r: block, lambda q: block)

    def quarter_pass(kind, copies):
        passed = []
        for q, copy in enumerate(copies, 1):
            copy.wait_recv()
            block = quarters.at[kind, c, (y + NY - q) % NY]
            passed += over_c(block, block)
        return passed

    def over_z(blocks):
        return over_l(blocks(mp), blocks(mp))

    def relay(blocks, copies):
        arrive(copies)
        block = blocks(partner)
        return spread_x(block), over_c(block, block)

    def assemble(kind):
        for half in range(2):
            for q in range(1, NM):
                for r in range(NY):
                    rows = slice(DIRECT + r * QUARTER, DIRECT + (r + 1) * QUARTER)
                    weights[kind, 1, half, m_from(q), rows] = quarters[kind, half, r, q - 1]

    def embed(kind, tower, rows, into, first):
        for half in range(2):
            span = slice(half * WIDE, (half + 1) * WIDE)
            total = 0.0
            for block in range(0, NM, 2):
                deep = slice(block * PART, (block + 2) * PART)
                piece = weights[kind, tower, half, block : block + 2].reshape(2 * PART, WIDE)
                total += dot(feats[tower, rows, deep], piece)
            into[first : first + total.shape[0], span] = total

    def column_block(kind, high, row):
        return cols.at[c, high, row, kind]

    def column_rows(kind, high):
        block = column_block(kind, high, y)
        col_passed[high_place(high)] += over_c(block, block)
        waiting[kind].append((high, over_y(lambda r: block, lambda q: block)))

    def column_start(kind):
        block = column_block(kind, zh, y)
        copies = over_h(lambda h: block, lambda q: block)
        column_rows(kind, zh)
        return copies

    def column_relay(kind, copies, q):
        copies[q - 1].wait_recv()
        column_rows(kind, highs[q])

    def column_pass(kind, place):
        high, copies = waiting[kind][place]
        for q, copy in enumerate(copies, 1):
            copy.wait_recv()
            block = column_block(kind, high, (y + NY - q) % NY)
            col_passed[place] += over_c(block, block)

    highs = {q: (zh + NH - q) % NH for q in (0, 1, 3, 2)}
    order = list(highs.values())

    def high_place(high):
        return next(place for place, other in enumerate(order) if other is high)

    waiting = [[], []]
    col_passed = [[], [], [], []]
    highs[0] = order[0] = zh

    quarter_copies = quarter_start(0)
    z_copies = over_z(optical(0))
    x_copies = spread_x(optical(0)(mp))
    for copy in load_proj[1]:
        copy.wait()
    load_direc[1].wait()
    own_direction(0)
    passed_first, quarter_copies = quarter_rows(0, quarter_copies)
    quarter_second = quarter_start(1)
    z_second = over_z(optical(1))
    x_second = spread_x(optical(1)(mp))
    relays, passed = relay(optical(0), z_copies)
    passed_first += passed
    sar_z = [over_z(sar(kind)) for kind in range(2)]
    passed_first += pass_on(optical(0), zl, x_copies)
    passed_second, quarter_second = quarter_rows(1, quarter_second)
    passed_first += quarter_pass(0, quarter_copies)
    passed_first += pass_on(optical(0), 1 - zl, relays)
    relays_second, passed = relay(optical(1), z_second)
    passed_second += passed
    sar_x = spread_x(sar(0)(mp))
    load_feats[0].wait()
    arrive(passed_first)
    assemble(0)
    own = pl.ds(pl.multiple_of(mp * SHARE, SHARE), SHARE)
    share = slice(ROWS, ROWS + SHARE)
    embed(0, 1, own, rawbuf, ROWS)
    unit, inverse = unit_of(rawbuf[share])
    cols[c, zh, y, 0] = unit.astype(BF16)
    high_u = column_start(0)
    passed_second += pass_on(optical(1), zl, x_second)
    passed_second += quarter_pass(1, quarter_second)
    passed_second += pass_on(optical(1), 1 - zl, relays_second)
    sar_relays, sar_passed = relay(sar(0), sar_z[0])
    arrive(passed_second)
    assemble(1)
    embed(1, 1, own, tanbuf, ROWS)
    unit, inverse = unit_of(rawbuf[share])
    turned, along = turn_of(tanbuf[share], unit, inverse)
    cols[c, zh, y, 1] = turned.astype(BF16)
    slope = inverse * along
    high_t = column_start(1)
    sar_x_second = spread_x(sar(1)(mp))
    sar_relays_second, sar_passed_second = relay(sar(1), sar_z[1])
    column_relay(0, high_u, 1)
    column_relay(0, high_u, 3)
    column_pass(0, 0)
    column_relay(0, high_u, 2)
    first_col = pl.multiple_of(((c * NH + zh) * NY + y) * SHARE, SHARE)
    cvec[...] = jnp.zeros_like(cvec)
    cvec[pl.ds(first_col, SHARE)] = jnp.broadcast_to(slope, (SHARE, 128))
    slope_row = cvec[...].T[0:1]
    column_relay(1, high_t, 1)
    column_relay(1, high_t, 3)
    sar_passed += pass_on(sar(0), zl, sar_x)
    column_pass(1, 0)
    column_pass(0, 1)
    sar_passed += pass_on(sar(0), 1 - zl, sar_relays)
    column_relay(1, high_t, 2)
    column_pass(0, 2)
    load_feats[1].wait()
    arrive(sar_passed)
    every = slice(0, ROWS)
    embed(0, 0, every, rawbuf, 0)
    unit, inverse = unit_of(rawbuf[every])
    rows_u[...] = unit.astype(BF16)
    column_pass(0, 3)
    column_pass(1, 1)
    sar_passed_second += pass_on(sar(1), zl, sar_x_second)
    column_pass(1, 2)
    sar_passed_second += pass_on(sar(1), 1 - zl, sar_relays_second)
    arrive(sar_passed_second)
    column_pass(1, 3)
    embed(1, 0, every, tanbuf, 0)
    unit, inverse = unit_of(rawbuf[every])
    turned, along = turn_of(tanbuf[every], unit, inverse)
    rows_t[...] = turned.astype(BF16)
    row_slope = inverse * along

    NT = ((1,), (1,))
    tiles = COLS // TILE
    for place, high in enumerate(order):
        arrive(col_passed[place])
        piece = [cols[:, high, :, kind].reshape(NC * BLOCKS, WIDTH) for kind in range(2)]
        for target, rows, kind in ((scores, rows_u, 0), (left_ts, rows_t, 0), (right_ts, rows_u, 1)):
            product = LOGIT_SCALE * dot(rows[...], piece[kind], NT)
            for core in range(NC):
                start = pl.multiple_of((core * NH + high) * BLOCKS, BLOCKS)
                target[:, pl.ds(start, BLOCKS)] = product[:, core * BLOCKS : (core + 1) * BLOCKS]
    row_max = jnp.max(scores[...], 1, keepdims=True)
    col_max = jnp.max(scores[...], 0, keepdims=True)
    row_sum = jnp.zeros((ROWS, 1), F32)
    row_weighted = jnp.zeros((ROWS, 1), F32)
    col_sum, col_weighted = [], []
    for tile in range(tiles):
        span = slice(tile * TILE, (tile + 1) * TILE)
        score = scores[:, span]
        tscore = left_ts[:, span] + right_ts[:, span]
        weight = jnp.exp(score - row_max)
        row_sum += jnp.sum(weight, 1, keepdims=True)
        row_weighted += jnp.sum(weight * tscore, 1, keepdims=True)
        weight = jnp.exp(score - col_max[:, span])
        col_sum.append(jnp.sum(weight, 0, keepdims=True))
        col_weighted.append(jnp.sum(weight * tscore, 0, keepdims=True))
    load_resid.wait()
    resid_norm = jnp.sum(resid[...] * resid[...])
    constant = lambda value: jnp.full((ROWS, 1), value, F32)
    row_slots[pl.ds(mp, 1)] = pack_lanes(
        [row_max, row_sum, row_weighted, constant(resid_norm)]
    )[None]
    plane_stat[pl.ds(c * NY + y, 1)] = fold(
        [col_max, jnp.concatenate(col_sum, 1), jnp.concatenate(col_weighted, 1), slope_row]
    )[None]

    def join_columns(slots, count):
        parts = [unfold(slots[k], 4) for k in range(count)]
        top, total, weighted = softmax_join([(part[0:1], part[1:2], part[2:3]) for part in parts])
        slopes = functools.reduce(jnp.add, [part[3:4] for part in parts])
        return top, total, weighted, slopes

    def sum_slots(slots, count):
        return functools.reduce(jnp.add, [slots[k] for k in range(count)])

    def spread_h(slots):
        return over_h(lambda h: slots.at[zh], lambda q: slots.at[zh])

    def spread_m(slots):
        return over_m(lambda m: slots.at[mp], lambda q: slots.at[mp])

    copies = over_plane(plane_stat)
    row_copies = spread_m(row_slots)
    arrive(copies)
    z_stat[pl.ds(zh, 1)] = fold(join_columns(plane_stat, NC * NY))[None]
    copies = spread_h(z_stat)
    arrive(row_copies)
    parts = [row_slots[k] for k in range(NM)]
    top, total, weighted = softmax_join([(part[0:1], part[1:2], part[2:3]) for part in parts])
    norms = functools.reduce(jnp.add, [part[3:4] for part in parts])
    norm_old = norms[0:1, 0:1]
    row_info = unpack_lanes(jnp.concatenate([top + jnp.log(total), weighted / total], 0))
    row_lse, row_dot = row_info[:, 0:1], row_info[:, 1:2]
    arrive(copies)
    top, total, weighted, slopes = join_columns(z_stat, NH)
    col_lse, col_dot = top + jnp.log(total), weighted / total
    col_slope = unpack_lanes(slopes)

    row_ids = lax.broadcasted_iota(jnp.int32, (ROWS, TILE), 0)
    col_ids = lax.broadcasted_iota(jnp.int32, (ROWS, TILE), 1)
    offset = mp * SHARE - first_col
    row_along = jnp.zeros((ROWS, 1), F32)
    row_turned = jnp.zeros((ROWS, 1), F32)
    col_along, col_turned = [], []
    for tile in range(tiles):
        span = slice(tile * TILE, (tile + 1) * TILE)
        score = scores[:, span]
        left, right = left_ts[:, span], right_ts[:, span]
        tscore = left + right
        row_w = jnp.exp(score - row_lse)
        col_w = jnp.exp(score - col_lse[:, span])
        place = col_ids + tile * TILE
        mine = (place >= first_col) & (place < first_col + SHARE) & (row_ids == place + offset)
        low = ((row_w + col_w - 2.0 * mine.astype(F32)) / (2.0 * PAIRS)).astype(BF16)
        dsc[:, span] = low
        tdsc[:, span] = (
            (row_w * (tscore - row_dot) + col_w * (tscore - col_dot[:, span])) / (2.0 * PAIRS)
        ).astype(BF16)
        wide = low.astype(F32)
        row_along += jnp.sum(wide * score, 1, keepdims=True)
        row_turned += jnp.sum(wide * left, 1, keepdims=True)
        col_along.append(jnp.sum(wide * score, 0, keepdims=True))
        col_turned.append(jnp.sum(wide * right, 0, keepdims=True))
    grad_slots[pl.ds(mp, 1)] = pack_lanes([row_along, row_turned])[None]
    plane_grad[pl.ds(c * NY + y, 1)] = fold([jnp.concatenate(col_along, 1), jnp.concatenate(col_turned, 1)])[None]
    grad_copies = spread_m(grad_slots)
    plane_copies = over_plane(plane_grad)

    TN = ((0,), (0,))
    cvec[...] = col_slope

    def column_terms(core, high):
        start = pl.multiple_of((core * NH + high) * BLOCKS, BLOCKS)
        d_low, t_low = dsc[:, pl.ds(start, BLOCKS)], tdsc[:, pl.ds(start, BLOCKS)]
        total = dot(t_low, rows_u[...], TN) + dot(d_low, rows_t[...], TN)
        total -= cvec[pl.ds(start, BLOCKS), 0:1] * dot(d_low, rows_u[...], TN)
        return (LOGIT_SCALE * total).reshape(NY, SHARE, WIDTH)

    steps = (2, 1, 3, 0)
    passed = []

    def away(place):
        col_away[place] = column_terms(1 - c, h_at(steps[place]))
        passed.extend(over_c(col_away.at[place], col_recv.at[place]))

    away(0)
    away(1)

    for tile in range(WIDTH // TILE):
        span = slice(tile * TILE, (tile + 1) * TILE)
        u_piece = cols[:, :, :, 0, :, span].reshape(COLS, TILE)
        t_piece = cols[:, :, :, 1, :, span].reshape(COLS, TILE)
        total = dot(tdsc[...], u_piece) + dot(dsc[...], t_piece) - row_slope * dot(dsc[...], u_piece)
        row_part[:, :, :, span] = (LOGIT_SCALE * total).reshape(NL, NX, SHARE, TILE)
    x_copies = over_x(lambda k: row_part.at[:, k], lambda q: x_recv.at[q - 1])

    y_copies = []
    for place, step in enumerate(steps):
        terms = column_terms(c, h_at(step))
        passed[place].wait_recv()
        terms = terms + col_recv[place]
        col_low[place] = terms.astype(BF16)
        col_part[place] = terms
        y_copies.append(over_y(lambda r: col_low.at[place, r], lambda q: y_recv.at[place, q - 1]))
        if place + 2 < NH:
            away(place + 2)

    arrive(plane_copies)
    z_grad[pl.ds(zh, 1)] = sum_slots(plane_grad, NC * NY)[None]
    z_grad_copies = spread_h(z_grad)

    def column_sum(place):
        arrive(y_copies[place])
        return functools.reduce(jnp.add, [y_recv[place, q].astype(F32) for q in range(NY - 1)], col_part[place, y])

    def column_high(place):
        step = steps[place]
        col_part[place, y] = column_sum(place)
        return [send(col_part.at[place, y], z_recv.at[step - 1], device(high=h_at(step)))]

    high_copies = column_high(0)
    high_copies += column_high(1)
    high_copies += column_high(2)
    arrive(x_copies)
    for low in range(NL):
        row_part[low, x] += x_recv[0, low] + x_recv[1, low] + x_recv[2, low]
    l_copies = over_l(row_part.at[1 - zl, x], l_recv)
    arrive(grad_copies)
    grad_rows[...] = unpack_lanes(sum_slots(grad_slots, NM))

    def finish(raw, tangent, value, terms):
        unit, inverse = unit_of(raw)
        turned, _ = turn_of(tangent, unit, inverse)
        mixed = terms[:, 1:2] + jnp.sum(unit * value, -1, keepdims=True)
        return ((value - turned * terms[:, 0:1] - unit * mixed) * inverse).astype(BF16)

    def spread_tdz(tower):
        block = tdz.at[tower, mp]
        return over_m(lambda m: block, lambda q: block)

    arrive(l_copies)
    tdz[0, mp] = finish(rawbuf[own], tanbuf[own], row_part[zl, x] + l_recv[...], grad_rows[own])
    sar_copies = spread_tdz(0)
    arrive(z_grad_copies)
    grad_cols[...] = unpack_lanes(unfold(sum_slots(z_grad, NH), 2))
    own_sum = column_sum(3)
    arrive(high_copies)
    tdz[1, mp] = finish(
        rawbuf[ROWS : ROWS + SHARE],
        tanbuf[ROWS : ROWS + SHARE],
        own_sum + z_recv[0] + z_recv[1] + z_recv[2],
        grad_cols[pl.ds(first_col, SHARE)],
    )
    optical_copies = spread_tdz(1)

    lanes = pl.ds(pl.multiple_of(c * WIDE, 128), WIDE)
    block_rows = pl.ds(pl.multiple_of(y * BLOCK, BLOCK), BLOCK)

    def hess_terms(tower):
        part = dot(feats[tower, :, pl.ds(pl.multiple_of(mp * PART, PART), PART)], tdz[tower].reshape(ROWS, WIDTH), TN)
        for half in range(2):
            part_hess[tower, half] = part[:, half * WIDE : (half + 1) * WIDE].reshape(NY, BLOCK, WIDE)
        return over_c(part_hess.at[tower, 1 - c], core_hess.at[tower])

    def hess_rows(tower, copies):
        arrive(copies)
        part_hess[tower, c] += core_hess[tower]
        return over_y(lambda r: part_hess.at[tower, c, r], lambda q: y_hess.at[tower, q - 1])

    def hess_high(tower, copies):
        arrive(copies)
        z_hess[tower, zh] = part_hess[tower, c, y] + y_hess[tower, 0] + y_hess[tower, 1] + y_hess[tower, 2]
        block = z_hess.at[tower, zh]
        return over_h(lambda h: block, lambda q: block)

    def hess_sum(tower, copies):
        arrive(copies)
        hess[tower, c, block_rows] = functools.reduce(jnp.add, [z_hess[tower, k] for k in range(NH)])

    def hess_back(tower):
        block = hess.at[tower, c, block_rows]
        return over_c(block, block), over_y(lambda r: block, lambda q: block)

    def hess_pass(tower, copies):
        passed = []
        for q, copy in enumerate(copies, 1):
            copy.wait_recv()
            row = (y + NY - q) % NY
            block = hess.at[tower, c, pl.ds(pl.multiple_of(row * BLOCK, BLOCK), BLOCK)]
            passed += over_c(block, block)
        return passed

    def hess_inner(tower):
        old = resid[tower, block_rows, lanes]
        along = direc[tower, block_rows, lanes]
        new = hess[tower, c, block_rows] + DAMPING * along
        return [jnp.sum(along * new), jnp.sum(old * new), jnp.sum(new * new)]

    arrive(sar_copies)
    core_first = hess_terms(0)
    row_first = hess_rows(0, core_first)
    arrive(optical_copies)
    core_second = hess_terms(1)
    high_first = hess_high(0, row_first)
    row_second = hess_rows(1, core_second)
    high_second = hess_high(1, row_second)
    hess_sum(0, high_first)
    passed, back_first = hess_back(0)
    inner = hess_inner(0)
    hess_sum(1, high_second)
    inner = [first + second for first, second in zip(inner, hess_inner(1))]
    place = lax.broadcasted_iota(jnp.int32, (1, 8, 128), 1)
    norm_p[pl.ds(c * NY + y, 1)] = jnp.where(place == 0, inner[0], jnp.where(place == 1, inner[1], inner[2]))
    scal_copies = over_plane(norm_p)
    more, back_second = hess_back(1)
    passed += more
    passed += hess_pass(0, back_first)
    arrive(scal_copies)
    norm_m[pl.ds(mp, 1)] = sum_slots(norm_p, NC * NY)[None]
    scal_copies = spread_m(norm_m)
    passed += hess_pass(1, back_second)
    arrive(passed)
    stores = []
    for tower in range(2):
        for half in range(2):
            target = hess_out.at[tower * PART : (tower + 1) * PART, half * WIDE : (half + 1) * WIDE]
            stores.append(load(hess.at[tower, half], target, 7 + 2 * tower + half))
    arrive(scal_copies)
    sums = sum_slots(norm_m, NM)
    alpha = norm_old / sums[0:1, 0:1]
    norm_new = norm_old - 2.0 * alpha * sums[1:2, 0:1] + alpha * alpha * sums[2:3, 0:1]
    first_row = lax.broadcasted_iota(jnp.int32, (8, WIDTH), 0) == 0
    info[...] = jnp.where(first_row, alpha, norm_new / norm_old)
    stores.append(load(info, hess_out.at[2 * PART : 2 * PART + 8], 11))
    for store in stores:
        store.wait()
    for copy in pending:
        copy.wait_send()
    assert counter[0] <= SEMS


def last_kernel(hess, direc, resid, solu, out_sol, out_res, out_dir, sol, res, way, store_sem):
    alpha, beta = hess[2 * PART : 2 * PART + 1, 0:1], hess[2 * PART + 1 : 2 * PART + 2, 0:1]
    stores = []

    def store(source, target, tower):
        copy = pltpu.make_async_copy(source.at[tower], target.at[tower], store_sem.at[len(stores)])
        copy.start()
        stores.append(copy)

    for tower in range(2):
        direction = direc[tower]
        sol[tower] = solu[tower] + alpha * direction
        store(sol, out_sol, tower)
        part = hess[tower * PART : (tower + 1) * PART]
        after = resid[tower] - alpha * (part + DAMPING * direction)
        res[tower] = after
        store(res, out_res, tower)
        way[tower] = after + beta * direction
        store(way, out_dir, tower)
    for copy in stores:
        copy.wait()


def body(features, projections, solution, residual, direction):
    vmem = pl.BlockSpec(memory_space=pltpu.VMEM)
    hbm = pl.BlockSpec(memory_space=pltpu.HBM)
    f32 = lambda *size: pltpu.VMEM(size, F32)
    bf16 = lambda *size: pltpu.VMEM(size, BF16)
    scratch = [
        bf16(2, ROWS, DEPTH), f32(2, PART, WIDTH), f32(2, PART, WIDTH),
        bf16(2, 2, 2, NM, PART, WIDE), bf16(2, 2, NY, NM - 1, QUARTER, WIDE),
        f32(ROWS + SHARE, WIDTH), f32(ROWS + SHARE, WIDTH),
        bf16(ROWS, WIDTH), bf16(ROWS, WIDTH),
        bf16(NC, NH, NY, 2, SHARE, WIDTH),
        f32(ROWS, COLS), f32(ROWS, COLS), f32(ROWS, COLS),
        bf16(ROWS, COLS), bf16(ROWS, COLS), f32(COLS, 128),
        f32(NM, 8, ROWS), f32(NC * NY, 8, COLS // 2), f32(NH, 8, COLS // 2),
        f32(NM, 8, ROWS), f32(NC * NY, 8, COLS // 4), f32(NH, 8, COLS // 4),
        f32(NL, NX, SHARE, WIDTH), f32(NX - 1, NL, SHARE, WIDTH), f32(SHARE, WIDTH),
        f32(NH, NY, SHARE, WIDTH), f32(NH, NY, SHARE, WIDTH), bf16(NH, NY, SHARE, WIDTH),
        f32(NH, NY, SHARE, WIDTH), bf16(NH, NY - 1, SHARE, WIDTH), f32(NH - 1, SHARE, WIDTH),
        f32(COLS, 128), f32(ROWS, 128),
        bf16(2, NM, SHARE, WIDTH),
        f32(2, 2, NY, BLOCK, WIDE), f32(2, NY, BLOCK, WIDE),
        f32(2, NY - 1, BLOCK, WIDE), f32(2, NH, BLOCK, WIDE), f32(2, 2, PART, WIDE),
        f32(NC * NY, 8, 128), f32(NM, 8, 128), f32(8, WIDTH),
        pltpu.SemaphoreType.DMA((SEMS,)), pltpu.SemaphoreType.DMA((SEMS,)), pltpu.SemaphoreType.DMA((16,)),
    ]
    hess = pl.pallas_call(
        kernel,
        name="cg_step",
        out_shape=jax.ShapeDtypeStruct((2 * PART + 8, WIDTH), F32),
        in_specs=[hbm] * 4,
        out_specs=pl.BlockSpec(memory_space=pl.ANY),
        scratch_shapes=scratch,
        compiler_params=pltpu.CompilerParams(
            collective_id=0, has_side_effects=True, vmem_limit_bytes=58 * 2**20
        ),
    )(features, projections, direction, residual)
    shape = jax.ShapeDtypeStruct(direction.shape, F32)
    return pl.pallas_call(
        last_kernel,
        name="updates",
        out_shape=(shape, shape, shape),
        in_specs=[vmem] * 4,
        out_specs=(hbm, hbm, hbm),
        scratch_shapes=[f32(2, PART, WIDTH)] * 3 + [pltpu.SemaphoreType.DMA((6,))],
        compiler_params=pltpu.CompilerParams(vmem_limit_bytes=16 * 2**20),
    )(hess, direction, residual, solution)


def solution(mesh):
    placed = (
        P(None, "dp", None),
        P(None, "mp", None),
        P(None, "mp", None),
        P(None, "mp", None),
        P(None, "mp", None),
    )
    return jax.shard_map(
        body,
        mesh=mesh,
        in_specs=placed,
        out_specs=(P(None, "mp", None), P(None, "mp", None), P(None, "mp", None)),
        check_vma=False,
    )
```

```python
import functools

import jax
import jax.numpy as jnp
from jax import lax
from jax.experimental import pallas as pl
from jax.experimental.pallas import tpu as pltpu
from jax.sharding import PartitionSpec as P

LOGIT_SCALE = 100.0
DAMPING = 1.0
EPSILON = 1e-06

NC, NY, NH, NX, NL = 2, 4, 4, 4, 2
NM = NX * NL
ROWS, DEPTH, WIDTH = 256, 1024, 768
PART = DEPTH // NM
SHARE = ROWS // NM
COLS = SHARE * NY * NH
BOTH = NC * ROWS
PAIRS = ROWS * NC * NY * NH
TILE = 256
SEMS = 288
QUARTER = 16
DIRECT = PART - NY * QUARTER
BLOCK = PART // NY
BLOCKS = SHARE * NY
WIDE = WIDTH // 2
F32, BF16 = jnp.float32, jnp.bfloat16
MESH = pl.DeviceIdType.MESH


def dot(left, right, dims=((1,), (0,))):
    return lax.dot_general(left, right, (dims, ((), ())), preferred_element_type=F32)


def unit_of(raw):
    inverse = lax.rsqrt(jnp.sum(raw * raw, -1, keepdims=True) + EPSILON)
    return raw * inverse, inverse


def turn_of(tangent, unit, inverse):
    along = jnp.sum(unit * tangent, -1, keepdims=True)
    return (tangent - unit * along) * inverse, along


def pack_lanes(columns):
    size = columns[0].shape[0]
    lane = lax.broadcasted_iota(jnp.int32, (size, 128), 1)
    wide = jnp.zeros((size, 128), F32)
    for place, column in enumerate(columns):
        wide = jnp.where(lane == place, column, wide)
    return wide.T[0:8]


def unpack_lanes(rows):
    return jnp.concatenate([rows, jnp.zeros((128 - rows.shape[0], rows.shape[1]), F32)], 0).T


def fold(rows):
    size = rows[0].shape[1] * len(rows) // 8
    stacked = jnp.concatenate(rows, 0)
    return jnp.concatenate([stacked[:, k : k + size] for k in range(0, stacked.shape[1], size)], 0)


def unfold(block, count):
    return jnp.concatenate([block[k : k + count] for k in range(0, 8, count)], 1)


def softmax_join(slots):
    top = functools.reduce(jnp.maximum, [slot[0] for slot in slots])
    total = 0.0
    weighted = 0.0
    for slot in slots:
        factor = jnp.exp(slot[0] - top)
        total = total + factor * slot[1]
        weighted = weighted + factor * slot[2]
    return top, total, weighted


def kernel(
    feats_in, proj_in, direc_in, resid_in,
    hess_out,
    feats, direc, resid, weights, quarters, rawbuf, tanbuf, rows_u, rows_t, cols,
    scores, left_ts, right_ts, dsc, tdsc, cvec, row_info,
    core_rows, row_slots, y_stat, z_stat,
    core_grad, grad_slots, y_grad, z_grad,
    row_part, row_away, row_got, x_recv, l_recv, col_part, col_low, y_recv, z_recv,
    grad_cols, grad_rows, tdz, part_hess, core_hess, y_hess, z_hess, hess,
    norm_p, norm_m, info,
    send_sem, recv_sem, load_sem,
):
    dp, mp = lax.axis_index("dp"), lax.axis_index("mp")
    c, y, zh = dp % NC, (dp // NC) % NY, dp // (NC * NY)
    x, zl = mp % NX, mp // NX
    partner = (1 - zl) * NX + x
    counter = [0]

    def device(core=None, row=None, high=None, model=None):
        core, row, high = c if core is None else core, y if row is None else row, zh if high is None else high
        return {"dp": (high * NY + row) * NC + core, "mp": mp if model is None else model}

    def m_at(step):
        return ((zl + step // NX) % NL) * NX + (x + step % NX) % NX

    def m_from(step):
        return ((zl + step // NX) % NL) * NX + (x + NX - step % NX) % NX

    def x_at(step):
        return (x + step) % NX

    def y_at(step):
        return (y + step) % NY

    def h_at(step):
        return (zh + step) % NH

    def send(source, target, where):
        place = counter[0]
        counter[0] += 1
        copy = pltpu.make_async_remote_copy(
            src_ref=source, dst_ref=target, send_sem=send_sem.at[place], recv_sem=recv_sem.at[place],
            device_id=where, device_id_type=MESH,
        )
        copy.start()
        pending.append(copy)
        return copy

    pending = []

    def arrive(copies):
        for copy in copies:
            copy.wait_recv()

    def over_m(source, target):
        return [send(source(m_at(q)), target(q), device(model=m_at(q))) for q in range(1, NM)]

    def over_y(source, target):
        return [send(source(y_at(q)), target(q), device(row=y_at(q))) for q in range(1, NY)]

    def over_h(source, target):
        copies = {q: send(source(h_at(q)), target(q), device(high=h_at(q))) for q in (2, 1, 3)}
        return [copies[q] for q in range(1, NH)]

    def over_x(source, target):
        return [send(source(x_at(q)), target(q), device(model=zl * NX + x_at(q))) for q in range(1, NX)]

    def over_l(source, target):
        return [send(source, target, device(model=partner))]

    def over_plane(slots):
        place = slots.at[c * NY + y]
        return [
            send(place, place, device(core=(c + q // NY) % NC, row=(y + q % NY) % NY)) for q in range(1, NC * NY)
        ]

    def over_c(source, target):
        return [send(source, target, device(core=1 - c))]

    def load(source, target, place):
        copy = pltpu.make_async_copy(source, target, load_sem.at[place])
        copy.start()
        return copy

    barrier = pltpu.get_barrier_semaphore()
    for q in (2, 1, 3):
        pl.semaphore_signal(barrier, inc=1, device_id=device(high=h_at(q)), device_id_type=MESH)
    for q in range(1, NM):
        pl.semaphore_signal(barrier, inc=1, device_id=device(model=m_at(q)), device_id_type=MESH)
    for q in range(1, NC * NY):
        where = device(core=(c + q // NY) % NC, row=(y + q % NY) % NY)
        pl.semaphore_signal(barrier, inc=1, device_id=where, device_id_type=MESH)
    load_direc = [load(direc_in.at[tower], direc.at[tower], tower) for tower in (1, 0)]
    load_proj = [
        [
            load(
                proj_in.at[tower, :, half * WIDE : (half + 1) * WIDE],
                weights.at[0, tower, half, mp],
                12 + 2 * tower + half,
            )
            for half in range(2)
        ]
        for tower in (1, 0)
    ]
    load_feats = [load(feats_in.at[tower], feats.at[tower], 4 + tower) for tower in (1, 0)]
    load_resid = load(resid_in, resid, 6)
    def own_direction(tower):
        for half in range(2):
            piece = direc[tower, :, half * WIDE : (half + 1) * WIDE].astype(BF16)
            weights[1, tower, half, pl.ds(mp, 1)] = piece[None]

    for copy in load_proj[0]:
        copy.wait()
    load_direc[0].wait()
    own_direction(1)
    pl.semaphore_wait(barrier, NM + NC * NY + NH - 3)

    def optical(kind):
        return lambda m: weights.at[kind, 1, c, m, pl.ds(0, DIRECT)]

    def sar(kind):
        return lambda m: weights.at[kind, 0, c, m]

    def spread_x(block):
        return over_x(lambda m: block, lambda q: block)

    def pass_on(blocks, low, copies):
        passed = []
        for q, copy in enumerate(copies, 1):
            copy.wait_recv()
            block = blocks(low * NX + (x + NX - q) % NX)
            passed += over_c(block, block)
        return passed

    def quarter_start(kind):
        part = weights.at[kind, 1, c, mp, pl.ds(pl.multiple_of(DIRECT + y * QUARTER, QUARTER), QUARTER)]
        return over_m(lambda m: part, lambda q: quarters.at[kind, c, y, q - 1])

    def quarter_rows(kind, copies):
        arrive(copies)
        block = quarters.at[kind, c, y]
        return over_c(block, block), over_y(lambda r: block, lambda q: block)

    def quarter_pass(kind, copies):
        passed = []
        for q, copy in enumerate(copies, 1):
            copy.wait_recv()
            block = quarters.at[kind, c, (y + NY - q) % NY]
            passed += over_c(block, block)
        return passed

    def over_z(blocks):
        return over_l(blocks(mp), blocks(mp))

    def relay(blocks, copies):
        arrive(copies)
        block = blocks(partner)
        return spread_x(block), over_c(block, block)

    def assemble(kind):
        for half in range(2):
            for q in range(1, NM):
                for r in range(NY):
                    rows = slice(DIRECT + r * QUARTER, DIRECT + (r + 1) * QUARTER)
                    weights[kind, 1, half, m_from(q), rows] = quarters[kind, half, r, q - 1]

    def embed(kind, tower, rows, into, first):
        for half in range(2):
            span = slice(half * WIDE, (half + 1) * WIDE)
            total = 0.0
            for block in range(0, NM, 2):
                deep = slice(block * PART, (block + 2) * PART)
                piece = weights[kind, tower, half, block : block + 2].reshape(2 * PART, WIDE)
                total += dot(feats[tower, rows, deep], piece)
            into[first : first + total.shape[0], span] = total

    def column_block(kind, high, row):
        return cols.at[high, row, kind]

    def column_rows(kind, high):
        block = column_block(kind, high, y)
        col_copies.extend(over_y(lambda r: block, lambda q: block))

    def column_start(kind):
        block = column_block(kind, zh, y)
        copies = over_h(lambda h: block, lambda q: block)
        column_rows(kind, zh)
        return copies

    def column_relay(kind, copies, q):
        copies[q - 1].wait_recv()
        column_rows(kind, (zh + NH - q) % NH)

    col_copies = []
    quarter_copies = quarter_start(0)
    z_copies = over_z(optical(0))
    x_copies = spread_x(optical(0)(mp))
    for copy in load_proj[1]:
        copy.wait()
    load_direc[1].wait()
    own_direction(0)
    passed_first, quarter_copies = quarter_rows(0, quarter_copies)
    quarter_second = quarter_start(1)
    z_second = over_z(optical(1))
    x_second = spread_x(optical(1)(mp))
    relays, passed = relay(optical(0), z_copies)
    passed_first += passed
    sar_z = [over_z(sar(kind)) for kind in range(2)]
    passed_first += pass_on(optical(0), zl, x_copies)
    passed_second, quarter_second = quarter_rows(1, quarter_second)
    passed_first += quarter_pass(0, quarter_copies)
    passed_first += pass_on(optical(0), 1 - zl, relays)
    relays_second, passed = relay(optical(1), z_second)
    passed_second += passed
    sar_x = spread_x(sar(0)(mp))
    load_feats[0].wait()
    arrive(passed_first)
    assemble(0)
    own = pl.ds(pl.multiple_of(mp * SHARE, SHARE), SHARE)
    share = slice(ROWS, ROWS + SHARE)
    embed(0, 1, own, rawbuf, ROWS)
    unit, inverse = unit_of(rawbuf[share])
    cols[zh, y, 0] = unit.astype(BF16)
    high_u = column_start(0)
    passed_second += pass_on(optical(1), zl, x_second)
    passed_second += quarter_pass(1, quarter_second)
    passed_second += pass_on(optical(1), 1 - zl, relays_second)
    sar_relays, sar_passed = relay(sar(0), sar_z[0])
    arrive(passed_second)
    assemble(1)
    embed(1, 1, own, tanbuf, ROWS)
    unit, inverse = unit_of(rawbuf[share])
    turned, along = turn_of(tanbuf[share], unit, inverse)
    cols[zh, y, 1] = turned.astype(BF16)
    slope = inverse * along
    high_t = column_start(1)
    sar_x_second = spread_x(sar(1)(mp))
    sar_relays_second, sar_passed_second = relay(sar(1), sar_z[1])
    column_relay(0, high_u, 1)
    column_relay(0, high_u, 3)
    column_relay(0, high_u, 2)
    first_col = pl.multiple_of((zh * NY + y) * SHARE, SHARE)
    cvec[...] = jnp.zeros_like(cvec)
    cvec[pl.ds(first_col, SHARE)] = jnp.broadcast_to(slope, (SHARE, 128))
    slope_row = cvec[...].T[0:1]
    column_relay(1, high_t, 1)
    column_relay(1, high_t, 3)
    sar_passed += pass_on(sar(0), zl, sar_x)
    sar_passed += pass_on(sar(0), 1 - zl, sar_relays)
    column_relay(1, high_t, 2)
    load_feats[1].wait()
    arrive(sar_passed)
    every = slice(0, ROWS)
    embed(0, 0, every, rawbuf, 0)
    unit, inverse = unit_of(rawbuf[every])
    rows_u[c] = unit.astype(BF16)
    unit_copies = over_c(rows_u.at[c], rows_u.at[c])
    sar_passed_second += pass_on(sar(1), zl, sar_x_second)
    sar_passed_second += pass_on(sar(1), 1 - zl, sar_relays_second)
    arrive(sar_passed_second)
    embed(1, 0, every, tanbuf, 0)
    unit, inverse = unit_of(rawbuf[every])
    turned, along = turn_of(tanbuf[every], unit, inverse)
    rows_t[c] = turned.astype(BF16)
    turned_copies = over_c(rows_t.at[c], rows_t.at[c])
    row_slope = inverse * along
    row_slope = jnp.concatenate([jnp.where(c == core, row_slope, 0.0) for core in range(NC)], 0)

    NT = ((1,), (1,))
    tiles = COLS // TILE
    arrive(unit_copies)
    arrive(col_copies)

    def score_tile(target, rows, kind, tile):
        piece = cols[2 * tile : 2 * tile + 2, :, kind].reshape(TILE, WIDTH)
        product = dot(rows[...].reshape(BOTH, WIDTH), piece, NT)
        target[:, tile * TILE : (tile + 1) * TILE] = LOGIT_SCALE * product

    for tile in range(tiles):
        score_tile(scores, rows_u, 0, tile)
        score_tile(right_ts, rows_u, 1, tile)
    row_max = jnp.max(scores[...], 1, keepdims=True)
    col_max = jnp.max(scores[...], 0, keepdims=True)
    arrive(turned_copies)
    for tile in range(tiles):
        score_tile(left_ts, rows_t, 0, tile)

    row_sum = jnp.zeros((BOTH, 1), F32)
    row_weighted = jnp.zeros((BOTH, 1), F32)
    col_sum, col_weighted = [], []
    for tile in range(tiles):
        span = slice(tile * TILE, (tile + 1) * TILE)
        score = scores[:, span]
        tscore = left_ts[:, span] + right_ts[:, span]
        weight = jnp.exp(score - row_max)
        row_sum += jnp.sum(weight, 1, keepdims=True)
        row_weighted += jnp.sum(weight * tscore, 1, keepdims=True)
        weight = jnp.exp(score - col_max[:, span])
        col_sum.append(jnp.sum(weight, 0, keepdims=True))
        col_weighted.append(jnp.sum(weight * tscore, 0, keepdims=True))
    load_resid.wait()
    resid_norm = jnp.sum(resid[...] * resid[...])
    core_rows[pl.ds(c, 1)] = pack_lanes(
        [row_max, row_sum, row_weighted, row_slope, jnp.full((BOTH, 1), resid_norm, F32)]
    )[None]
    y_stat[pl.ds(y, 1)] = fold(
        [col_max, jnp.concatenate(col_sum, 1), jnp.concatenate(col_weighted, 1), slope_row]
    )[None]

    def join_columns(slots, count):
        parts = [unfold(slots[k], 4) for k in range(count)]
        top, total, weighted = softmax_join([(part[0:1], part[1:2], part[2:3]) for part in parts])
        slopes = functools.reduce(jnp.add, [part[3:4] for part in parts])
        return top, total, weighted, slopes

    def sum_slots(slots, count):
        return functools.reduce(jnp.add, [slots[k] for k in range(count)])

    def spread_y(slots):
        return over_y(lambda r: slots.at[y], lambda q: slots.at[y])

    def spread_h(slots):
        return over_h(lambda h: slots.at[zh], lambda q: slots.at[zh])

    def spread_m(slots):
        return over_m(lambda m: slots.at[mp], lambda q: slots.at[mp])

    core_copies = over_c(core_rows.at[c], core_rows.at[c])
    copies = spread_y(y_stat)

    def join_rows(slots, count):
        parts = [slots[k] for k in range(count)]
        return softmax_join([(part[0:1], part[1:2], part[2:3]) for part in parts])

    arrive(core_copies)
    slopes = core_rows[0, 3:4] + core_rows[1, 3:4]
    joined = join_rows(core_rows, NC)
    row_slots[pl.ds(mp, 1)] = jnp.concatenate(
        [*joined, core_rows[0, 4:5], jnp.zeros((4, BOTH), F32)], 0
    )[None]
    row_copies = spread_m(row_slots)
    arrive(copies)
    z_stat[pl.ds(zh, 1)] = fold(join_columns(y_stat, NY))[None]
    copies = spread_h(z_stat)
    arrive(row_copies)
    top, total, weighted = join_rows(row_slots, NM)
    norm_old = functools.reduce(jnp.add, [row_slots[k, 3:4] for k in range(NM)])[0:1, 0:1]
    row_info[...] = unpack_lanes(jnp.concatenate([top + jnp.log(total), weighted / total, slopes], 0))
    row_lse, row_dot = row_info[:, 0:1], row_info[:, 1:2]
    arrive(copies)
    top, total, weighted, slopes = join_columns(z_stat, NH)
    col_lse, col_dot = top + jnp.log(total), weighted / total
    col_slope = unpack_lanes(slopes)

    row_ids = lax.broadcasted_iota(jnp.int32, (BOTH, TILE), 0)
    col_ids = lax.broadcasted_iota(jnp.int32, (BOTH, TILE), 1)
    offset = c * ROWS + mp * SHARE - first_col
    row_along = jnp.zeros((BOTH, 1), F32)
    row_turned = jnp.zeros((BOTH, 1), F32)
    col_along, col_turned = [], []
    for tile in range(tiles):
        span = slice(tile * TILE, (tile + 1) * TILE)
        score = scores[:, span]
        left, right = left_ts[:, span], right_ts[:, span]
        tscore = left + right
        row_w = jnp.exp(score - row_lse)
        col_w = jnp.exp(score - col_lse[:, span])
        place = col_ids + tile * TILE
        mine = (place >= first_col) & (place < first_col + SHARE) & (row_ids == place + offset)
        low = ((row_w + col_w - 2.0 * mine.astype(F32)) / (2.0 * PAIRS)).astype(BF16)
        dsc[:, span] = low
        tdsc[:, span] = (
            (row_w * (tscore - row_dot) + col_w * (tscore - col_dot[:, span])) / (2.0 * PAIRS)
        ).astype(BF16)
        wide = low.astype(F32)
        row_along += jnp.sum(wide * score, 1, keepdims=True)
        row_turned += jnp.sum(wide * left, 1, keepdims=True)
        col_along.append(jnp.sum(wide * score, 0, keepdims=True))
        col_turned.append(jnp.sum(wide * right, 0, keepdims=True))
    core_grad[pl.ds(c, 1)] = pack_lanes([row_along, row_turned])[None]
    y_grad[pl.ds(y, 1)] = fold([jnp.concatenate(col_along, 1), jnp.concatenate(col_turned, 1)])[None]
    core_copies = over_c(core_grad.at[c], core_grad.at[c])
    y_grad_copies = spread_y(y_grad)

    TN = ((0,), (0,))
    cvec[...] = col_slope

    def column_terms(high):
        start = pl.multiple_of(high * BLOCKS, BLOCKS)
        d_low, t_low = dsc[:, pl.ds(start, BLOCKS)], tdsc[:, pl.ds(start, BLOCKS)]
        units, turns = rows_u[...].reshape(BOTH, WIDTH), rows_t[...].reshape(BOTH, WIDTH)
        total = dot(t_low, units, TN) + dot(d_low, turns, TN)
        total -= cvec[pl.ds(start, BLOCKS), 0:1] * dot(d_low, units, TN)
        return (LOGIT_SCALE * total).reshape(NY, SHARE, WIDTH)

    def row_terms(core, into):
        here = pl.ds(pl.multiple_of(core * ROWS, ROWS), ROWS)
        d_low, t_low, slope = dsc[here], tdsc[here], row_info[here, 2:3]
        for tile in range(WIDTH // TILE):
            span = slice(tile * TILE, (tile + 1) * TILE)
            u_piece = cols[:, :, 0, :, span].reshape(COLS, TILE)
            t_piece = cols[:, :, 1, :, span].reshape(COLS, TILE)
            total = dot(t_low, u_piece) + dot(d_low, t_piece) - slope * dot(d_low, u_piece)
            into[:, :, :, span] = (LOGIT_SCALE * total).reshape(NL, NX, SHARE, TILE)

    steps = (2, 1, 3, 0)
    y_copies = []

    def column_out(place):
        terms = column_terms(h_at(steps[place]))
        col_low[place] = terms.astype(BF16)
        col_part[place] = terms
        y_copies.append(over_y(lambda r: col_low.at[place, r], lambda q: y_recv.at[place, q - 1]))

    column_out(0)
    row_terms(1 - c, row_away)
    away_copies = over_c(row_away, row_got)
    column_out(1)
    row_terms(c, row_part)
    arrive(away_copies)
    row_part[...] += row_got[...]
    x_copies = over_x(lambda k: row_part.at[:, k], lambda q: x_recv.at[q - 1])
    column_out(2)
    column_out(3)
    arrive(core_copies)
    grad_slots[pl.ds(mp, 1)] = sum_slots(core_grad, NC)[None]
    grad_copies = spread_m(grad_slots)
    arrive(y_grad_copies)
    z_grad[pl.ds(zh, 1)] = sum_slots(y_grad, NY)[None]
    z_grad_copies = spread_h(z_grad)

    def column_sum(place):
        arrive(y_copies[place])
        return functools.reduce(jnp.add, [y_recv[place, q].astype(F32) for q in range(NY - 1)], col_part[place, y])

    def column_high(place):
        step = steps[place]
        col_part[place, y] = column_sum(place)
        return [send(col_part.at[place, y], z_recv.at[step - 1], device(high=h_at(step)))]

    high_copies = column_high(0)
    high_copies += column_high(1)
    high_copies += column_high(2)
    arrive(x_copies)
    for low in range(NL):
        row_part[low, x] += x_recv[0, low] + x_recv[1, low] + x_recv[2, low]
    l_copies = over_l(row_part.at[1 - zl, x], l_recv)
    arrive(grad_copies)
    grad_rows[...] = unpack_lanes(sum_slots(grad_slots, NM))

    def finish(raw, tangent, value, terms):
        unit, inverse = unit_of(raw)
        turned, _ = turn_of(tangent, unit, inverse)
        mixed = terms[:, 1:2] + jnp.sum(unit * value, -1, keepdims=True)
        return ((value - turned * terms[:, 0:1] - unit * mixed) * inverse).astype(BF16)

    def spread_tdz(tower):
        block = tdz.at[tower, mp]
        return over_m(lambda m: block, lambda q: block)

    arrive(l_copies)
    mine = pl.ds(pl.multiple_of(c * ROWS + mp * SHARE, SHARE), SHARE)
    tdz[0, mp] = finish(rawbuf[own], tanbuf[own], row_part[zl, x] + l_recv[...], grad_rows[mine])
    sar_copies = spread_tdz(0)
    arrive(z_grad_copies)
    grad_cols[...] = unpack_lanes(unfold(sum_slots(z_grad, NH), 2))
    own_sum = column_sum(3)
    arrive(high_copies)
    tdz[1, mp] = finish(
        rawbuf[ROWS : ROWS + SHARE],
        tanbuf[ROWS : ROWS + SHARE],
        own_sum + z_recv[0] + z_recv[1] + z_recv[2],
        grad_cols[pl.ds(first_col, SHARE)],
    )
    optical_copies = spread_tdz(1)

    lanes = pl.ds(pl.multiple_of(c * WIDE, 128), WIDE)
    block_rows = pl.ds(pl.multiple_of(y * BLOCK, BLOCK), BLOCK)

    def hess_terms(tower):
        part = dot(feats[tower, :, pl.ds(pl.multiple_of(mp * PART, PART), PART)], tdz[tower].reshape(ROWS, WIDTH), TN)
        for half in range(2):
            part_hess[tower, half] = part[:, half * WIDE : (half + 1) * WIDE].reshape(NY, BLOCK, WIDE)
        return over_c(part_hess.at[tower, 1 - c], core_hess.at[tower])

    def hess_rows(tower, copies):
        arrive(copies)
        part_hess[tower, c] += core_hess[tower]
        return over_y(lambda r: part_hess.at[tower, c, r], lambda q: y_hess.at[tower, q - 1])

    def hess_high(tower, copies):
        arrive(copies)
        z_hess[tower, zh] = part_hess[tower, c, y] + y_hess[tower, 0] + y_hess[tower, 1] + y_hess[tower, 2]
        block = z_hess.at[tower, zh]
        return over_h(lambda h: block, lambda q: block)

    def hess_sum(tower, copies):
        arrive(copies)
        hess[tower, c, block_rows] = functools.reduce(jnp.add, [z_hess[tower, k] for k in range(NH)])

    def hess_back(tower):
        block = hess.at[tower, c, block_rows]
        return over_c(block, block), over_y(lambda r: block, lambda q: block)

    def hess_pass(tower, copies):
        passed = []
        for q, copy in enumerate(copies, 1):
            copy.wait_recv()
            row = (y + NY - q) % NY
            block = hess.at[tower, c, pl.ds(pl.multiple_of(row * BLOCK, BLOCK), BLOCK)]
            passed += over_c(block, block)
        return passed

    def hess_inner(tower):
        old = resid[tower, block_rows, lanes]
        along = direc[tower, block_rows, lanes]
        new = hess[tower, c, block_rows] + DAMPING * along
        return [jnp.sum(along * new), jnp.sum(old * new), jnp.sum(new * new)]

    arrive(sar_copies)
    core_first = hess_terms(0)
    row_first = hess_rows(0, core_first)
    arrive(optical_copies)
    core_second = hess_terms(1)
    high_first = hess_high(0, row_first)
    row_second = hess_rows(1, core_second)
    high_second = hess_high(1, row_second)
    hess_sum(0, high_first)
    passed, back_first = hess_back(0)
    inner = hess_inner(0)
    hess_sum(1, high_second)
    inner = [first + second for first, second in zip(inner, hess_inner(1))]
    place = lax.broadcasted_iota(jnp.int32, (1, 8, 128), 1)
    norm_p[pl.ds(c * NY + y, 1)] = jnp.where(place == 0, inner[0], jnp.where(place == 1, inner[1], inner[2]))
    scal_copies = over_plane(norm_p)
    more, back_second = hess_back(1)
    passed += more
    passed += hess_pass(0, back_first)
    arrive(scal_copies)
    norm_m[pl.ds(mp, 1)] = sum_slots(norm_p, NC * NY)[None]
    scal_copies = spread_m(norm_m)
    passed += hess_pass(1, back_second)
    arrive(passed)
    stores = []
    for tower in range(2):
        for half in range(2):
            target = hess_out.at[tower * PART : (tower + 1) * PART, half * WIDE : (half + 1) * WIDE]
            stores.append(load(hess.at[tower, half], target, 7 + 2 * tower + half))
    arrive(scal_copies)
    sums = sum_slots(norm_m, NM)
    alpha = norm_old / sums[0:1, 0:1]
    norm_new = norm_old - 2.0 * alpha * sums[1:2, 0:1] + alpha * alpha * sums[2:3, 0:1]
    first_row = lax.broadcasted_iota(jnp.int32, (8, WIDTH), 0) == 0
    info[...] = jnp.where(first_row, alpha, norm_new / norm_old)
    stores.append(load(info, hess_out.at[2 * PART : 2 * PART + 8], 11))
    for store in stores:
        store.wait()
    for copy in pending:
        copy.wait_send()
    assert counter[0] <= SEMS


def last_kernel(hess, direc, resid, solu, out_sol, out_res, out_dir, sol, res, way, store_sem):
    alpha, beta = hess[2 * PART : 2 * PART + 1, 0:1], hess[2 * PART + 1 : 2 * PART + 2, 0:1]
    stores = []

    def store(source, target, tower):
        copy = pltpu.make_async_copy(source.at[tower], target.at[tower], store_sem.at[len(stores)])
        copy.start()
        stores.append(copy)

    for tower in range(2):
        direction = direc[tower]
        sol[tower] = solu[tower] + alpha * direction
        store(sol, out_sol, tower)
        part = hess[tower * PART : (tower + 1) * PART]
        after = resid[tower] - alpha * (part + DAMPING * direction)
        res[tower] = after
        store(res, out_res, tower)
        way[tower] = after + beta * direction
        store(way, out_dir, tower)
    for copy in stores:
        copy.wait()


def body(features, projections, solution, residual, direction):
    vmem = pl.BlockSpec(memory_space=pltpu.VMEM)
    hbm = pl.BlockSpec(memory_space=pltpu.HBM)
    f32 = lambda *size: pltpu.VMEM(size, F32)
    bf16 = lambda *size: pltpu.VMEM(size, BF16)
    scratch = [
        bf16(2, ROWS, DEPTH), f32(2, PART, WIDTH), f32(2, PART, WIDTH),
        bf16(2, 2, 2, NM, PART, WIDE), bf16(2, 2, NY, NM - 1, QUARTER, WIDE),
        f32(ROWS + SHARE, WIDTH), f32(ROWS + SHARE, WIDTH),
        bf16(NC, ROWS, WIDTH), bf16(NC, ROWS, WIDTH),
        bf16(NH, NY, 2, SHARE, WIDTH),
        f32(BOTH, COLS), f32(BOTH, COLS), f32(BOTH, COLS),
        bf16(BOTH, COLS), bf16(BOTH, COLS), f32(COLS, 128), f32(BOTH, 128),
        f32(NC, 8, BOTH), f32(NM, 8, BOTH), f32(NY, 8, COLS // 2), f32(NH, 8, COLS // 2),
        f32(NC, 8, BOTH), f32(NM, 8, BOTH), f32(NY, 8, COLS // 4), f32(NH, 8, COLS // 4),
        f32(NL, NX, SHARE, WIDTH), f32(NL, NX, SHARE, WIDTH), f32(NL, NX, SHARE, WIDTH),
        f32(NX - 1, NL, SHARE, WIDTH), f32(SHARE, WIDTH),
        f32(NH, NY, SHARE, WIDTH), bf16(NH, NY, SHARE, WIDTH),
        bf16(NH, NY - 1, SHARE, WIDTH), f32(NH - 1, SHARE, WIDTH),
        f32(COLS, 128), f32(BOTH, 128),
        bf16(2, NM, SHARE, WIDTH),
        f32(2, 2, NY, BLOCK, WIDE), f32(2, NY, BLOCK, WIDE),
        f32(2, NY - 1, BLOCK, WIDE), f32(2, NH, BLOCK, WIDE), f32(2, 2, PART, WIDE),
        f32(NC * NY, 8, 128), f32(NM, 8, 128), f32(8, WIDTH),
        pltpu.SemaphoreType.DMA((SEMS,)), pltpu.SemaphoreType.DMA((SEMS,)), pltpu.SemaphoreType.DMA((16,)),
    ]
    hess = pl.pallas_call(
        kernel,
        name="cg_step",
        out_shape=jax.ShapeDtypeStruct((2 * PART + 8, WIDTH), F32),
        in_specs=[hbm] * 4,
        out_specs=pl.BlockSpec(memory_space=pl.ANY),
        scratch_shapes=scratch,
        compiler_params=pltpu.CompilerParams(
            collective_id=0, has_side_effects=True, vmem_limit_bytes=58 * 2**20
        ),
    )(features, projections, direction, residual)
    shape = jax.ShapeDtypeStruct(direction.shape, F32)
    return pl.pallas_call(
        last_kernel,
        name="updates",
        out_shape=(shape, shape, shape),
        in_specs=[vmem] * 4,
        out_specs=(hbm, hbm, hbm),
        scratch_shapes=[f32(2, PART, WIDTH)] * 3 + [pltpu.SemaphoreType.DMA((6,))],
        compiler_params=pltpu.CompilerParams(vmem_limit_bytes=16 * 2**20),
    )(hess, direction, residual, solution)


def solution(mesh):
    placed = (
        P(None, "dp", None),
        P(None, "mp", None),
        P(None, "mp", None),
        P(None, "mp", None),
        P(None, "mp", None),
    )
    return jax.shard_map(
        body,
        mesh=mesh,
        in_specs=placed,
        out_specs=(P(None, "mp", None), P(None, "mp", None), P(None, "mp", None)),
        check_vma=False,
    )
```

```python
import functools

import jax
import jax.numpy as jnp
from jax import lax
from jax.experimental import pallas as pl
from jax.experimental.pallas import tpu as pltpu
from jax.sharding import PartitionSpec as P

LOGIT_SCALE = 100.0
DAMPING = 1.0
EPSILON = 1e-06

NC, NY, NH, NX, NL = 2, 4, 4, 4, 2
NM = NX * NL
ROWS, DEPTH, WIDTH = 256, 1024, 768
PART = DEPTH // NM
SHARE = ROWS // NM
COLS = SHARE * NY * NH
BOTH = NC * ROWS
PAIRS = ROWS * NC * NY * NH
TILE = 256
SEMS = 288
QUARTER = 16
DIRECT = PART - NY * QUARTER
BLOCK = PART // NY
BLOCKS = SHARE * NY
WIDE = WIDTH // 2
F32, BF16 = jnp.float32, jnp.bfloat16
MESH = pl.DeviceIdType.MESH


def dot(left, right, dims=((1,), (0,))):
    return lax.dot_general(left, right, (dims, ((), ())), preferred_element_type=F32)


def unit_of(raw):
    inverse = lax.rsqrt(jnp.sum(raw * raw, -1, keepdims=True) + EPSILON)
    return raw * inverse, inverse


def turn_of(tangent, unit, inverse):
    along = jnp.sum(unit * tangent, -1, keepdims=True)
    return (tangent - unit * along) * inverse, along


def pack_lanes(columns):
    size = columns[0].shape[0]
    lane = lax.broadcasted_iota(jnp.int32, (size, 128), 1)
    wide = jnp.zeros((size, 128), F32)
    for place, column in enumerate(columns):
        wide = jnp.where(lane == place, column, wide)
    return wide.T[0:8]


def unpack_lanes(rows):
    return jnp.concatenate([rows, jnp.zeros((128 - rows.shape[0], rows.shape[1]), F32)], 0).T


def fold(rows):
    size = rows[0].shape[1] * len(rows) // 8
    stacked = jnp.concatenate(rows, 0)
    return jnp.concatenate([stacked[:, k : k + size] for k in range(0, stacked.shape[1], size)], 0)


def unfold(block, count):
    return jnp.concatenate([block[k : k + count] for k in range(0, 8, count)], 1)


def softmax_join(slots):
    top = functools.reduce(jnp.maximum, [slot[0] for slot in slots])
    total = 0.0
    weighted = 0.0
    for slot in slots:
        factor = jnp.exp(slot[0] - top)
        total = total + factor * slot[1]
        weighted = weighted + factor * slot[2]
    return top, total, weighted


def kernel(
    feats_in, proj_in, direc_in, resid_in,
    hess_out,
    feats, direc, resid, weights, quarters, rawbuf, tanbuf, rows_u, rows_t, cols,
    scores, left_ts, right_ts, dsc, tdsc, cvec, row_info,
    core_rows, row_slots, y_stat, z_stat,
    core_grad, grad_slots, y_grad, z_grad,
    row_part, row_away, row_got, x_recv, l_recv, col_part, col_low, y_recv, z_recv,
    grad_cols, grad_rows, tdz, part_hess, core_hess, y_hess, z_hess, hess,
    norm_p, norm_m, info,
    send_sem, recv_sem, load_sem,
):
    dp, mp = lax.axis_index("dp"), lax.axis_index("mp")
    c, y, zh = dp % NC, (dp // NC) % NY, dp // (NC * NY)
    x, zl = mp % NX, mp // NX
    partner = (1 - zl) * NX + x
    counter = [0]

    def device(core=None, row=None, high=None, model=None):
        core, row, high = c if core is None else core, y if row is None else row, zh if high is None else high
        return {"dp": (high * NY + row) * NC + core, "mp": mp if model is None else model}

    def m_at(step):
        return ((zl + step // NX) % NL) * NX + (x + step % NX) % NX

    def m_from(step):
        return ((zl + step // NX) % NL) * NX + (x + NX - step % NX) % NX

    def x_at(step):
        return (x + step) % NX

    def y_at(step):
        return (y + step) % NY

    def h_at(step):
        return (zh + step) % NH

    def send(source, target, where):
        place = counter[0]
        counter[0] += 1
        copy = pltpu.make_async_remote_copy(
            src_ref=source, dst_ref=target, send_sem=send_sem.at[place], recv_sem=recv_sem.at[place],
            device_id=where, device_id_type=MESH,
        )
        copy.start()
        pending.append(copy)
        return copy

    pending = []

    def arrive(copies):
        for copy in copies:
            copy.wait_recv()

    def over_m(source, target):
        return [send(source(m_at(q)), target(q), device(model=m_at(q))) for q in range(1, NM)]

    def over_y(source, target):
        return [send(source(y_at(q)), target(q), device(row=y_at(q))) for q in range(1, NY)]

    def over_h(source, target):
        copies = {q: send(source(h_at(q)), target(q), device(high=h_at(q))) for q in (2, 1, 3)}
        return [copies[q] for q in range(1, NH)]

    def over_x(source, target):
        return [send(source(x_at(q)), target(q), device(model=zl * NX + x_at(q))) for q in range(1, NX)]

    def over_l(source, target):
        return [send(source, target, device(model=partner))]

    def over_plane(slots):
        place = slots.at[c * NY + y]
        return [
            send(place, place, device(core=(c + q // NY) % NC, row=(y + q % NY) % NY)) for q in range(1, NC * NY)
        ]

    def over_c(source, target):
        return [send(source, target, device(core=1 - c))]

    def load(source, target, place):
        copy = pltpu.make_async_copy(source, target, load_sem.at[place])
        copy.start()
        return copy

    barrier = pltpu.get_barrier_semaphore()
    for q in (2, 1, 3):
        pl.semaphore_signal(barrier, inc=1, device_id=device(high=h_at(q)), device_id_type=MESH)
    for q in range(1, NM):
        pl.semaphore_signal(barrier, inc=1, device_id=device(model=m_at(q)), device_id_type=MESH)
    for q in range(1, NC * NY):
        where = device(core=(c + q // NY) % NC, row=(y + q % NY) % NY)
        pl.semaphore_signal(barrier, inc=1, device_id=where, device_id_type=MESH)
    load_direc = [load(direc_in.at[tower], direc.at[tower], tower) for tower in (1, 0)]
    load_proj = [
        [
            load(
                proj_in.at[tower, :, half * WIDE : (half + 1) * WIDE],
                weights.at[0, tower, half, mp],
                12 + 2 * tower + half,
            )
            for half in range(2)
        ]
        for tower in (1, 0)
    ]
    load_feats = [load(feats_in.at[tower], feats.at[tower], 4 + tower) for tower in (1, 0)]
    load_resid = load(resid_in, resid, 6)
    def own_direction(tower):
        for half in range(2):
            piece = direc[tower, :, half * WIDE : (half + 1) * WIDE].astype(BF16)
            weights[1, tower, half, pl.ds(mp, 1)] = piece[None]

    for copy in load_proj[0]:
        copy.wait()
    load_direc[0].wait()
    own_direction(1)
    pl.semaphore_wait(barrier, NM + NC * NY + NH - 3)

    def optical(kind):
        return lambda m: weights.at[kind, 1, c, m, pl.ds(0, DIRECT)]

    def sar(kind):
        return lambda m: weights.at[kind, 0, c, m]

    def spread_x(block):
        return over_x(lambda m: block, lambda q: block)

    def pass_on(blocks, low, copies):
        passed = []
        for q, copy in enumerate(copies, 1):
            copy.wait_recv()
            block = blocks(low * NX + (x + NX - q) % NX)
            passed += over_c(block, block)
        return passed

    def quarter_start(kind):
        part = weights.at[kind, 1, c, mp, pl.ds(pl.multiple_of(DIRECT + y * QUARTER, QUARTER), QUARTER)]
        return over_m(lambda m: part, lambda q: quarters.at[kind, c, y, q - 1])

    def quarter_rows(kind, copies):
        arrive(copies)
        block = quarters.at[kind, c, y]
        return over_c(block, block), over_y(lambda r: block, lambda q: block)

    def quarter_pass(kind, copies):
        passed = []
        for q, copy in enumerate(copies, 1):
            copy.wait_recv()
            block = quarters.at[kind, c, (y + NY - q) % NY]
            passed += over_c(block, block)
        return passed

    def over_z(blocks):
        return over_l(blocks(mp), blocks(mp))

    def relay(blocks, copies):
        arrive(copies)
        block = blocks(partner)
        return spread_x(block), over_c(block, block)

    def assemble(kind):
        for half in range(2):
            for q in range(1, NM):
                for r in range(NY):
                    rows = slice(DIRECT + r * QUARTER, DIRECT + (r + 1) * QUARTER)
                    weights[kind, 1, half, m_from(q), rows] = quarters[kind, half, r, q - 1]

    def embed(kind, tower, rows, into, first):
        for half in range(2):
            span = slice(half * WIDE, (half + 1) * WIDE)
            total = 0.0
            for block in range(0, NM, 2):
                deep = slice(block * PART, (block + 2) * PART)
                piece = weights[kind, tower, half, block : block + 2].reshape(2 * PART, WIDE)
                total += dot(feats[tower, rows, deep], piece)
            into[first : first + total.shape[0], span] = total

    def column_block(kind, high, row):
        return cols.at[high, row, kind]

    def column_rows(kind, high):
        block = column_block(kind, high, y)
        col_copies.extend(over_y(lambda r: block, lambda q: block))

    def column_start(kind):
        block = column_block(kind, zh, y)
        copies = over_h(lambda h: block, lambda q: block)
        column_rows(kind, zh)
        return copies

    def column_relay(kind, copies, q):
        copies[q - 1].wait_recv()
        column_rows(kind, (zh + NH - q) % NH)

    col_copies = []
    quarter_copies = quarter_start(0)
    z_copies = over_z(optical(0))
    x_copies = spread_x(optical(0)(mp))
    quarter_second = quarter_start(1)
    z_second = over_z(optical(1))
    x_second = spread_x(optical(1)(mp))
    for copy in load_proj[1]:
        copy.wait()
    load_direc[1].wait()
    own_direction(0)
    sar_z = [over_z(sar(kind)) for kind in range(2)]
    passed_first, quarter_copies = quarter_rows(0, quarter_copies)
    relays, passed = relay(optical(0), z_copies)
    passed_first += passed
    passed_second, quarter_second = quarter_rows(1, quarter_second)
    relays_second, passed = relay(optical(1), z_second)
    passed_second += passed
    passed_first += pass_on(optical(0), zl, x_copies)
    sar_x = spread_x(sar(0)(mp))
    passed_first += quarter_pass(0, quarter_copies)
    passed_first += pass_on(optical(0), 1 - zl, relays)
    load_feats[0].wait()
    arrive(passed_first)
    assemble(0)
    own = pl.ds(pl.multiple_of(mp * SHARE, SHARE), SHARE)
    share = slice(ROWS, ROWS + SHARE)
    embed(0, 1, own, rawbuf, ROWS)
    unit, inverse = unit_of(rawbuf[share])
    cols[zh, y, 0] = unit.astype(BF16)
    high_u = column_start(0)
    passed_second += pass_on(optical(1), zl, x_second)
    sar_relays, sar_passed = relay(sar(0), sar_z[0])
    passed_second += quarter_pass(1, quarter_second)
    passed_second += pass_on(optical(1), 1 - zl, relays_second)
    sar_x_second = spread_x(sar(1)(mp))
    sar_relays_second, sar_passed_second = relay(sar(1), sar_z[1])
    arrive(passed_second)
    assemble(1)
    embed(1, 1, own, tanbuf, ROWS)
    unit, inverse = unit_of(rawbuf[share])
    turned, along = turn_of(tanbuf[share], unit, inverse)
    cols[zh, y, 1] = turned.astype(BF16)
    slope = inverse * along
    high_t = column_start(1)
    column_relay(0, high_u, 1)
    column_relay(0, high_u, 3)
    column_relay(0, high_u, 2)
    first_col = pl.multiple_of((zh * NY + y) * SHARE, SHARE)
    cvec[...] = jnp.zeros_like(cvec)
    cvec[pl.ds(first_col, SHARE)] = jnp.broadcast_to(slope, (SHARE, 128))
    slope_row = cvec[...].T[0:1]
    column_relay(1, high_t, 1)
    column_relay(1, high_t, 3)
    sar_passed += pass_on(sar(0), zl, sar_x)
    sar_passed += pass_on(sar(0), 1 - zl, sar_relays)
    column_relay(1, high_t, 2)
    load_feats[1].wait()
    arrive(sar_passed)
    every = slice(0, ROWS)
    embed(0, 0, every, rawbuf, 0)
    unit, inverse = unit_of(rawbuf[every])
    rows_u[c] = unit.astype(BF16)
    unit_copies = over_c(rows_u.at[c], rows_u.at[c])
    sar_passed_second += pass_on(sar(1), zl, sar_x_second)
    sar_passed_second += pass_on(sar(1), 1 - zl, sar_relays_second)
    arrive(sar_passed_second)
    embed(1, 0, every, tanbuf, 0)
    unit, inverse = unit_of(rawbuf[every])
    turned, along = turn_of(tanbuf[every], unit, inverse)
    rows_t[c] = turned.astype(BF16)
    turned_copies = over_c(rows_t.at[c], rows_t.at[c])
    row_slope = inverse * along
    row_slope = jnp.concatenate([jnp.where(c == core, row_slope, 0.0) for core in range(NC)], 0)

    NT = ((1,), (1,))
    tiles = COLS // TILE
    arrive(unit_copies)
    arrive(col_copies)

    def score_tile(target, rows, kind, tile):
        piece = cols[2 * tile : 2 * tile + 2, :, kind].reshape(TILE, WIDTH)
        product = dot(rows[...].reshape(BOTH, WIDTH), piece, NT)
        target[:, tile * TILE : (tile + 1) * TILE] = LOGIT_SCALE * product

    for tile in range(tiles):
        score_tile(scores, rows_u, 0, tile)
        score_tile(right_ts, rows_u, 1, tile)
    row_max = jnp.max(scores[...], 1, keepdims=True)
    col_max = jnp.max(scores[...], 0, keepdims=True)
    arrive(turned_copies)
    for tile in range(tiles):
        score_tile(left_ts, rows_t, 0, tile)

    row_sum = jnp.zeros((BOTH, 1), F32)
    row_weighted = jnp.zeros((BOTH, 1), F32)
    col_sum, col_weighted = [], []
    for tile in range(tiles):
        span = slice(tile * TILE, (tile + 1) * TILE)
        score = scores[:, span]
        tscore = left_ts[:, span] + right_ts[:, span]
        weight = jnp.exp(score - row_max)
        row_sum += jnp.sum(weight, 1, keepdims=True)
        row_weighted += jnp.sum(weight * tscore, 1, keepdims=True)
        weight = jnp.exp(score - col_max[:, span])
        col_sum.append(jnp.sum(weight, 0, keepdims=True))
        col_weighted.append(jnp.sum(weight * tscore, 0, keepdims=True))
    load_resid.wait()
    resid_norm = jnp.sum(resid[...] * resid[...])
    core_rows[pl.ds(c, 1)] = pack_lanes(
        [row_max, row_sum, row_weighted, row_slope, jnp.full((BOTH, 1), resid_norm, F32)]
    )[None]
    y_stat[pl.ds(y, 1)] = fold(
        [col_max, jnp.concatenate(col_sum, 1), jnp.concatenate(col_weighted, 1), slope_row]
    )[None]

    def join_columns(slots, count):
        parts = [unfold(slots[k], 4) for k in range(count)]
        top, total, weighted = softmax_join([(part[0:1], part[1:2], part[2:3]) for part in parts])
        slopes = functools.reduce(jnp.add, [part[3:4] for part in parts])
        return top, total, weighted, slopes

    def sum_slots(slots, count):
        return functools.reduce(jnp.add, [slots[k] for k in range(count)])

    def spread_y(slots):
        return over_y(lambda r: slots.at[y], lambda q: slots.at[y])

    def spread_h(slots):
        return over_h(lambda h: slots.at[zh], lambda q: slots.at[zh])

    def spread_m(slots):
        return over_m(lambda m: slots.at[mp], lambda q: slots.at[mp])

    core_copies = over_c(core_rows.at[c], core_rows.at[c])
    copies = spread_y(y_stat)

    def join_rows(slots, count):
        parts = [slots[k] for k in range(count)]
        return softmax_join([(part[0:1], part[1:2], part[2:3]) for part in parts])

    arrive(core_copies)
    slopes = core_rows[0, 3:4] + core_rows[1, 3:4]
    joined = join_rows(core_rows, NC)
    row_slots[pl.ds(mp, 1)] = jnp.concatenate(
        [*joined, core_rows[0, 4:5], jnp.zeros((4, BOTH), F32)], 0
    )[None]
    row_copies = spread_m(row_slots)
    arrive(copies)
    z_stat[pl.ds(zh, 1)] = fold(join_columns(y_stat, NY))[None]
    copies = spread_h(z_stat)
    arrive(row_copies)
    top, total, weighted = join_rows(row_slots, NM)
    norm_old = functools.reduce(jnp.add, [row_slots[k, 3:4] for k in range(NM)])[0:1, 0:1]
    row_info[...] = unpack_lanes(jnp.concatenate([top + jnp.log(total), weighted / total, slopes], 0))
    row_lse, row_dot = row_info[:, 0:1], row_info[:, 1:2]
    arrive(copies)
    top, total, weighted, slopes = join_columns(z_stat, NH)
    col_lse, col_dot = top + jnp.log(total), weighted / total
    col_slope = unpack_lanes(slopes)

    row_ids = lax.broadcasted_iota(jnp.int32, (BOTH, TILE), 0)
    col_ids = lax.broadcasted_iota(jnp.int32, (BOTH, TILE), 1)
    offset = c * ROWS + mp * SHARE - first_col
    row_along = jnp.zeros((BOTH, 1), F32)
    row_turned = jnp.zeros((BOTH, 1), F32)
    col_along, col_turned = [], []
    for tile in range(tiles):
        span = slice(tile * TILE, (tile + 1) * TILE)
        score = scores[:, span]
        left, right = left_ts[:, span], right_ts[:, span]
        tscore = left + right
        row_w = jnp.exp(score - row_lse)
        col_w = jnp.exp(score - col_lse[:, span])
        place = col_ids + tile * TILE
        mine = (place >= first_col) & (place < first_col + SHARE) & (row_ids == place + offset)
        low = ((row_w + col_w - 2.0 * mine.astype(F32)) / (2.0 * PAIRS)).astype(BF16)
        dsc[:, span] = low
        tdsc[:, span] = (
            (row_w * (tscore - row_dot) + col_w * (tscore - col_dot[:, span])) / (2.0 * PAIRS)
        ).astype(BF16)
        wide = low.astype(F32)
        row_along += jnp.sum(wide * score, 1, keepdims=True)
        row_turned += jnp.sum(wide * left, 1, keepdims=True)
        col_along.append(jnp.sum(wide * score, 0, keepdims=True))
        col_turned.append(jnp.sum(wide * right, 0, keepdims=True))
    core_grad[pl.ds(c, 1)] = pack_lanes([row_along, row_turned])[None]
    y_grad[pl.ds(y, 1)] = fold([jnp.concatenate(col_along, 1), jnp.concatenate(col_turned, 1)])[None]
    core_copies = over_c(core_grad.at[c], core_grad.at[c])
    y_grad_copies = spread_y(y_grad)

    TN = ((0,), (0,))
    cvec[...] = col_slope

    def column_terms(high):
        start = pl.multiple_of(high * BLOCKS, BLOCKS)
        d_low, t_low = dsc[:, pl.ds(start, BLOCKS)], tdsc[:, pl.ds(start, BLOCKS)]
        units, turns = rows_u[...].reshape(BOTH, WIDTH), rows_t[...].reshape(BOTH, WIDTH)
        total = dot(t_low, units, TN) + dot(d_low, turns, TN)
        total -= cvec[pl.ds(start, BLOCKS), 0:1] * dot(d_low, units, TN)
        return (LOGIT_SCALE * total).reshape(NY, SHARE, WIDTH)

    def row_terms(core, into):
        here = pl.ds(pl.multiple_of(core * ROWS, ROWS), ROWS)
        d_low, t_low, slope = dsc[here], tdsc[here], row_info[here, 2:3]
        for tile in range(WIDTH // TILE):
            span = slice(tile * TILE, (tile + 1) * TILE)
            u_piece = cols[:, :, 0, :, span].reshape(COLS, TILE)
            t_piece = cols[:, :, 1, :, span].reshape(COLS, TILE)
            total = dot(t_low, u_piece) + dot(d_low, t_piece) - slope * dot(d_low, u_piece)
            into[:, :, :, span] = (LOGIT_SCALE * total).reshape(NL, NX, SHARE, TILE)

    steps = (2, 1, 3, 0)
    y_copies = []

    def column_out(place):
        terms = column_terms(h_at(steps[place]))
        col_low[place] = terms.astype(BF16)
        col_part[place] = terms
        y_copies.append(over_y(lambda r: col_low.at[place, r], lambda q: y_recv.at[place, q - 1]))

    column_out(0)
    row_terms(1 - c, row_away)
    away_copies = over_c(row_away, row_got)
    column_out(1)
    arrive(core_copies)
    grad_slots[pl.ds(mp, 1)] = sum_slots(core_grad, NC)[None]
    grad_copies = spread_m(grad_slots)
    row_terms(c, row_part)
    arrive(away_copies)
    row_part[...] += row_got[...]
    x_copies = over_x(lambda k: row_part.at[:, k], lambda q: x_recv.at[q - 1])
    column_out(2)
    arrive(y_grad_copies)
    z_grad[pl.ds(zh, 1)] = sum_slots(y_grad, NY)[None]
    z_grad_copies = spread_h(z_grad)
    column_out(3)

    def column_sum(place):
        arrive(y_copies[place])
        return functools.reduce(jnp.add, [y_recv[place, q].astype(F32) for q in range(NY - 1)], col_part[place, y])

    def column_high(place):
        step = steps[place]
        col_part[place, y] = column_sum(place)
        return [send(col_part.at[place, y], z_recv.at[step - 1], device(high=h_at(step)))]

    high_copies = column_high(0)
    high_copies += column_high(1)
    high_copies += column_high(2)
    arrive(x_copies)
    for low in range(NL):
        row_part[low, x] += x_recv[0, low] + x_recv[1, low] + x_recv[2, low]
    l_copies = over_l(row_part.at[1 - zl, x], l_recv)
    arrive(grad_copies)
    grad_rows[...] = unpack_lanes(sum_slots(grad_slots, NM))

    def finish(raw, tangent, value, terms):
        unit, inverse = unit_of(raw)
        turned, _ = turn_of(tangent, unit, inverse)
        mixed = terms[:, 1:2] + jnp.sum(unit * value, -1, keepdims=True)
        return ((value - turned * terms[:, 0:1] - unit * mixed) * inverse).astype(BF16)

    def spread_tdz(tower):
        block = tdz.at[tower, mp]
        return over_m(lambda m: block, lambda q: block)

    arrive(l_copies)
    mine = pl.ds(pl.multiple_of(c * ROWS + mp * SHARE, SHARE), SHARE)
    tdz[0, mp] = finish(rawbuf[own], tanbuf[own], row_part[zl, x] + l_recv[...], grad_rows[mine])
    sar_copies = spread_tdz(0)
    arrive(z_grad_copies)
    grad_cols[...] = unpack_lanes(unfold(sum_slots(z_grad, NH), 2))
    own_sum = column_sum(3)
    arrive(high_copies)
    tdz[1, mp] = finish(
        rawbuf[ROWS : ROWS + SHARE],
        tanbuf[ROWS : ROWS + SHARE],
        own_sum + z_recv[0] + z_recv[1] + z_recv[2],
        grad_cols[pl.ds(first_col, SHARE)],
    )
    optical_copies = spread_tdz(1)

    lanes = pl.ds(pl.multiple_of(c * WIDE, 128), WIDE)
    block_rows = pl.ds(pl.multiple_of(y * BLOCK, BLOCK), BLOCK)

    def hess_terms(tower):
        part = dot(feats[tower, :, pl.ds(pl.multiple_of(mp * PART, PART), PART)], tdz[tower].reshape(ROWS, WIDTH), TN)
        for half in range(2):
            part_hess[tower, half] = part[:, half * WIDE : (half + 1) * WIDE].reshape(NY, BLOCK, WIDE)
        return over_c(part_hess.at[tower, 1 - c], core_hess.at[tower])

    def hess_rows(tower, copies):
        arrive(copies)
        part_hess[tower, c] += core_hess[tower]
        return over_y(lambda r: part_hess.at[tower, c, r], lambda q: y_hess.at[tower, q - 1])

    def hess_high(tower, copies):
        arrive(copies)
        z_hess[tower, zh] = part_hess[tower, c, y] + y_hess[tower, 0] + y_hess[tower, 1] + y_hess[tower, 2]
        block = z_hess.at[tower, zh]
        return over_h(lambda h: block, lambda q: block)

    def hess_sum(tower, copies):
        arrive(copies)
        hess[tower, c, block_rows] = functools.reduce(jnp.add, [z_hess[tower, k] for k in range(NH)])

    def hess_back(tower):
        block = hess.at[tower, c, block_rows]
        return over_c(block, block), over_y(lambda r: block, lambda q: block)

    def hess_pass(tower, copies):
        passed = []
        for q, copy in enumerate(copies, 1):
            copy.wait_recv()
            row = (y + NY - q) % NY
            block = hess.at[tower, c, pl.ds(pl.multiple_of(row * BLOCK, BLOCK), BLOCK)]
            passed += over_c(block, block)
        return passed

    def hess_inner(tower):
        old = resid[tower, block_rows, lanes]
        along = direc[tower, block_rows, lanes]
        new = hess[tower, c, block_rows] + DAMPING * along
        return [jnp.sum(along * new), jnp.sum(old * new), jnp.sum(new * new)]

    arrive(sar_copies)
    core_first = hess_terms(0)
    row_first = hess_rows(0, core_first)
    arrive(optical_copies)
    core_second = hess_terms(1)
    high_first = hess_high(0, row_first)
    row_second = hess_rows(1, core_second)
    high_second = hess_high(1, row_second)
    hess_sum(0, high_first)
    passed, back_first = hess_back(0)
    inner = hess_inner(0)
    hess_sum(1, high_second)
    inner = [first + second for first, second in zip(inner, hess_inner(1))]
    place = lax.broadcasted_iota(jnp.int32, (1, 8, 128), 1)
    norm_p[pl.ds(c * NY + y, 1)] = jnp.where(place == 0, inner[0], jnp.where(place == 1, inner[1], inner[2]))
    scal_copies = over_plane(norm_p)
    more, back_second = hess_back(1)
    passed += more
    passed += hess_pass(0, back_first)
    arrive(scal_copies)
    norm_m[pl.ds(mp, 1)] = sum_slots(norm_p, NC * NY)[None]
    scal_copies = spread_m(norm_m)
    passed += hess_pass(1, back_second)
    arrive(passed)
    stores = []
    for tower in range(2):
        for half in range(2):
            target = hess_out.at[tower * PART : (tower + 1) * PART, half * WIDE : (half + 1) * WIDE]
            stores.append(load(hess.at[tower, half], target, 7 + 2 * tower + half))
    arrive(scal_copies)
    sums = sum_slots(norm_m, NM)
    alpha = norm_old / sums[0:1, 0:1]
    norm_new = norm_old - 2.0 * alpha * sums[1:2, 0:1] + alpha * alpha * sums[2:3, 0:1]
    first_row = lax.broadcasted_iota(jnp.int32, (8, WIDTH), 0) == 0
    info[...] = jnp.where(first_row, alpha, norm_new / norm_old)
    stores.append(load(info, hess_out.at[2 * PART : 2 * PART + 8], 11))
    for store in stores:
        store.wait()
    for copy in pending:
        copy.wait_send()
    assert counter[0] <= SEMS


def last_kernel(hess, direc, resid, solu, out_sol, out_res, out_dir, sol, res, way, store_sem):
    alpha, beta = hess[2 * PART : 2 * PART + 1, 0:1], hess[2 * PART + 1 : 2 * PART + 2, 0:1]
    stores = []

    def store(source, target, tower):
        copy = pltpu.make_async_copy(source.at[tower], target.at[tower], store_sem.at[len(stores)])
        copy.start()
        stores.append(copy)

    for tower in range(2):
        direction = direc[tower]
        sol[tower] = solu[tower] + alpha * direction
        store(sol, out_sol, tower)
        part = hess[tower * PART : (tower + 1) * PART]
        after = resid[tower] - alpha * (part + DAMPING * direction)
        res[tower] = after
        store(res, out_res, tower)
        way[tower] = after + beta * direction
        store(way, out_dir, tower)
    for copy in stores:
        copy.wait()


def body(features, projections, solution, residual, direction):
    vmem = pl.BlockSpec(memory_space=pltpu.VMEM)
    hbm = pl.BlockSpec(memory_space=pltpu.HBM)
    f32 = lambda *size: pltpu.VMEM(size, F32)
    bf16 = lambda *size: pltpu.VMEM(size, BF16)
    scratch = [
        bf16(2, ROWS, DEPTH), f32(2, PART, WIDTH), f32(2, PART, WIDTH),
        bf16(2, 2, 2, NM, PART, WIDE), bf16(2, 2, NY, NM - 1, QUARTER, WIDE),
        f32(ROWS + SHARE, WIDTH), f32(ROWS + SHARE, WIDTH),
        bf16(NC, ROWS, WIDTH), bf16(NC, ROWS, WIDTH),
        bf16(NH, NY, 2, SHARE, WIDTH),
        f32(BOTH, COLS), f32(BOTH, COLS), f32(BOTH, COLS),
        bf16(BOTH, COLS), bf16(BOTH, COLS), f32(COLS, 128), f32(BOTH, 128),
        f32(NC, 8, BOTH), f32(NM, 8, BOTH), f32(NY, 8, COLS // 2), f32(NH, 8, COLS // 2),
        f32(NC, 8, BOTH), f32(NM, 8, BOTH), f32(NY, 8, COLS // 4), f32(NH, 8, COLS // 4),
        f32(NL, NX, SHARE, WIDTH), f32(NL, NX, SHARE, WIDTH), f32(NL, NX, SHARE, WIDTH),
        f32(NX - 1, NL, SHARE, WIDTH), f32(SHARE, WIDTH),
        f32(NH, NY, SHARE, WIDTH), bf16(NH, NY, SHARE, WIDTH),
        bf16(NH, NY - 1, SHARE, WIDTH), f32(NH - 1, SHARE, WIDTH),
        f32(COLS, 128), f32(BOTH, 128),
        bf16(2, NM, SHARE, WIDTH),
        f32(2, 2, NY, BLOCK, WIDE), f32(2, NY, BLOCK, WIDE),
        f32(2, NY - 1, BLOCK, WIDE), f32(2, NH, BLOCK, WIDE), f32(2, 2, PART, WIDE),
        f32(NC * NY, 8, 128), f32(NM, 8, 128), f32(8, WIDTH),
        pltpu.SemaphoreType.DMA((SEMS,)), pltpu.SemaphoreType.DMA((SEMS,)), pltpu.SemaphoreType.DMA((16,)),
    ]
    hess = pl.pallas_call(
        kernel,
        name="cg_step",
        out_shape=jax.ShapeDtypeStruct((2 * PART + 8, WIDTH), F32),
        in_specs=[hbm] * 4,
        out_specs=pl.BlockSpec(memory_space=pl.ANY),
        scratch_shapes=scratch,
        compiler_params=pltpu.CompilerParams(
            collective_id=0, has_side_effects=True, vmem_limit_bytes=58 * 2**20
        ),
    )(features, projections, direction, residual)
    shape = jax.ShapeDtypeStruct(direction.shape, F32)
    return pl.pallas_call(
        last_kernel,
        name="updates",
        out_shape=(shape, shape, shape),
        in_specs=[vmem] * 4,
        out_specs=(hbm, hbm, hbm),
        scratch_shapes=[f32(2, PART, WIDTH)] * 3 + [pltpu.SemaphoreType.DMA((6,))],
        compiler_params=pltpu.CompilerParams(vmem_limit_bytes=16 * 2**20),
    )(hess, direction, residual, solution)


def solution(mesh):
    placed = (
        P(None, "dp", None),
        P(None, "mp", None),
        P(None, "mp", None),
        P(None, "mp", None),
        P(None, "mp", None),
    )
    return jax.shard_map(
        body,
        mesh=mesh,
        in_specs=placed,
        out_specs=(P(None, "mp", None), P(None, "mp", None), P(None, "mp", None)),
        check_vma=False,
    )
```

```python
import functools

import jax
import jax.numpy as jnp
from jax import lax
from jax.experimental import pallas as pl
from jax.experimental.pallas import tpu as pltpu
from jax.sharding import PartitionSpec as P

LOGIT_SCALE = 100.0
DAMPING = 1.0
EPSILON = 1e-06

NC, NY, NH, NX, NL = 2, 4, 4, 4, 2
NM = NX * NL
ROWS, DEPTH, WIDTH = 256, 1024, 768
PART = DEPTH // NM
SHARE = ROWS // NM
COLS = SHARE * NY * NH
BOTH = NC * ROWS
PAIRS = ROWS * NC * NY * NH
TILE = 256
SEMS = 288
QUARTER = 16
DIRECT = PART - NY * QUARTER
BLOCK = PART // NY
BLOCKS = SHARE * NY
WIDE = WIDTH // 2
F32, BF16 = jnp.float32, jnp.bfloat16
MESH = pl.DeviceIdType.MESH


def dot(left, right, dims=((1,), (0,))):
    return lax.dot_general(left, right, (dims, ((), ())), preferred_element_type=F32)


def unit_of(raw):
    inverse = lax.rsqrt(jnp.sum(raw * raw, -1, keepdims=True) + EPSILON)
    return raw * inverse, inverse


def turn_of(tangent, unit, inverse):
    along = jnp.sum(unit * tangent, -1, keepdims=True)
    return (tangent - unit * along) * inverse, along


def pack_lanes(columns):
    size = columns[0].shape[0]
    lane = lax.broadcasted_iota(jnp.int32, (size, 128), 1)
    wide = jnp.zeros((size, 128), F32)
    for place, column in enumerate(columns):
        wide = jnp.where(lane == place, column, wide)
    return wide.T[0:8]


def unpack_lanes(rows):
    return jnp.concatenate([rows, jnp.zeros((128 - rows.shape[0], rows.shape[1]), F32)], 0).T


def fold(rows):
    size = rows[0].shape[1] * len(rows) // 8
    stacked = jnp.concatenate(rows, 0)
    return jnp.concatenate([stacked[:, k : k + size] for k in range(0, stacked.shape[1], size)], 0)


def unfold(block, count):
    return jnp.concatenate([block[k : k + count] for k in range(0, 8, count)], 1)


def softmax_join(slots):
    top = functools.reduce(jnp.maximum, [slot[0] for slot in slots])
    total = 0.0
    weighted = 0.0
    for slot in slots:
        factor = jnp.exp(slot[0] - top)
        total = total + factor * slot[1]
        weighted = weighted + factor * slot[2]
    return top, total, weighted


def kernel(
    feats_in, proj_in, direc_in, resid_in,
    hess_out,
    feats, direc, resid, weights, quarters, rawbuf, tanbuf, rows_u, rows_t, cols,
    scores, left_ts, right_ts, row_weight, col_weight, dsc, tdsc, cvec, row_info,
    core_rows, row_slots, y_stat, z_stat,
    core_grad, grad_slots, y_grad, z_grad,
    row_part, row_away, row_got, x_recv, l_recv, col_part, col_low, y_recv, z_recv,
    grad_cols, grad_rows, tdz, part_hess, core_hess, y_hess, z_hess, hess,
    norm_p, norm_m, info,
    send_sem, recv_sem, load_sem,
):
    dp, mp = lax.axis_index("dp"), lax.axis_index("mp")
    c, y, zh = dp % NC, (dp // NC) % NY, dp // (NC * NY)
    x, zl = mp % NX, mp // NX
    partner = (1 - zl) * NX + x
    counter = [0]

    def device(core=None, row=None, high=None, model=None):
        core, row, high = c if core is None else core, y if row is None else row, zh if high is None else high
        return {"dp": (high * NY + row) * NC + core, "mp": mp if model is None else model}

    def m_at(step):
        return ((zl + step // NX) % NL) * NX + (x + step % NX) % NX

    def m_from(step):
        return ((zl + step // NX) % NL) * NX + (x + NX - step % NX) % NX

    def x_at(step):
        return (x + step) % NX

    def y_at(step):
        return (y + step) % NY

    def h_at(step):
        return (zh + step) % NH

    def send(source, target, where):
        place = counter[0]
        counter[0] += 1
        copy = pltpu.make_async_remote_copy(
            src_ref=source, dst_ref=target, send_sem=send_sem.at[place], recv_sem=recv_sem.at[place],
            device_id=where, device_id_type=MESH,
        )
        copy.start()
        pending.append(copy)
        return copy

    pending = []

    def arrive(copies):
        for copy in copies:
            copy.wait_recv()

    def over_m(source, target):
        return [send(source(m_at(q)), target(q), device(model=m_at(q))) for q in range(1, NM)]

    def over_y(source, target):
        return [send(source(y_at(q)), target(q), device(row=y_at(q))) for q in range(1, NY)]

    def over_h(source, target):
        copies = {q: send(source(h_at(q)), target(q), device(high=h_at(q))) for q in (2, 1, 3)}
        return [copies[q] for q in range(1, NH)]

    def over_x(source, target):
        return [send(source(x_at(q)), target(q), device(model=zl * NX + x_at(q))) for q in range(1, NX)]

    def over_l(source, target):
        return [send(source, target, device(model=partner))]

    def over_plane(slots):
        place = slots.at[c * NY + y]
        return [
            send(place, place, device(core=(c + q // NY) % NC, row=(y + q % NY) % NY)) for q in range(1, NC * NY)
        ]

    def over_c(source, target):
        return [send(source, target, device(core=1 - c))]

    def load(source, target, place):
        copy = pltpu.make_async_copy(source, target, load_sem.at[place])
        copy.start()
        return copy

    barrier = pltpu.get_barrier_semaphore()
    for q in (2, 1, 3):
        pl.semaphore_signal(barrier, inc=1, device_id=device(high=h_at(q)), device_id_type=MESH)
    for q in range(1, NM):
        pl.semaphore_signal(barrier, inc=1, device_id=device(model=m_at(q)), device_id_type=MESH)
    for q in range(1, NC * NY):
        where = device(core=(c + q // NY) % NC, row=(y + q % NY) % NY)
        pl.semaphore_signal(barrier, inc=1, device_id=where, device_id_type=MESH)
    load_direc = [load(direc_in.at[tower], direc.at[tower], tower) for tower in (1, 0)]
    load_proj = [
        [
            load(
                proj_in.at[tower, :, half * WIDE : (half + 1) * WIDE],
                weights.at[0, tower, half, mp],
                12 + 2 * tower + half,
            )
            for half in range(2)
        ]
        for tower in (1, 0)
    ]
    load_feats = [load(feats_in.at[tower], feats.at[tower], 4 + tower) for tower in (1, 0)]
    load_resid = load(resid_in, resid, 6)
    def own_direction(tower):
        for half in range(2):
            piece = direc[tower, :, half * WIDE : (half + 1) * WIDE].astype(BF16)
            weights[1, tower, half, pl.ds(mp, 1)] = piece[None]

    for copy in load_proj[0]:
        copy.wait()
    load_direc[0].wait()
    own_direction(1)
    pl.semaphore_wait(barrier, NM + NC * NY + NH - 3)

    def optical(kind):
        return lambda m: weights.at[kind, 1, c, m, pl.ds(0, DIRECT)]

    def sar(kind):
        return lambda m: weights.at[kind, 0, c, m]

    def spread_x(block):
        return over_x(lambda m: block, lambda q: block)

    def pass_on(blocks, low, copies):
        passed = []
        for q, copy in enumerate(copies, 1):
            copy.wait_recv()
            block = blocks(low * NX + (x + NX - q) % NX)
            passed += over_c(block, block)
        return passed

    def quarter_start(kind):
        part = weights.at[kind, 1, c, mp, pl.ds(pl.multiple_of(DIRECT + y * QUARTER, QUARTER), QUARTER)]
        return over_m(lambda m: part, lambda q: quarters.at[kind, c, y, q - 1])

    def quarter_rows(kind, copies):
        arrive(copies)
        block = quarters.at[kind, c, y]
        return over_c(block, block), over_y(lambda r: block, lambda q: block)

    def quarter_pass(kind, copies):
        passed = []
        for q, copy in enumerate(copies, 1):
            copy.wait_recv()
            block = quarters.at[kind, c, (y + NY - q) % NY]
            passed += over_c(block, block)
        return passed

    def over_z(blocks):
        return over_l(blocks(mp), blocks(mp))

    def relay(blocks, copies):
        arrive(copies)
        block = blocks(partner)
        return spread_x(block), over_c(block, block)

    def assemble(kind):
        for half in range(2):
            for q in range(1, NM):
                for r in range(NY):
                    rows = slice(DIRECT + r * QUARTER, DIRECT + (r + 1) * QUARTER)
                    weights[kind, 1, half, m_from(q), rows] = quarters[kind, half, r, q - 1]

    def embed(kind, tower, rows, into, first):
        for half in range(2):
            span = slice(half * WIDE, (half + 1) * WIDE)
            total = 0.0
            for block in range(0, NM, 2):
                deep = slice(block * PART, (block + 2) * PART)
                piece = weights[kind, tower, half, block : block + 2].reshape(2 * PART, WIDE)
                total += dot(feats[tower, rows, deep], piece)
            into[first : first + total.shape[0], span] = total

    def column_block(kind, high, row):
        return cols.at[high, row, kind]

    def column_rows(kind, high):
        block = column_block(kind, high, y)
        col_copies[kind].extend(over_y(lambda r: block, lambda q: block))

    def column_start(kind):
        block = column_block(kind, zh, y)
        copies = over_h(lambda h: block, lambda q: block)
        column_rows(kind, zh)
        return copies

    def column_relay(kind, copies, q):
        copies[q - 1].wait_recv()
        column_rows(kind, (zh + NH - q) % NH)

    col_copies = ([], [])
    quarter_copies = quarter_start(0)
    z_copies = over_z(optical(0))
    x_copies = spread_x(optical(0)(mp))
    quarter_second = quarter_start(1)
    z_second = over_z(optical(1))
    x_second = spread_x(optical(1)(mp))
    for copy in load_proj[1]:
        copy.wait()
    load_direc[1].wait()
    own_direction(0)
    sar_z = [over_z(sar(kind)) for kind in range(2)]
    passed_first, quarter_copies = quarter_rows(0, quarter_copies)
    relays, passed = relay(optical(0), z_copies)
    passed_first += passed
    passed_second, quarter_second = quarter_rows(1, quarter_second)
    relays_second, passed = relay(optical(1), z_second)
    passed_second += passed
    passed_first += pass_on(optical(0), zl, x_copies)
    sar_x = spread_x(sar(0)(mp))
    passed_first += quarter_pass(0, quarter_copies)
    passed_first += pass_on(optical(0), 1 - zl, relays)
    load_feats[0].wait()
    arrive(passed_first)
    assemble(0)
    own = pl.ds(pl.multiple_of(mp * SHARE, SHARE), SHARE)
    share = slice(ROWS, ROWS + SHARE)
    embed(0, 1, own, rawbuf, ROWS)
    unit, inverse = unit_of(rawbuf[share])
    cols[zh, y, 0] = unit.astype(BF16)
    high_u = column_start(0)
    passed_second += pass_on(optical(1), zl, x_second)
    sar_relays, sar_passed = relay(sar(0), sar_z[0])
    passed_second += quarter_pass(1, quarter_second)
    passed_second += pass_on(optical(1), 1 - zl, relays_second)
    sar_x_second = spread_x(sar(1)(mp))
    sar_relays_second, sar_passed_second = relay(sar(1), sar_z[1])
    arrive(passed_second)
    assemble(1)
    embed(1, 1, own, tanbuf, ROWS)
    unit, inverse = unit_of(rawbuf[share])
    turned, along = turn_of(tanbuf[share], unit, inverse)
    cols[zh, y, 1] = turned.astype(BF16)
    slope = inverse * along
    high_t = column_start(1)
    column_relay(0, high_u, 1)
    column_relay(0, high_u, 3)
    column_relay(0, high_u, 2)
    first_col = pl.multiple_of((zh * NY + y) * SHARE, SHARE)
    cvec[...] = jnp.zeros_like(cvec)
    cvec[pl.ds(first_col, SHARE)] = jnp.broadcast_to(slope, (SHARE, 128))
    slope_row = cvec[...].T[0:1]
    column_relay(1, high_t, 1)
    column_relay(1, high_t, 3)
    sar_passed += pass_on(sar(0), zl, sar_x)
    sar_passed += pass_on(sar(0), 1 - zl, sar_relays)
    column_relay(1, high_t, 2)
    load_feats[1].wait()
    arrive(sar_passed)
    every = slice(0, ROWS)
    embed(0, 0, every, rawbuf, 0)
    unit, inverse = unit_of(rawbuf[every])
    rows_u[c] = unit.astype(BF16)
    unit_copies = over_c(rows_u.at[c], rows_u.at[c])
    sar_passed_second += pass_on(sar(1), zl, sar_x_second)
    sar_passed_second += pass_on(sar(1), 1 - zl, sar_relays_second)
    NT = ((1,), (1,))
    tiles = COLS // TILE

    def score_tile(target, rows, kind, tile):
        piece = cols[2 * tile : 2 * tile + 2, :, kind].reshape(TILE, WIDTH)
        product = dot(rows[...].reshape(BOTH, WIDTH), piece, NT)
        target[:, tile * TILE : (tile + 1) * TILE] = LOGIT_SCALE * product

    arrive(unit_copies)
    arrive(col_copies[0])
    for tile in range(tiles):
        score_tile(scores, rows_u, 0, tile)
    row_max = jnp.max(scores[...], 1, keepdims=True)
    col_max = jnp.max(scores[...], 0, keepdims=True)
    row_sum = jnp.zeros((BOTH, 1), F32)
    col_sum = []
    for tile in range(tiles):
        span = slice(tile * TILE, (tile + 1) * TILE)
        weight = jnp.exp(scores[:, span] - row_max)
        row_weight[:, span] = weight
        row_sum += jnp.sum(weight, 1, keepdims=True)
        weight = jnp.exp(scores[:, span] - col_max[:, span])
        col_weight[:, span] = weight
        col_sum.append(jnp.sum(weight, 0, keepdims=True))
    arrive(sar_passed_second)
    embed(1, 0, every, tanbuf, 0)
    unit, inverse = unit_of(rawbuf[every])
    turned, along = turn_of(tanbuf[every], unit, inverse)
    rows_t[c] = turned.astype(BF16)
    turned_copies = over_c(rows_t.at[c], rows_t.at[c])
    row_slope = inverse * along
    row_slope = jnp.concatenate([jnp.where(c == core, row_slope, 0.0) for core in range(NC)], 0)
    arrive(col_copies[1])
    for tile in range(tiles):
        score_tile(right_ts, rows_u, 1, tile)
    arrive(turned_copies)
    row_weighted = jnp.zeros((BOTH, 1), F32)
    col_weighted = []
    for tile in range(tiles):
        span = slice(tile * TILE, (tile + 1) * TILE)
        score_tile(left_ts, rows_t, 0, tile)
        tscore = left_ts[:, span] + right_ts[:, span]
        row_weighted += jnp.sum(row_weight[:, span] * tscore, 1, keepdims=True)
        col_weighted.append(jnp.sum(col_weight[:, span] * tscore, 0, keepdims=True))
    load_resid.wait()
    resid_norm = jnp.sum(resid[...] * resid[...])
    core_rows[pl.ds(c, 1)] = pack_lanes(
        [row_max, row_sum, row_weighted, row_slope, jnp.full((BOTH, 1), resid_norm, F32)]
    )[None]
    y_stat[pl.ds(y, 1)] = fold(
        [col_max, jnp.concatenate(col_sum, 1), jnp.concatenate(col_weighted, 1), slope_row]
    )[None]

    def join_columns(slots, count):
        parts = [unfold(slots[k], 4) for k in range(count)]
        top, total, weighted = softmax_join([(part[0:1], part[1:2], part[2:3]) for part in parts])
        slopes = functools.reduce(jnp.add, [part[3:4] for part in parts])
        return top, total, weighted, slopes

    def sum_slots(slots, count):
        return functools.reduce(jnp.add, [slots[k] for k in range(count)])

    def spread_y(slots):
        return over_y(lambda r: slots.at[y], lambda q: slots.at[y])

    def spread_h(slots):
        return over_h(lambda h: slots.at[zh], lambda q: slots.at[zh])

    def spread_m(slots):
        return over_m(lambda m: slots.at[mp], lambda q: slots.at[mp])

    core_copies = over_c(core_rows.at[c], core_rows.at[c])
    copies = spread_y(y_stat)

    def join_rows(slots, count):
        parts = [slots[k] for k in range(count)]
        return softmax_join([(part[0:1], part[1:2], part[2:3]) for part in parts])

    arrive(core_copies)
    slopes = core_rows[0, 3:4] + core_rows[1, 3:4]
    joined = join_rows(core_rows, NC)
    row_slots[pl.ds(mp, 1)] = jnp.concatenate(
        [*joined, core_rows[0, 4:5], jnp.zeros((4, BOTH), F32)], 0
    )[None]
    row_copies = spread_m(row_slots)
    arrive(copies)
    z_stat[pl.ds(zh, 1)] = fold(join_columns(y_stat, NY))[None]
    copies = spread_h(z_stat)
    arrive(row_copies)
    top, total, weighted = join_rows(row_slots, NM)
    norm_old = functools.reduce(jnp.add, [row_slots[k, 3:4] for k in range(NM)])[0:1, 0:1]
    row_info[...] = unpack_lanes(jnp.concatenate([top + jnp.log(total), weighted / total, slopes], 0))
    row_lse, row_dot = row_info[:, 0:1], row_info[:, 1:2]
    arrive(copies)
    top, total, weighted, slopes = join_columns(z_stat, NH)
    col_lse, col_dot = top + jnp.log(total), weighted / total
    col_slope = unpack_lanes(slopes)

    row_ids = lax.broadcasted_iota(jnp.int32, (BOTH, TILE), 0)
    col_ids = lax.broadcasted_iota(jnp.int32, (BOTH, TILE), 1)
    offset = c * ROWS + mp * SHARE - first_col
    row_along = jnp.zeros((BOTH, 1), F32)
    row_turned = jnp.zeros((BOTH, 1), F32)
    col_along, col_turned = [], []
    for tile in range(tiles):
        span = slice(tile * TILE, (tile + 1) * TILE)
        score = scores[:, span]
        left, right = left_ts[:, span], right_ts[:, span]
        tscore = left + right
        row_w = jnp.exp(score - row_lse)
        col_w = jnp.exp(score - col_lse[:, span])
        place = col_ids + tile * TILE
        mine = (place >= first_col) & (place < first_col + SHARE) & (row_ids == place + offset)
        low = ((row_w + col_w - 2.0 * mine.astype(F32)) / (2.0 * PAIRS)).astype(BF16)
        dsc[:, span] = low
        tdsc[:, span] = (
            (row_w * (tscore - row_dot) + col_w * (tscore - col_dot[:, span])) / (2.0 * PAIRS)
        ).astype(BF16)
        wide = low.astype(F32)
        row_along += jnp.sum(wide * score, 1, keepdims=True)
        row_turned += jnp.sum(wide * left, 1, keepdims=True)
        col_along.append(jnp.sum(wide * score, 0, keepdims=True))
        col_turned.append(jnp.sum(wide * right, 0, keepdims=True))
    core_grad[pl.ds(c, 1)] = pack_lanes([row_along, row_turned])[None]
    y_grad[pl.ds(y, 1)] = fold([jnp.concatenate(col_along, 1), jnp.concatenate(col_turned, 1)])[None]
    core_copies = over_c(core_grad.at[c], core_grad.at[c])
    y_grad_copies = spread_y(y_grad)

    TN = ((0,), (0,))
    cvec[...] = col_slope

    def column_terms(high):
        start = pl.multiple_of(high * BLOCKS, BLOCKS)
        d_low, t_low = dsc[:, pl.ds(start, BLOCKS)], tdsc[:, pl.ds(start, BLOCKS)]
        units, turns = rows_u[...].reshape(BOTH, WIDTH), rows_t[...].reshape(BOTH, WIDTH)
        total = dot(t_low, units, TN) + dot(d_low, turns, TN)
        total -= cvec[pl.ds(start, BLOCKS), 0:1] * dot(d_low, units, TN)
        return (LOGIT_SCALE * total).reshape(NY, SHARE, WIDTH)

    def row_terms(core, into):
        here = pl.ds(pl.multiple_of(core * ROWS, ROWS), ROWS)
        d_low, t_low, slope = dsc[here], tdsc[here], row_info[here, 2:3]
        for tile in range(WIDTH // TILE):
            span = slice(tile * TILE, (tile + 1) * TILE)
            u_piece = cols[:, :, 0, :, span].reshape(COLS, TILE)
            t_piece = cols[:, :, 1, :, span].reshape(COLS, TILE)
            total = dot(t_low, u_piece) + dot(d_low, t_piece) - slope * dot(d_low, u_piece)
            into[:, :, :, span] = (LOGIT_SCALE * total).reshape(NL, NX, SHARE, TILE)

    steps = (2, 1, 3, 0)
    y_copies = []

    def column_out(place):
        terms = column_terms(h_at(steps[place]))
        col_low[place] = terms.astype(BF16)
        col_part[place] = terms
        y_copies.append(over_y(lambda r: col_low.at[place, r], lambda q: y_recv.at[place, q - 1]))

    column_out(0)
    row_terms(1 - c, row_away)
    away_copies = over_c(row_away, row_got)
    column_out(1)
    arrive(core_copies)
    grad_slots[pl.ds(mp, 1)] = sum_slots(core_grad, NC)[None]
    grad_copies = spread_m(grad_slots)
    row_terms(c, row_part)
    arrive(away_copies)
    row_part[...] += row_got[...]
    x_copies = over_x(lambda k: row_part.at[:, k], lambda q: x_recv.at[q - 1])
    column_out(2)
    arrive(y_grad_copies)
    z_grad[pl.ds(zh, 1)] = sum_slots(y_grad, NY)[None]
    z_grad_copies = spread_h(z_grad)
    column_out(3)

    def column_sum(place):
        arrive(y_copies[place])
        return functools.reduce(jnp.add, [y_recv[place, q].astype(F32) for q in range(NY - 1)], col_part[place, y])

    def column_high(place):
        step = steps[place]
        col_part[place, y] = column_sum(place)
        return [send(col_part.at[place, y], z_recv.at[step - 1], device(high=h_at(step)))]

    high_copies = column_high(0)
    high_copies += column_high(1)
    high_copies += column_high(2)
    arrive(x_copies)
    for low in range(NL):
        row_part[low, x] += x_recv[0, low] + x_recv[1, low] + x_recv[2, low]
    l_copies = over_l(row_part.at[1 - zl, x], l_recv)
    arrive(grad_copies)
    grad_rows[...] = unpack_lanes(sum_slots(grad_slots, NM))

    def finish(raw, tangent, value, terms):
        unit, inverse = unit_of(raw)
        turned, _ = turn_of(tangent, unit, inverse)
        mixed = terms[:, 1:2] + jnp.sum(unit * value, -1, keepdims=True)
        return ((value - turned * terms[:, 0:1] - unit * mixed) * inverse).astype(BF16)

    def spread_tdz(tower):
        block = tdz.at[tower, mp]
        return over_m(lambda m: block, lambda q: block)

    arrive(l_copies)
    mine = pl.ds(pl.multiple_of(c * ROWS + mp * SHARE, SHARE), SHARE)
    tdz[0, mp] = finish(rawbuf[own], tanbuf[own], row_part[zl, x] + l_recv[...], grad_rows[mine])
    sar_copies = spread_tdz(0)
    arrive(z_grad_copies)
    grad_cols[...] = unpack_lanes(unfold(sum_slots(z_grad, NH), 2))
    own_sum = column_sum(3)
    arrive(high_copies)
    tdz[1, mp] = finish(
        rawbuf[ROWS : ROWS + SHARE],
        tanbuf[ROWS : ROWS + SHARE],
        own_sum + z_recv[0] + z_recv[1] + z_recv[2],
        grad_cols[pl.ds(first_col, SHARE)],
    )
    optical_copies = spread_tdz(1)

    lanes = pl.ds(pl.multiple_of(c * WIDE, 128), WIDE)
    block_rows = pl.ds(pl.multiple_of(y * BLOCK, BLOCK), BLOCK)

    def hess_terms(tower):
        part = dot(feats[tower, :, pl.ds(pl.multiple_of(mp * PART, PART), PART)], tdz[tower].reshape(ROWS, WIDTH), TN)
        for half in range(2):
            part_hess[tower, half] = part[:, half * WIDE : (half + 1) * WIDE].reshape(NY, BLOCK, WIDE)
        return over_c(part_hess.at[tower, 1 - c], core_hess.at[tower])

    def hess_rows(tower, copies):
        arrive(copies)
        part_hess[tower, c] += core_hess[tower]
        return over_y(lambda r: part_hess.at[tower, c, r], lambda q: y_hess.at[tower, q - 1])

    def hess_high(tower, copies):
        arrive(copies)
        z_hess[tower, zh] = part_hess[tower, c, y] + y_hess[tower, 0] + y_hess[tower, 1] + y_hess[tower, 2]
        block = z_hess.at[tower, zh]
        return over_h(lambda h: block, lambda q: block)

    def hess_sum(tower, copies):
        arrive(copies)
        hess[tower, c, block_rows] = functools.reduce(jnp.add, [z_hess[tower, k] for k in range(NH)])

    def hess_back(tower):
        block = hess.at[tower, c, block_rows]
        return over_c(block, block), over_y(lambda r: block, lambda q: block)

    def hess_pass(tower, copies):
        passed = []
        for q, copy in enumerate(copies, 1):
            copy.wait_recv()
            row = (y + NY - q) % NY
            block = hess.at[tower, c, pl.ds(pl.multiple_of(row * BLOCK, BLOCK), BLOCK)]
            passed += over_c(block, block)
        return passed

    def hess_inner(tower):
        old = resid[tower, block_rows, lanes]
        along = direc[tower, block_rows, lanes]
        new = hess[tower, c, block_rows] + DAMPING * along
        return [jnp.sum(along * new), jnp.sum(old * new), jnp.sum(new * new)]

    arrive(sar_copies)
    core_first = hess_terms(0)
    row_first = hess_rows(0, core_first)
    arrive(optical_copies)
    core_second = hess_terms(1)
    high_first = hess_high(0, row_first)
    row_second = hess_rows(1, core_second)
    high_second = hess_high(1, row_second)
    hess_sum(0, high_first)
    passed, back_first = hess_back(0)
    inner = hess_inner(0)
    hess_sum(1, high_second)
    inner = [first + second for first, second in zip(inner, hess_inner(1))]
    place = lax.broadcasted_iota(jnp.int32, (1, 8, 128), 1)
    norm_p[pl.ds(c * NY + y, 1)] = jnp.where(place == 0, inner[0], jnp.where(place == 1, inner[1], inner[2]))
    scal_copies = over_plane(norm_p)
    more, back_second = hess_back(1)
    passed += more
    passed += hess_pass(0, back_first)
    arrive(scal_copies)
    norm_m[pl.ds(mp, 1)] = sum_slots(norm_p, NC * NY)[None]
    scal_copies = spread_m(norm_m)
    passed += hess_pass(1, back_second)
    arrive(passed)
    stores = []
    for tower in range(2):
        for half in range(2):
            target = hess_out.at[tower * PART : (tower + 1) * PART, half * WIDE : (half + 1) * WIDE]
            stores.append(load(hess.at[tower, half], target, 7 + 2 * tower + half))
    arrive(scal_copies)
    sums = sum_slots(norm_m, NM)
    alpha = norm_old / sums[0:1, 0:1]
    norm_new = norm_old - 2.0 * alpha * sums[1:2, 0:1] + alpha * alpha * sums[2:3, 0:1]
    first_row = lax.broadcasted_iota(jnp.int32, (8, WIDTH), 0) == 0
    info[...] = jnp.where(first_row, alpha, norm_new / norm_old)
    stores.append(load(info, hess_out.at[2 * PART : 2 * PART + 8], 11))
    for store in stores:
        store.wait()
    for copy in pending:
        copy.wait_send()
    assert counter[0] <= SEMS


def last_kernel(hess, direc, resid, solu, out_sol, out_res, out_dir, sol, res, way, store_sem):
    alpha, beta = hess[2 * PART : 2 * PART + 1, 0:1], hess[2 * PART + 1 : 2 * PART + 2, 0:1]
    stores = []

    def store(source, target, tower):
        copy = pltpu.make_async_copy(source.at[tower], target.at[tower], store_sem.at[len(stores)])
        copy.start()
        stores.append(copy)

    for tower in range(2):
        direction = direc[tower]
        sol[tower] = solu[tower] + alpha * direction
        store(sol, out_sol, tower)
        part = hess[tower * PART : (tower + 1) * PART]
        after = resid[tower] - alpha * (part + DAMPING * direction)
        res[tower] = after
        store(res, out_res, tower)
        way[tower] = after + beta * direction
        store(way, out_dir, tower)
    for copy in stores:
        copy.wait()


def body(features, projections, solution, residual, direction):
    vmem = pl.BlockSpec(memory_space=pltpu.VMEM)
    hbm = pl.BlockSpec(memory_space=pltpu.HBM)
    f32 = lambda *size: pltpu.VMEM(size, F32)
    bf16 = lambda *size: pltpu.VMEM(size, BF16)
    scratch = [
        bf16(2, ROWS, DEPTH), f32(2, PART, WIDTH), f32(2, PART, WIDTH),
        bf16(2, 2, 2, NM, PART, WIDE), bf16(2, 2, NY, NM - 1, QUARTER, WIDE),
        f32(ROWS + SHARE, WIDTH), f32(ROWS + SHARE, WIDTH),
        bf16(NC, ROWS, WIDTH), bf16(NC, ROWS, WIDTH),
        bf16(NH, NY, 2, SHARE, WIDTH),
        f32(BOTH, COLS), f32(BOTH, COLS), f32(BOTH, COLS), f32(BOTH, COLS), f32(BOTH, COLS),
        bf16(BOTH, COLS), bf16(BOTH, COLS), f32(COLS, 128), f32(BOTH, 128),
        f32(NC, 8, BOTH), f32(NM, 8, BOTH), f32(NY, 8, COLS // 2), f32(NH, 8, COLS // 2),
        f32(NC, 8, BOTH), f32(NM, 8, BOTH), f32(NY, 8, COLS // 4), f32(NH, 8, COLS // 4),
        f32(NL, NX, SHARE, WIDTH), f32(NL, NX, SHARE, WIDTH), f32(NL, NX, SHARE, WIDTH),
        f32(NX - 1, NL, SHARE, WIDTH), f32(SHARE, WIDTH),
        f32(NH, NY, SHARE, WIDTH), bf16(NH, NY, SHARE, WIDTH),
        bf16(NH, NY - 1, SHARE, WIDTH), f32(NH - 1, SHARE, WIDTH),
        f32(COLS, 128), f32(BOTH, 128),
        bf16(2, NM, SHARE, WIDTH),
        f32(2, 2, NY, BLOCK, WIDE), f32(2, NY, BLOCK, WIDE),
        f32(2, NY - 1, BLOCK, WIDE), f32(2, NH, BLOCK, WIDE), f32(2, 2, PART, WIDE),
        f32(NC * NY, 8, 128), f32(NM, 8, 128), f32(8, WIDTH),
        pltpu.SemaphoreType.DMA((SEMS,)), pltpu.SemaphoreType.DMA((SEMS,)), pltpu.SemaphoreType.DMA((16,)),
    ]
    hess = pl.pallas_call(
        kernel,
        name="cg_step",
        out_shape=jax.ShapeDtypeStruct((2 * PART + 8, WIDTH), F32),
        in_specs=[hbm] * 4,
        out_specs=pl.BlockSpec(memory_space=pl.ANY),
        scratch_shapes=scratch,
        compiler_params=pltpu.CompilerParams(
            collective_id=0, has_side_effects=True, vmem_limit_bytes=58 * 2**20
        ),
    )(features, projections, direction, residual)
    shape = jax.ShapeDtypeStruct(direction.shape, F32)
    return pl.pallas_call(
        last_kernel,
        name="updates",
        out_shape=(shape, shape, shape),
        in_specs=[vmem] * 4,
        out_specs=(hbm, hbm, hbm),
        scratch_shapes=[f32(2, PART, WIDTH)] * 3 + [pltpu.SemaphoreType.DMA((6,))],
        compiler_params=pltpu.CompilerParams(vmem_limit_bytes=16 * 2**20),
    )(hess, direction, residual, solution)


def solution(mesh):
    placed = (
        P(None, "dp", None),
        P(None, "mp", None),
        P(None, "mp", None),
        P(None, "mp", None),
        P(None, "mp", None),
    )
    return jax.shard_map(
        body,
        mesh=mesh,
        in_specs=placed,
        out_specs=(P(None, "mp", None), P(None, "mp", None), P(None, "mp", None)),
        check_vma=False,
    )
```

```python
import functools

import jax
import jax.numpy as jnp
from jax import lax
from jax.experimental import pallas as pl
from jax.experimental.pallas import tpu as pltpu
from jax.sharding import PartitionSpec as P

LOGIT_SCALE = 100.0
DAMPING = 1.0
EPSILON = 1e-06

NC, NY, NH, NX, NL = 2, 4, 4, 4, 2
NM = NX * NL
ROWS, DEPTH, WIDTH = 256, 1024, 768
PART = DEPTH // NM
SHARE = ROWS // NM
COLS = SHARE * NY * NH
BOTH = NC * ROWS
PAIRS = ROWS * NC * NY * NH
TILE = 256
SEMS = 288
QUARTER = 16
DIRECT = PART - NY * QUARTER
BLOCK = PART // NY
BLOCKS = SHARE * NY
WIDE = WIDTH // 2
F32, BF16 = jnp.float32, jnp.bfloat16
MESH = pl.DeviceIdType.MESH


def dot(left, right, dims=((1,), (0,))):
    return lax.dot_general(left, right, (dims, ((), ())), preferred_element_type=F32)


def unit_of(raw):
    inverse = lax.rsqrt(jnp.sum(raw * raw, -1, keepdims=True) + EPSILON)
    return raw * inverse, inverse


def turn_of(tangent, unit, inverse):
    along = jnp.sum(unit * tangent, -1, keepdims=True)
    return (tangent - unit * along) * inverse, along


def pack_lanes(columns):
    size = columns[0].shape[0]
    lane = lax.broadcasted_iota(jnp.int32, (size, 128), 1)
    wide = jnp.zeros((size, 128), F32)
    for place, column in enumerate(columns):
        wide = jnp.where(lane == place, column, wide)
    return wide.T[0:8]


def unpack_lanes(rows):
    return jnp.concatenate([rows, jnp.zeros((128 - rows.shape[0], rows.shape[1]), F32)], 0).T


def fold(rows):
    size = rows[0].shape[1] * len(rows) // 8
    stacked = jnp.concatenate(rows, 0)
    return jnp.concatenate([stacked[:, k : k + size] for k in range(0, stacked.shape[1], size)], 0)


def unfold(block, count):
    return jnp.concatenate([block[k : k + count] for k in range(0, 8, count)], 1)


def softmax_join(slots):
    top = functools.reduce(jnp.maximum, [slot[0] for slot in slots])
    total = 0.0
    weighted = 0.0
    for slot in slots:
        factor = jnp.exp(slot[0] - top)
        total = total + factor * slot[1]
        weighted = weighted + factor * slot[2]
    return top, total, weighted


def kernel(
    feats_in, proj_in, direc_in, resid_in,
    hess_out,
    feats, direc, resid, weights, quarters, rawbuf, tanbuf, rows_u, rows_t, cols,
    scores, left_ts, right_ts, row_weight, col_weight, dsc, tdsc, cvec, row_info,
    core_rows, row_slots, y_stat, z_stat,
    core_grad, grad_slots, y_grad, z_grad,
    row_part, row_away, row_got, x_recv, l_recv, col_part, col_low, y_recv, z_recv,
    grad_cols, grad_rows, tdz, part_hess, core_hess, y_hess, z_hess, hess,
    norm_p, norm_m, info,
    send_sem, recv_sem, load_sem,
):
    dp, mp = lax.axis_index("dp"), lax.axis_index("mp")
    c, y, zh = dp % NC, (dp // NC) % NY, dp // (NC * NY)
    x, zl = mp % NX, mp // NX
    partner = (1 - zl) * NX + x
    counter = [0]

    def device(core=None, row=None, high=None, model=None):
        core, row, high = c if core is None else core, y if row is None else row, zh if high is None else high
        return {"dp": (high * NY + row) * NC + core, "mp": mp if model is None else model}

    def m_at(step):
        return ((zl + step // NX) % NL) * NX + (x + step % NX) % NX

    def m_from(step):
        return ((zl + step // NX) % NL) * NX + (x + NX - step % NX) % NX

    def x_at(step):
        return (x + step) % NX

    def y_at(step):
        return (y + step) % NY

    def h_at(step):
        return (zh + step) % NH

    def send(source, target, where):
        place = counter[0]
        counter[0] += 1
        copy = pltpu.make_async_remote_copy(
            src_ref=source, dst_ref=target, send_sem=send_sem.at[place], recv_sem=recv_sem.at[place],
            device_id=where, device_id_type=MESH,
        )
        copy.start()
        pending.append(copy)
        return copy

    pending = []

    def arrive(copies):
        for copy in copies:
            copy.wait_recv()

    def over_m(source, target):
        return [send(source(m_at(q)), target(q), device(model=m_at(q))) for q in range(1, NM)]

    def over_y(source, target):
        return [send(source(y_at(q)), target(q), device(row=y_at(q))) for q in range(1, NY)]

    def over_h(source, target):
        copies = {q: send(source(h_at(q)), target(q), device(high=h_at(q))) for q in (2, 1, 3)}
        return [copies[q] for q in range(1, NH)]

    def over_x(source, target):
        return [send(source(x_at(q)), target(q), device(model=zl * NX + x_at(q))) for q in range(1, NX)]

    def over_l(source, target):
        return [send(source, target, device(model=partner))]

    def over_plane(slots):
        place = slots.at[c * NY + y]
        return [
            send(place, place, device(core=(c + q // NY) % NC, row=(y + q % NY) % NY)) for q in range(1, NC * NY)
        ]

    def over_c(source, target):
        return [send(source, target, device(core=1 - c))]

    def load(source, target, place):
        copy = pltpu.make_async_copy(source, target, load_sem.at[place])
        copy.start()
        return copy

    barrier = pltpu.get_barrier_semaphore()
    for q in (2, 1, 3):
        pl.semaphore_signal(barrier, inc=1, device_id=device(high=h_at(q)), device_id_type=MESH)
    for q in range(1, NM):
        pl.semaphore_signal(barrier, inc=1, device_id=device(model=m_at(q)), device_id_type=MESH)
    for q in range(1, NC * NY):
        where = device(core=(c + q // NY) % NC, row=(y + q % NY) % NY)
        pl.semaphore_signal(barrier, inc=1, device_id=where, device_id_type=MESH)
    load_direc = [load(direc_in.at[tower], direc.at[tower], tower) for tower in (1, 0)]
    load_proj = [
        [
            load(
                proj_in.at[tower, :, half * WIDE : (half + 1) * WIDE],
                weights.at[0, tower, half, mp],
                12 + 2 * tower + half,
            )
            for half in range(2)
        ]
        for tower in (1, 0)
    ]
    load_feats = [load(feats_in.at[tower], feats.at[tower], 4 + tower) for tower in (1, 0)]
    load_resid = load(resid_in, resid, 6)
    def own_direction(tower):
        for half in range(2):
            piece = direc[tower, :, half * WIDE : (half + 1) * WIDE].astype(BF16)
            weights[1, tower, half, pl.ds(mp, 1)] = piece[None]

    for copy in load_proj[0]:
        copy.wait()
    load_direc[0].wait()
    own_direction(1)
    pl.semaphore_wait(barrier, NM + NC * NY + NH - 3)

    def optical(kind):
        return lambda m: weights.at[kind, 1, c, m, pl.ds(0, DIRECT)]

    def sar(kind):
        return lambda m: weights.at[kind, 0, c, m]

    def spread_x(block):
        return over_x(lambda m: block, lambda q: block)

    def pass_on(blocks, low, copies):
        passed = []
        for q, copy in enumerate(copies, 1):
            copy.wait_recv()
            block = blocks(low * NX + (x + NX - q) % NX)
            passed += over_c(block, block)
        return passed

    def quarter_start(kind):
        part = weights.at[kind, 1, c, mp, pl.ds(pl.multiple_of(DIRECT + y * QUARTER, QUARTER), QUARTER)]
        return over_m(lambda m: part, lambda q: quarters.at[kind, c, y, q - 1])

    def quarter_rows(kind, copies):
        arrive(copies)
        block = quarters.at[kind, c, y]
        return over_c(block, block), over_y(lambda r: block, lambda q: block)

    def quarter_pass(kind, copies):
        passed = []
        for q, copy in enumerate(copies, 1):
            copy.wait_recv()
            block = quarters.at[kind, c, (y + NY - q) % NY]
            passed += over_c(block, block)
        return passed

    def over_z(blocks):
        return over_l(blocks(mp), blocks(mp))

    def relay(blocks, copies):
        arrive(copies)
        block = blocks(partner)
        return spread_x(block), over_c(block, block)

    def assemble(kind):
        for half in range(2):
            for q in range(1, NM):
                for r in range(NY):
                    rows = slice(DIRECT + r * QUARTER, DIRECT + (r + 1) * QUARTER)
                    weights[kind, 1, half, m_from(q), rows] = quarters[kind, half, r, q - 1]

    def embed(kind, tower, rows, into, first):
        for half in range(2):
            span = slice(half * WIDE, (half + 1) * WIDE)
            total = 0.0
            for block in range(0, NM, 2):
                deep = slice(block * PART, (block + 2) * PART)
                piece = weights[kind, tower, half, block : block + 2].reshape(2 * PART, WIDE)
                total += dot(feats[tower, rows, deep], piece)
            into[first : first + total.shape[0], span] = total

    def column_block(kind, high, row):
        return cols.at[high, row, kind]

    def column_rows(kind, high):
        block = column_block(kind, high, y)
        col_copies[kind].extend(over_y(lambda r: block, lambda q: block))

    def column_start(kind):
        block = column_block(kind, zh, y)
        copies = over_h(lambda h: block, lambda q: block)
        column_rows(kind, zh)
        return copies

    def column_relay(kind, copies, q):
        copies[q - 1].wait_recv()
        column_rows(kind, (zh + NH - q) % NH)

    col_copies = ([], [])
    quarter_copies = quarter_start(0)
    z_copies = over_z(optical(0))
    x_copies = spread_x(optical(0)(mp))
    quarter_second = quarter_start(1)
    z_second = over_z(optical(1))
    x_second = spread_x(optical(1)(mp))
    for copy in load_proj[1]:
        copy.wait()
    load_direc[1].wait()
    own_direction(0)
    sar_z = [over_z(sar(kind)) for kind in range(2)]
    passed_first, quarter_copies = quarter_rows(0, quarter_copies)
    relays, passed = relay(optical(0), z_copies)
    passed_first += passed
    passed_second, quarter_second = quarter_rows(1, quarter_second)
    relays_second, passed = relay(optical(1), z_second)
    passed_second += passed
    passed_first += pass_on(optical(0), zl, x_copies)
    sar_x = spread_x(sar(0)(mp))
    passed_first += quarter_pass(0, quarter_copies)
    passed_first += pass_on(optical(0), 1 - zl, relays)
    load_feats[0].wait()
    arrive(passed_first)
    assemble(0)
    own = pl.ds(pl.multiple_of(mp * SHARE, SHARE), SHARE)
    share = slice(ROWS, ROWS + SHARE)
    embed(0, 1, own, rawbuf, ROWS)
    unit, inverse = unit_of(rawbuf[share])
    cols[zh, y, 0] = unit.astype(BF16)
    high_u = column_start(0)
    passed_second += pass_on(optical(1), zl, x_second)
    sar_relays, sar_passed = relay(sar(0), sar_z[0])
    passed_second += quarter_pass(1, quarter_second)
    passed_second += pass_on(optical(1), 1 - zl, relays_second)
    sar_x_second = spread_x(sar(1)(mp))
    sar_relays_second, sar_passed_second = relay(sar(1), sar_z[1])
    arrive(passed_second)
    assemble(1)
    embed(1, 1, own, tanbuf, ROWS)
    unit, inverse = unit_of(rawbuf[share])
    turned, along = turn_of(tanbuf[share], unit, inverse)
    cols[zh, y, 1] = turned.astype(BF16)
    slope = inverse * along
    high_t = column_start(1)
    column_relay(0, high_u, 1)
    column_relay(0, high_u, 3)
    column_relay(0, high_u, 2)
    first_col = pl.multiple_of((zh * NY + y) * SHARE, SHARE)
    cvec[...] = jnp.zeros_like(cvec)
    cvec[pl.ds(first_col, SHARE)] = jnp.broadcast_to(slope, (SHARE, 128))
    slope_row = cvec[...].T[0:1]
    column_relay(1, high_t, 1)
    column_relay(1, high_t, 3)
    sar_passed += pass_on(sar(0), zl, sar_x)
    sar_passed += pass_on(sar(0), 1 - zl, sar_relays)
    column_relay(1, high_t, 2)
    load_feats[1].wait()
    arrive(sar_passed)
    every = slice(0, ROWS)
    embed(0, 0, every, rawbuf, 0)
    unit, inverse = unit_of(rawbuf[every])
    rows_u[c] = unit.astype(BF16)
    unit_copies = over_c(rows_u.at[c], rows_u.at[c])
    sar_passed_second += pass_on(sar(1), zl, sar_x_second)
    sar_passed_second += pass_on(sar(1), 1 - zl, sar_relays_second)
    NT = ((1,), (1,))
    tiles = COLS // TILE

    def score_tile(target, rows, kind, tile):
        piece = cols[2 * tile : 2 * tile + 2, :, kind].reshape(TILE, WIDTH)
        product = dot(rows[...].reshape(BOTH, WIDTH), piece, NT)
        target[:, tile * TILE : (tile + 1) * TILE] = LOGIT_SCALE * product

    arrive(unit_copies)
    arrive(col_copies[0])
    for tile in range(tiles):
        score_tile(scores, rows_u, 0, tile)
    row_max = jnp.max(scores[...], 1, keepdims=True)
    col_max = jnp.max(scores[...], 0, keepdims=True)
    row_sum = jnp.zeros((BOTH, 1), F32)
    col_sum = []
    for tile in range(tiles):
        span = slice(tile * TILE, (tile + 1) * TILE)
        weight = jnp.exp(scores[:, span] - row_max)
        row_weight[:, span] = weight
        row_sum += jnp.sum(weight, 1, keepdims=True)
        weight = jnp.exp(scores[:, span] - col_max[:, span])
        col_weight[:, span] = weight
        col_sum.append(jnp.sum(weight, 0, keepdims=True))
    arrive(sar_passed_second)
    embed(1, 0, every, tanbuf, 0)
    unit, inverse = unit_of(rawbuf[every])
    turned, along = turn_of(tanbuf[every], unit, inverse)
    rows_t[c] = turned.astype(BF16)
    turned_copies = over_c(rows_t.at[c], rows_t.at[c])
    row_slope = inverse * along
    row_slope = jnp.concatenate([jnp.where(c == core, row_slope, 0.0) for core in range(NC)], 0)
    arrive(col_copies[1])
    for tile in range(tiles):
        score_tile(right_ts, rows_u, 1, tile)
    arrive(turned_copies)
    row_weighted = jnp.zeros((BOTH, 1), F32)
    col_weighted = []
    for tile in range(tiles):
        span = slice(tile * TILE, (tile + 1) * TILE)
        score_tile(left_ts, rows_t, 0, tile)
        tscore = left_ts[:, span] + right_ts[:, span]
        row_weighted += jnp.sum(row_weight[:, span] * tscore, 1, keepdims=True)
        col_weighted.append(jnp.sum(col_weight[:, span] * tscore, 0, keepdims=True))
    load_resid.wait()
    resid_norm = jnp.sum(resid[...] * resid[...])
    core_rows[pl.ds(c, 1)] = pack_lanes(
        [row_max, row_sum, row_weighted, row_slope, jnp.full((BOTH, 1), resid_norm, F32)]
    )[None]
    y_stat[pl.ds(y, 1)] = fold(
        [col_max, jnp.concatenate(col_sum, 1), jnp.concatenate(col_weighted, 1), slope_row]
    )[None]

    def join_columns(slots, count):
        parts = [unfold(slots[k], 4) for k in range(count)]
        top, total, weighted = softmax_join([(part[0:1], part[1:2], part[2:3]) for part in parts])
        slopes = functools.reduce(jnp.add, [part[3:4] for part in parts])
        return top, total, weighted, slopes

    def sum_slots(slots, count):
        return functools.reduce(jnp.add, [slots[k] for k in range(count)])

    def spread_y(slots):
        return over_y(lambda r: slots.at[y], lambda q: slots.at[y])

    def spread_h(slots):
        return over_h(lambda h: slots.at[zh], lambda q: slots.at[zh])

    def spread_m(slots):
        return over_m(lambda m: slots.at[mp], lambda q: slots.at[mp])

    core_copies = over_c(core_rows.at[c], core_rows.at[c])
    copies = spread_y(y_stat)

    def join_rows(slots, count):
        parts = [slots[k] for k in range(count)]
        return softmax_join([(part[0:1], part[1:2], part[2:3]) for part in parts])

    arrive(core_copies)
    slopes = core_rows[0, 3:4] + core_rows[1, 3:4]
    joined = join_rows(core_rows, NC)
    row_slots[pl.ds(mp, 1)] = jnp.concatenate(
        [*joined, core_rows[0, 4:5], jnp.zeros((4, BOTH), F32)], 0
    )[None]
    row_copies = spread_m(row_slots)
    arrive(copies)
    z_stat[pl.ds(zh, 1)] = fold(join_columns(y_stat, NY))[None]
    copies = spread_h(z_stat)
    arrive(row_copies)
    top, total, weighted = join_rows(row_slots, NM)
    norm_old = functools.reduce(jnp.add, [row_slots[k, 3:4] for k in range(NM)])[0:1, 0:1]
    row_info[...] = unpack_lanes(jnp.concatenate([top + jnp.log(total), weighted / total, slopes], 0))
    row_lse, row_dot = row_info[:, 0:1], row_info[:, 1:2]
    arrive(copies)
    top, total, weighted, slopes = join_columns(z_stat, NH)
    col_lse, col_dot = top + jnp.log(total), weighted / total
    col_slope = unpack_lanes(slopes)

    row_ids = lax.broadcasted_iota(jnp.int32, (BOTH, TILE), 0)
    col_ids = lax.broadcasted_iota(jnp.int32, (BOTH, TILE), 1)
    offset = c * ROWS + mp * SHARE - first_col
    row_along = jnp.zeros((BOTH, 1), F32)
    row_turned = jnp.zeros((BOTH, 1), F32)
    col_along, col_turned = [], []
    for tile in range(tiles):
        span = slice(tile * TILE, (tile + 1) * TILE)
        score = scores[:, span]
        left, right = left_ts[:, span], right_ts[:, span]
        tscore = left + right
        row_w = jnp.exp(score - row_lse)
        col_w = jnp.exp(score - col_lse[:, span])
        place = col_ids + tile * TILE
        mine = (place >= first_col) & (place < first_col + SHARE) & (row_ids == place + offset)
        low = ((row_w + col_w - 2.0 * mine.astype(F32)) / (2.0 * PAIRS)).astype(BF16)
        dsc[:, span] = low
        tdsc[:, span] = (
            (row_w * (tscore - row_dot) + col_w * (tscore - col_dot[:, span])) / (2.0 * PAIRS)
        ).astype(BF16)
        wide = low.astype(F32)
        row_along += jnp.sum(wide * score, 1, keepdims=True)
        row_turned += jnp.sum(wide * left, 1, keepdims=True)
        col_along.append(jnp.sum(wide * score, 0, keepdims=True))
        col_turned.append(jnp.sum(wide * right, 0, keepdims=True))
    core_grad[pl.ds(c, 1)] = pack_lanes([row_along, row_turned])[None]
    y_grad[pl.ds(y, 1)] = fold([jnp.concatenate(col_along, 1), jnp.concatenate(col_turned, 1)])[None]
    core_copies = over_c(core_grad.at[c], core_grad.at[c])
    y_grad_copies = spread_y(y_grad)

    TN = ((0,), (0,))
    cvec[...] = col_slope

    def column_terms(high):
        start = pl.multiple_of(high * BLOCKS, BLOCKS)
        d_low, t_low = dsc[:, pl.ds(start, BLOCKS)], tdsc[:, pl.ds(start, BLOCKS)]
        units, turns = rows_u[...].reshape(BOTH, WIDTH), rows_t[...].reshape(BOTH, WIDTH)
        total = dot(t_low, units, TN) + dot(d_low, turns, TN)
        total -= cvec[pl.ds(start, BLOCKS), 0:1] * dot(d_low, units, TN)
        return (LOGIT_SCALE * total).reshape(NY, SHARE, WIDTH)

    def row_terms(core, into):
        here = pl.ds(pl.multiple_of(core * ROWS, ROWS), ROWS)
        d_low, t_low, slope = dsc[here], tdsc[here], row_info[here, 2:3]
        for tile in range(WIDTH // TILE):
            span = slice(tile * TILE, (tile + 1) * TILE)
            u_piece = cols[:, :, 0, :, span].reshape(COLS, TILE)
            t_piece = cols[:, :, 1, :, span].reshape(COLS, TILE)
            total = dot(t_low, u_piece) + dot(d_low, t_piece) - slope * dot(d_low, u_piece)
            into[:, :, :, span] = (LOGIT_SCALE * total).reshape(NL, NX, SHARE, TILE)

    steps = (2, 1, 3, 0)
    y_copies = []

    def column_out(place):
        terms = column_terms(h_at(steps[place]))
        col_low[place] = terms.astype(BF16)
        col_part[place] = terms
        y_copies.append(over_y(lambda r: col_low.at[place, r], lambda q: y_recv.at[place, q - 1]))

    column_out(0)
    row_terms(1 - c, row_away)
    away_copies = over_c(row_away, row_got)
    column_out(1)
    arrive(core_copies)
    grad_slots[pl.ds(mp, 1)] = sum_slots(core_grad, NC)[None]
    grad_copies = spread_m(grad_slots)
    row_terms(c, row_part)
    arrive(away_copies)
    row_part[...] += row_got[...]
    x_copies = over_x(lambda k: row_part.at[:, k], lambda q: x_recv.at[q - 1])
    column_out(2)
    arrive(y_grad_copies)
    z_grad[pl.ds(zh, 1)] = sum_slots(y_grad, NY)[None]
    z_grad_copies = spread_h(z_grad)
    column_out(3)

    def column_sum(place):
        arrive(y_copies[place])
        return functools.reduce(jnp.add, [y_recv[place, q].astype(F32) for q in range(NY - 1)], col_part[place, y])

    def column_high(place):
        step = steps[place]
        col_part[place, y] = column_sum(place)
        return [send(col_part.at[place, y], z_recv.at[step - 1], device(high=h_at(step)))]

    high_copies = column_high(0)
    high_copies += column_high(1)
    high_copies += column_high(2)
    arrive(x_copies)
    for low in range(NL):
        row_part[low, x] += x_recv[0, low] + x_recv[1, low] + x_recv[2, low]
    l_copies = over_l(row_part.at[1 - zl, x], l_recv)
    arrive(grad_copies)
    grad_rows[...] = unpack_lanes(sum_slots(grad_slots, NM))

    def finish(raw, tangent, value, terms):
        unit, inverse = unit_of(raw)
        turned, _ = turn_of(tangent, unit, inverse)
        mixed = terms[:, 1:2] + jnp.sum(unit * value, -1, keepdims=True)
        return ((value - turned * terms[:, 0:1] - unit * mixed) * inverse).astype(BF16)

    def spread_tdz(tower):
        block = tdz.at[tower, mp]
        return over_m(lambda m: block, lambda q: block)

    arrive(l_copies)
    mine = pl.ds(pl.multiple_of(c * ROWS + mp * SHARE, SHARE), SHARE)
    tdz[0, mp] = finish(rawbuf[own], tanbuf[own], row_part[zl, x] + l_recv[...], grad_rows[mine])
    sar_copies = spread_tdz(0)
    arrive(z_grad_copies)
    grad_cols[...] = unpack_lanes(unfold(sum_slots(z_grad, NH), 2))
    own_sum = column_sum(3)
    arrive(high_copies)
    tdz[1, mp] = finish(
        rawbuf[ROWS : ROWS + SHARE],
        tanbuf[ROWS : ROWS + SHARE],
        own_sum + z_recv[0] + z_recv[1] + z_recv[2],
        grad_cols[pl.ds(first_col, SHARE)],
    )
    optical_copies = spread_tdz(1)

    lanes = pl.ds(pl.multiple_of(c * WIDE, 128), WIDE)
    block_rows = pl.ds(pl.multiple_of(y * BLOCK, BLOCK), BLOCK)

    def hess_terms(tower):
        part = dot(feats[tower, :, pl.ds(pl.multiple_of(mp * PART, PART), PART)], tdz[tower].reshape(ROWS, WIDTH), TN)
        for half in range(2):
            part_hess[tower, half] = part[:, half * WIDE : (half + 1) * WIDE].reshape(NY, BLOCK, WIDE)
        return over_c(part_hess.at[tower, 1 - c], core_hess.at[tower])

    def hess_rows(tower, copies):
        arrive(copies)
        part_hess[tower, c] += core_hess[tower]
        return over_y(lambda r: part_hess.at[tower, c, r], lambda q: y_hess.at[tower, q - 1])

    def hess_high(tower, copies):
        arrive(copies)
        z_hess[tower, zh] = part_hess[tower, c, y] + y_hess[tower, 0] + y_hess[tower, 1] + y_hess[tower, 2]
        block = z_hess.at[tower, zh]
        return over_h(lambda h: block, lambda q: block)

    def hess_sum(tower, copies):
        arrive(copies)
        hess[tower, c, block_rows] = functools.reduce(jnp.add, [z_hess[tower, k] for k in range(NH)])

    def hess_back(tower):
        block = hess.at[tower, c, block_rows]
        return over_c(block, block), over_y(lambda r: block, lambda q: block)

    def hess_pass(tower, copies):
        passed = []
        for q, copy in enumerate(copies, 1):
            copy.wait_recv()
            row = (y + NY - q) % NY
            block = hess.at[tower, c, pl.ds(pl.multiple_of(row * BLOCK, BLOCK), BLOCK)]
            passed += over_c(block, block)
        return passed

    def hess_inner(tower):
        old = resid[tower, block_rows, lanes]
        along = direc[tower, block_rows, lanes]
        new = hess[tower, c, block_rows] + DAMPING * along
        return [jnp.sum(along * new), jnp.sum(old * new), jnp.sum(new * new)]

    arrive(sar_copies)
    core_first = hess_terms(0)
    row_first = hess_rows(0, core_first)
    arrive(optical_copies)
    core_second = hess_terms(1)
    high_first = hess_high(0, row_first)
    row_second = hess_rows(1, core_second)
    high_second = hess_high(1, row_second)
    hess_sum(0, high_first)
    passed, back_first = hess_back(0)
    inner = hess_inner(0)
    hess_sum(1, high_second)
    inner = [first + second for first, second in zip(inner, hess_inner(1))]
    place = lax.broadcasted_iota(jnp.int32, (1, 8, 128), 1)
    norm_p[pl.ds(c * NY + y, 1)] = jnp.where(place == 0, inner[0], jnp.where(place == 1, inner[1], inner[2]))
    scal_copies = over_plane(norm_p)
    more, back_second = hess_back(1)
    passed += more
    passed += hess_pass(0, back_first)
    arrive(scal_copies)
    norm_m[pl.ds(mp, 1)] = sum_slots(norm_p, NC * NY)[None]
    scal_copies = spread_m(norm_m)
    passed += hess_pass(1, back_second)
    arrive(passed)
    stores = []
    for tower in range(2):
        for half in range(2):
            target = hess_out.at[tower * PART : (tower + 1) * PART, half * WIDE : (half + 1) * WIDE]
            stores.append(load(hess.at[tower, half], target, 7 + 2 * tower + half))
    arrive(scal_copies)
    sums = sum_slots(norm_m, NM)
    alpha = norm_old / sums[0:1, 0:1]
    norm_new = norm_old - 2.0 * alpha * sums[1:2, 0:1] + alpha * alpha * sums[2:3, 0:1]
    first_row = lax.broadcasted_iota(jnp.int32, (8, WIDTH), 0) == 0
    info[...] = jnp.where(first_row, alpha, norm_new / norm_old)
    stores.append(load(info, hess_out.at[2 * PART : 2 * PART + 8], 11))
    for store in stores:
        store.wait()
    for copy in pending:
        copy.wait_send()
    assert counter[0] <= SEMS


def last_kernel(hess, direc, resid, solu, out_sol, out_res, out_dir, sol, res, way, store_sem):
    alpha, beta = hess[2 * PART : 2 * PART + 1, 0:1], hess[2 * PART + 1 : 2 * PART + 2, 0:1]
    stores = []

    def store(source, target, tower):
        copy = pltpu.make_async_copy(source.at[tower], target.at[tower], store_sem.at[len(stores)])
        copy.start()
        stores.append(copy)

    for tower in range(2):
        direction = direc[tower]
        sol[tower] = solu[tower] + alpha * direction
        store(sol, out_sol, tower)
        part = hess[tower * PART : (tower + 1) * PART]
        after = resid[tower] - alpha * (part + DAMPING * direction)
        res[tower] = after
        store(res, out_res, tower)
        way[tower] = after + beta * direction
        store(way, out_dir, tower)
    for copy in stores:
        copy.wait()


def body(features, projections, solution, residual, direction):
    vmem = pl.BlockSpec(memory_space=pltpu.VMEM)
    hbm = pl.BlockSpec(memory_space=pltpu.HBM)
    f32 = lambda *size: pltpu.VMEM(size, F32)
    bf16 = lambda *size: pltpu.VMEM(size, BF16)
    scratch = [
        bf16(2, ROWS, DEPTH), f32(2, PART, WIDTH), f32(2, PART, WIDTH),
        bf16(2, 2, 2, NM, PART, WIDE), bf16(2, 2, NY, NM - 1, QUARTER, WIDE),
        f32(ROWS + SHARE, WIDTH), f32(ROWS + SHARE, WIDTH),
        bf16(NC, ROWS, WIDTH), bf16(NC, ROWS, WIDTH),
        bf16(NH, NY, 2, SHARE, WIDTH),
        f32(BOTH, COLS), f32(BOTH, COLS), f32(BOTH, COLS), f32(BOTH, COLS), f32(BOTH, COLS),
        bf16(BOTH, COLS), bf16(BOTH, COLS), f32(COLS, 128), f32(BOTH, 128),
        f32(NC, 8, BOTH), f32(NM, 8, BOTH), f32(NY, 8, COLS // 2), f32(NH, 8, COLS // 2),
        f32(NC, 8, BOTH), f32(NM, 8, BOTH), f32(NY, 8, COLS // 4), f32(NH, 8, COLS // 4),
        f32(NL, NX, SHARE, WIDTH), f32(NL, NX, SHARE, WIDTH), f32(NL, NX, SHARE, WIDTH),
        f32(NX - 1, NL, SHARE, WIDTH), f32(SHARE, WIDTH),
        f32(NH, NY, SHARE, WIDTH), bf16(NH, NY, SHARE, WIDTH),
        bf16(NH, NY - 1, SHARE, WIDTH), f32(NH - 1, SHARE, WIDTH),
        f32(COLS, 128), f32(BOTH, 128),
        bf16(2, NM, SHARE, WIDTH),
        f32(2, 2, NY, BLOCK, WIDE), f32(2, NY, BLOCK, WIDE),
        f32(2, NY - 1, BLOCK, WIDE), f32(2, NH, BLOCK, WIDE), f32(2, 2, PART, WIDE),
        f32(NC * NY, 8, 128), f32(NM, 8, 128), f32(8, WIDTH),
        pltpu.SemaphoreType.DMA((SEMS,)), pltpu.SemaphoreType.DMA((SEMS,)), pltpu.SemaphoreType.DMA((16,)),
    ]
    hess = pl.pallas_call(
        kernel,
        name="cg_step",
        out_shape=jax.ShapeDtypeStruct((2 * PART + 8, WIDTH), F32),
        in_specs=[hbm] * 4,
        out_specs=pl.BlockSpec(memory_space=pl.ANY),
        scratch_shapes=scratch,
        compiler_params=pltpu.CompilerParams(
            collective_id=0, has_side_effects=True, vmem_limit_bytes=48 * 2**20
        ),
    )(features, projections, direction, residual)
    shape = jax.ShapeDtypeStruct(direction.shape, F32)
    return pl.pallas_call(
        last_kernel,
        name="updates",
        out_shape=(shape, shape, shape),
        in_specs=[vmem] * 4,
        out_specs=(hbm, hbm, hbm),
        scratch_shapes=[f32(2, PART, WIDTH)] * 3 + [pltpu.SemaphoreType.DMA((6,))],
        compiler_params=pltpu.CompilerParams(vmem_limit_bytes=16 * 2**20),
    )(hess, direction, residual, solution)


def solution(mesh):
    placed = (
        P(None, "dp", None),
        P(None, "mp", None),
        P(None, "mp", None),
        P(None, "mp", None),
        P(None, "mp", None),
    )
    return jax.shard_map(
        body,
        mesh=mesh,
        in_specs=placed,
        out_specs=(P(None, "mp", None), P(None, "mp", None), P(None, "mp", None)),
        check_vma=False,
    )
```
